32 devices in a mesh: section: 4 (over x, core), tensor: 8 (over z, y).
Axes of the slice: x: 2, y: 2, z: 4, core: 2. Of those that a mesh axis runs over, the one named last changes fastest.
Arguments:
- hidden: bfloat16 [256, 8192], P('section', 'tensor'), may hold values from -30 to 30
- audio: bfloat16 [128, 8192], P('section', 'tensor'), may hold values from -30 to 30
- audio_dest: int32 [128, 1], replicated, may hold values from 0 to 3; in each aligned block of 32 rows (0 to 31, 32 to 63, ...) at most 16 rows name the same one
- segment: int32 [8, 64], replicated, may hold values from 0 to 3, never falling along the last dimension, each value on 1 to 32 neighbouring positions
- norm_gain: bfloat16 [4, 8192], P('section', 'tensor'), may hold values from 0.25 to 1.75
- w_query: bfloat16 [4, 8192, 1024], P('section', None, 'tensor'), may hold values from -1 to 1
- w_keyval: bfloat16 [4, 8192, 1024], P('section', 'tensor'), may hold values from -1 to 1
- w_out: bfloat16 [4, 1024, 8192], P('section', None, 'tensor'), may hold values from -0.1875 to 0.1875
Outputs:
- lap_state: bfloat16 [512, 8192], P('section', 'tensor')
The draws below stay inside these ranges and needn't reach their ends.
Inputs may be any that keep to these rules, and one draw needn't show every extreme that they name: `audio_dest`: in each aligned block of 32 rows (the audio rows of one stop) no stop is named more than 16 times, a bound that some block reaches.
All inputs are finite; a program needn't handle non-finite values.
Results may differ from the reference program's by a relative error of at most 0.018.
Values may be sent and summed in bfloat16 or wider, within the bound.
A program may use at most 64 MiB of HBM per device.

```python
import math
import jax
import jax.numpy as jnp
import numpy as np
from jax import lax

D = 8192
HD = 128
KVH = 4
MB_DEV = 2
AUD_MB = 32
TXT_MB = 32
AUD_DEV = 32
STEPS = 4
HEADS = 8
MB_ROWS = 64
CAP = 16
N_SECTION = 4


def spread_scales(key, rows):
    first, second = jax.random.split(key)
    row_scale = jnp.exp(jax.random.uniform(first, (rows, 1)) * math.log(10.0))
    ramp = 3.0 ** (jnp.arange(D, dtype=jnp.float32) / (D - 1))
    col_scale = jnp.exp(jax.random.uniform(second, (1, D)) * math.log(10.0 / 3.0)) * ramp
    return (row_scale, col_scale)


def draw_hidden(key, part):
    key = jax.random.fold_in(key, 11)
    rows = N_SECTION * MB_DEV * TXT_MB
    key_scale, key_noise = jax.random.split(key, 2)
    row_scale, col_scale = spread_scales(key_scale, rows)
    base = jnp.clip(jax.random.normal(key_noise, (rows, D)), -6.0, 6.0)
    return (0.02 * base * row_scale * col_scale).astype(jnp.bfloat16)


def draw_audio(key, part):
    key = jax.random.fold_in(key, 12)
    rows = N_SECTION * AUD_DEV
    key_scale, key_noise = jax.random.split(key, 2)
    row_scale, col_scale = spread_scales(key_scale, rows)
    base = jnp.clip(jax.random.normal(key_noise, (rows, D)), -6.0, 6.0)
    return (0.02 * base * row_scale * col_scale).astype(jnp.bfloat16)


def draw_w_query(key, part):
    key = jax.random.fold_in(key, 21)
    key_noise = jax.random.fold_in(key, 0)
    group = HEADS // KVH
    values = jnp.clip(jax.random.normal(key_noise, (N_SECTION, D, KVH, group, HD)), -6.0, 6.0)
    scaled = jnp.clip(values / math.sqrt(D), -1.0, 1.0)
    return scaled.reshape(N_SECTION, D, HEADS * HD).astype(jnp.bfloat16)


def draw_w_keyval(key, part):
    key = jax.random.fold_in(key, 22)
    key_first, key_second = jax.random.split(key)
    value_part = jnp.clip(jax.random.normal(key_second, (N_SECTION, D, KVH, HD)), -6.0, 6.0)
    key_part = jnp.clip(jax.random.normal(key_first, (N_SECTION, D, KVH, HD)), -6.0, 6.0)
    both = jnp.stack([key_part, value_part], axis=3)
    scaled = jnp.clip(both / math.sqrt(D), -1.0, 1.0)
    return scaled.reshape(N_SECTION, D, KVH * 2 * HD).astype(jnp.bfloat16)


def level_of(own_key, extent, cuts, least, top_value):
    def one(dim, shards_of):
        heights = jax.random.uniform(jax.random.fold_in(jax.random.fold_in(own_key, 6), dim), (shards_of,), jnp.float32, least / len(cuts), top_value / len(cuts))
        return jnp.repeat(jnp.exp(heights), extent[dim] // shards_of).reshape((-1,) + (1,) * (len(extent) - dim - 1))

    factor_of = one(*cuts[0])
    for cut in cuts[1:]:
        factor_of = factor_of * one(*cut)
    return factor_of


def length_profile(number_of, total, most, skew):
    loads = [(1 << 20) // math.isqrt(grade ** skew) + 1 for grade in range(2, number_of + 1)]
    surplus, counts = total - most - (number_of - 1), [1] * (number_of - 1)
    while surplus > 0:
        candidates = [i for i in range(number_of - 1) if counts[i] < most]
        mass, budget = sum([loads[i] for i in candidates]), surplus
        for i in candidates:
            more = min(most - counts[i], max(1, budget * loads[i] // mass), surplus)
            counts[i] = counts[i] + more
            surplus = surplus - more
    return np.array([most] + counts)


def ragged(stream_key, count, total, most, slope):
    if count == 2:
        one = jax.random.randint(stream_key, (), max(1, total - most), min(most, total - 1) + 1)
        return jnp.stack([one, total - one])
    sizes = jnp.asarray(length_profile(count, total, most, slope), jnp.int32)
    pairs = (count - 1) // 2
    donor, taker = sizes[1:1 + 2 * pairs:2], sizes[2:2 + 2 * pairs:2]
    room = jnp.minimum(donor - 1, most - taker)
    shifted = jax.random.randint(jax.random.fold_in(stream_key, 1), (pairs,), 0, 1 << 20) % (room + 1)
    sizes = sizes.at[1:1 + 2 * pairs:2].set(donor - shifted).at[2:2 + 2 * pairs:2].set(taker + shifted)
    return sizes[jax.random.permutation(jax.random.fold_in(stream_key, 2), count)]


def routed_block(own_key, own, number, rows, number_of, top, bound, slope):
    order = jax.random.permutation(own_key, number_of)
    heavy_load, usual = shares(number_of, rows * top, bound, slope, True), shares(number_of, rows * top, bound, slope, False)
    places = jnp.arange(number_of)

    def named(tallies, rotation):
        used = int((tallies > 0).sum())
        fixed = max(1, used // 4)
        passed = fixed + (places - fixed + rotation * (used - fixed)) % max(1, number_of - fixed)
        return jnp.zeros((number_of,), jnp.int32).at[order[jnp.where(places < fixed, places, passed)]].set(jnp.asarray(tallies, jnp.int32))

    tallies = jnp.where(number % 4 == 0, named(heavy_load, number // 4), named(usual, number - number // 4 - 1))
    mixed = jax.random.permutation(jax.random.fold_in(own, 3), number_of)
    source_of, taker = mixed[0:number_of // 2 * 2:2], mixed[1:number_of // 2 * 2:2]
    margin = jnp.minimum(tallies[source_of] - 1, bound - tallies[taker]) // 2
    margin = jnp.where((source_of == order[0]) | (taker == order[0]) | (tallies[taker] == 0), 0, jnp.maximum(margin, 0))
    passed = jax.random.randint(jax.random.fold_in(own, 4), (number_of // 2,), 0, 1 << 20) % (margin + 1)
    tallies = tallies.at[source_of].add(-passed).at[taker].add(passed)
    items = jnp.searchsorted(jnp.cumsum(tallies), jnp.arange(rows * top), side="right").astype(jnp.int32)
    grid = items.reshape(top, rows).T
    grid = grid[jax.random.permutation(jax.random.fold_in(own, 1), rows)]
    rotation = jax.random.randint(jax.random.fold_in(own, 2), (rows, 1), 0, top)
    return jnp.take_along_axis(grid, (jnp.arange(top)[None, :] + rotation) % top, axis=1)


def shares(number_of, total, most, skew, full):
    loads = [(1 << 20) // math.isqrt(grade ** skew) + 1 for grade in range(1, number_of + 1)]
    largest = most if full else min(most, max(-(-total // number_of), total * loads[0] // sum(loads)))
    least = 1 if total - largest >= number_of - 1 else 0
    holding, spare = [largest] + [least] * (number_of - 1), total - largest - least * (number_of - 1)
    while spare > 0:
        movable = [i for i in range(1, number_of) if holding[i] < largest] or [i for i in range(1, number_of) if holding[i] < most]
        mass, left = sum([loads[i] for i in movable]), spare
        for i in movable:
            addition = min(most - holding[i], max(1, left * loads[i] // mass), spare)
            holding[i] = holding[i] + addition
            spare = spare - addition
    return np.array(holding)


def bell_draw(stream_key, extent, deviation, most, pieces=(), kind=jnp.bfloat16):
    entries = deviation * jax.random.normal(stream_key, extent, jnp.float32)
    if pieces:
        entries = entries * level_of(stream_key, extent, pieces, -0.22, 0.18)
    return jnp.clip(entries, -most, most).astype(kind)


def setup_inputs(seed: int = 0) -> dict:
    key_of = jax.random.split(jax.random.key(seed), 9)
    hidden = draw_hidden(jax.random.fold_in(key_of[8], 71), 0)
    audio = draw_audio(jax.random.fold_in(key_of[8], 71), 0)
    audio_dest_keys = jax.random.split(jax.random.fold_in(key_of[2], 1), (N_SECTION * AUD_DEV) // AUD_DEV)
    audio_dest_turns = jax.random.permutation(jax.random.fold_in(key_of[2], 3), (N_SECTION * AUD_DEV) // AUD_DEV)
    audio_dest = jax.vmap(lambda own, number: routed_block(jax.random.fold_in(key_of[2], 2), own, number, AUD_DEV, N_SECTION, 1, CAP, 2))(audio_dest_keys, audio_dest_turns).reshape((N_SECTION * AUD_DEV, 1))
    segment = jax.vmap(lambda own: jnp.searchsorted(jnp.cumsum(ragged(own, 4, MB_ROWS, MB_ROWS // 2, 2)), jnp.arange(MB_ROWS), side="right"))(jax.random.split(key_of[3], (N_SECTION * MB_DEV))).reshape((N_SECTION * MB_DEV, MB_ROWS)).astype(jnp.int32)
    norm_gain = jnp.clip(1.0 + 0.15 * jax.random.normal(key_of[4], (N_SECTION, D), jnp.float32), 0.25, 1.75).astype(jnp.bfloat16)
    w_query = draw_w_query(jax.random.fold_in(key_of[8], 71), 0)
    w_keyval = draw_w_keyval(jax.random.fold_in(key_of[8], 71), 0)
    w_out = bell_draw(key_of[7], (N_SECTION, HEADS * HD, D), (HEADS * HD) ** -0.5, 0.1875, ((0, 4), (2, 8)))
    return {"hidden": hidden, "audio": audio, "audio_dest": audio_dest, "segment": segment, "norm_gain": norm_gain, "w_query": w_query, "w_keyval": w_keyval, "w_out": w_out}


def rotate(values, cosine, sine):
    half = values.shape[-1] // 2
    first = values[..., :half]
    second = values[..., half:]
    return jnp.concatenate([first * cosine - second * sine, second * cosine + first * sine], -1)

def rope_tables(rows, width):
    position = jnp.arange(rows, dtype=jnp.float32)
    freq = 500000.0 ** (-(2.0 * jnp.arange(width // 2, dtype=jnp.float32)) / width)
    angle = position[:, None] * freq[None, :]
    return (jnp.cos(angle), jnp.sin(angle))

def section_layer(state, gain, w_q, w_kv, w_o, segment_now, live_keys, cosine, sine):
    state_wide = state.astype(jnp.float32)
    inverse = lax.rsqrt(lax.optimization_barrier(jnp.mean(state_wide * state_wide, axis=1, keepdims=True)) + 1e-05)
    normed = (state_wide * inverse * gain.astype(jnp.float32)[None, :]).astype(jnp.bfloat16)
    queries = jnp.dot(normed, w_q, preferred_element_type=jnp.float32).reshape(MB_DEV, MB_ROWS, HEADS, HD)
    key_values = jnp.dot(normed, w_kv, preferred_element_type=jnp.float32).reshape(MB_DEV, MB_ROWS, KVH, 2, HD)
    key_rows = key_values[:, :, :, 0]
    value_rows = key_values[:, :, :, 1].astype(jnp.bfloat16)
    queries = rotate(queries, cosine[:, None, :], sine[:, None, :]).astype(jnp.bfloat16)
    key_rows = rotate(key_rows, cosine[:, None, :], sine[:, None, :]).astype(jnp.bfloat16)
    group = HEADS // KVH
    key_rows = jnp.repeat(key_rows, group, axis=2)
    value_rows = jnp.repeat(value_rows, group, axis=2)
    scores = jnp.einsum('mihd,mjhd->mhij', queries.astype(jnp.float32), key_rows.astype(jnp.float32)) * (1.0 / math.sqrt(HD))
    row_ids = jnp.arange(MB_ROWS, dtype=jnp.int32)
    causal = row_ids[None, :] <= row_ids[:, None]
    diagonal = row_ids[None, :] == row_ids[:, None]
    allowed = causal[None] & (segment_now[:, :, None] == segment_now[:, None, :]) & (live_keys[:, None, :] | diagonal[None])
    scores = jnp.where(allowed[:, None], scores, -jnp.inf)
    highest = lax.optimization_barrier(jnp.max(scores, axis=-1, keepdims=True))
    weights = jnp.exp(scores - highest)
    probs = (weights / lax.optimization_barrier(jnp.sum(weights, axis=-1, keepdims=True))).astype(jnp.bfloat16)
    attended = jnp.einsum('mhij,mjhd->mihd', probs.astype(jnp.float32), value_rows.astype(jnp.float32)).astype(jnp.bfloat16)
    attended = attended.reshape(MB_DEV * MB_ROWS, HEADS * HD)
    projected = jnp.dot(attended, w_o, preferred_element_type=jnp.float32)
    return (state_wide + projected).astype(jnp.bfloat16)

def reference(hidden, audio, audio_dest, segment, norm_gain, w_query, w_keyval, w_out):
    targets = audio_dest[:, 0].reshape(N_SECTION, AUD_DEV).astype(jnp.int32)
    order = jnp.arange(AUD_DEV, dtype=jnp.int32)
    earlier = order[None, :] < order[:, None]
    row_rank = lax.optimization_barrier(jnp.sum(((targets[:, :, None] == targets[:, None, :]) & earlier[None]).astype(jnp.int32), axis=2)).astype(jnp.int32)
    sources = jnp.broadcast_to(jnp.arange(N_SECTION, dtype=jnp.int32)[:, None], targets.shape)
    slot_index = (sources * CAP + row_rank).astype(jnp.int32)
    audio_slots = jnp.zeros((N_SECTION, MB_DEV * AUD_MB, D), jnp.bfloat16).at[targets, slot_index].set(audio.reshape(N_SECTION, AUD_DEV, D))
    live_audio = jnp.zeros((N_SECTION, MB_DEV * AUD_MB), jnp.bool_).at[targets, slot_index].set(True)
    text_rows = hidden.reshape(N_SECTION, MB_DEV, TXT_MB, D)
    state = jnp.concatenate([audio_slots.reshape(N_SECTION, MB_DEV, AUD_MB, D), text_rows], 2).reshape(N_SECTION, MB_DEV * MB_ROWS, D)
    live_keys = jnp.concatenate([live_audio.reshape(N_SECTION, MB_DEV, AUD_MB), jnp.ones((N_SECTION, MB_DEV, TXT_MB), jnp.bool_)], 2)
    segment_now = segment.reshape(N_SECTION, MB_DEV, MB_ROWS)
    cosine, sine = rope_tables(MB_ROWS, HD)

    def one_stop(packed):
        return section_layer(packed[0], packed[1], packed[2], packed[3], packed[4], packed[5], packed[6], cosine, sine)
    for lap_step in range(STEPS):
        state = lax.map(one_stop, (state, norm_gain, w_query, w_keyval, w_out, segment_now, live_keys))
        state = jnp.roll(state, 1, 0)
        segment_now = jnp.roll(segment_now, 1, 0)
        live_keys = jnp.roll(live_keys, 1, 0)
    return state.reshape(N_SECTION * MB_DEV * MB_ROWS, D)
```

```python
import functools
import math

import jax
import jax.numpy as jnp
import numpy as np
from jax import lax
from jax.experimental import pallas as pl
from jax.experimental.pallas import tpu as pltpu
from jax.sharding import PartitionSpec as P

D = 8192
HD = 128
KVH = 4
MB_DEV = 2
AUD_MB = 32
TXT_MB = 32
AUD_DEV = 32
STEPS = 4
MB_ROWS = 64
MESH = pl.DeviceIdType.MESH
F32 = jnp.float32
BF16 = jnp.bfloat16


def rope_tables():
    position = np.arange(MB_ROWS, dtype=np.float32)
    freq = np.float32(500000.0) ** (-(2.0 * np.arange(HD // 2, dtype=np.float32)) / HD)
    angle = (position[:, None] * freq[None, :].astype(np.float32)).astype(np.float32)
    cosine, sine = np.cos(angle), np.sin(angle)
    return (
        np.concatenate([cosine, cosine], 1).astype(np.float32),
        np.concatenate([-sine, sine], 1).astype(np.float32),
    )


def iota(shape, dim):
    return lax.broadcasted_iota(jnp.int32, shape, dim)


def drain(ref, sem):
    pltpu.make_async_copy(ref, ref, sem).wait()


def kernel(
    S,
    T,
    hidden,
    audio,
    dest,
    segment,
    gain,
    wq,
    wkv,
    wo_hbm,
    cos_ref,
    sin_ref,
    out,
    w_all,
    wo,
    arecv,
    hid,
    xs,
    xnew,
    psend,
    yrecv,
    accum,
    zsend,
    zrecv,
    sssend,
    ssrecv,
    kvsend,
    kvrecv,
    att,
    local_sem,
    w_sems,
    a_sems,
    send_sems,
    recv_sems,
):
    Z = T // 2
    width = gain.shape[1]
    cap = MB_DEV * AUD_MB // S
    shift = cap.bit_length() - 1
    per_kv = Z // KVH
    q_cols = Z * HD
    me = lax.axis_index("section")
    t = lax.axis_index("tensor")
    y = lax.rem(t, 2)
    z = lax.div(t, 2)
    partner = t + 1 - 2 * y

    def lanes(index):
        return pl.ds(pl.multiple_of(index * HD, HD), HD)

    def tensor_peer(k):
        return lax.rem(t + k, T)

    def push(src, dst, send, recv, device):
        pltpu.make_async_remote_copy(
            src_ref=src,
            dst_ref=dst,
            send_sem=send,
            recv_sem=recv,
            device_id=device,
            device_id_type=MESH,
        ).start()

    stage = [
        pltpu.make_async_copy(
            wq.at[0, pl.ds(pl.multiple_of(t * width, width), width), :],
            w_all.at[y, :, lanes(z)],
            local_sem.at[0],
        ),
        pltpu.make_async_copy(audio, arecv.at[me], local_sem.at[1]),
        pltpu.make_async_copy(hidden, hid, local_sem.at[2]),
        pltpu.make_async_copy(wo_hbm.at[0], wo, local_sem.at[3]),
    ]
    for h in range(KVH):
        for part in range(2):
            stage.append(
                pltpu.make_async_copy(
                    wkv.at[0, :, pl.ds((2 * h + part) * HD, HD)],
                    w_all.at[part, :, pl.ds(q_cols + h * HD, HD)],
                    local_sem.at[4 + 2 * h + part],
                )
            )

    barrier = pltpu.get_barrier_semaphore()
    for k in range(1, T):
        pl.semaphore_signal(
            barrier, inc=1, device_id={"tensor": tensor_peer(k)}, device_id_type=MESH
        )
    for k in range(1, S):
        pl.semaphore_signal(
            barrier, inc=1, device_id={"section": lax.rem(me + k, S)}, device_id_type=MESH
        )
    for copy in stage:
        copy.start()
    pl.semaphore_wait(barrier, T + S - 2)

    for k in range(1, S):
        push(
            audio,
            arecv.at[me],
            a_sems.at[0],
            a_sems.at[1],
            {"section": lax.rem(me + k, S)},
        )
    for k in range(1, T):
        peer = tensor_peer(k)
        push(
            wq.at[0, pl.ds(pl.multiple_of(peer * width, width), width), :],
            w_all.at[y, :, lanes(z)],
            w_sems.at[0],
            w_sems.at[1],
            {"tensor": peer},
        )

    N = dest.shape[0]
    dcol = dest[...].astype(F32)
    sub, lane = iota((N, N), 0), iota((N, N), 1)
    drow = jnp.sum(jnp.where(sub == lane, dcol, 0.0), axis=0, keepdims=True)
    same = (dcol == drow) & ((sub >> 5) == (lane >> 5)) & (sub < lane)
    rank = jnp.sum(jnp.where(same, 1.0, 0.0), axis=0, keepdims=True)
    block = (iota((1, N), 1) >> 5).astype(F32)
    slot = block * float(cap) + rank
    mine = drow == me.astype(F32)

    for copy in stage:
        copy.wait()
    drain(arecv.at[pl.ds(0, S - 1)], a_sems.at[1])
    every_row = arecv[...].reshape(N, width)
    for m in range(MB_DEV):
        wanted = (iota((AUD_MB, N), 0) + m * AUD_MB).astype(F32)
        chosen = jnp.where((slot == wanted) & mine, 1.0, 0.0).astype(BF16)
        rows = jnp.dot(chosen, every_row, preferred_element_type=F32)
        xs[0, m, 0:AUD_MB, :] = rows.astype(BF16)
        xs[0, m, AUD_MB:MB_ROWS, :] = hid[m * TXT_MB : (m + 1) * TXT_MB, :]

    eye = iota((MB_ROWS, MB_ROWS), 0) == iota((MB_ROWS, MB_ROWS), 1)
    causal = iota((MB_ROWS, MB_ROWS), 1) <= iota((MB_ROWS, MB_ROWS), 0)
    scale = 1.0 / math.sqrt(HD)

    def to_col(row):
        return jnp.sum(jnp.where(eye, row, 0.0), axis=1, keepdims=True)

    def to_row(col):
        return jnp.sum(jnp.where(eye, col, 0.0), axis=0, keepdims=True)

    def allowed_of(root, m):
        seg_row = segment[pl.ds(root * MB_DEV + m, 1), :].astype(F32)
        seg_col = to_col(seg_row)
        position = iota((MB_ROWS, N), 0)
        owner = ((position + m * AUD_MB) >> shift).astype(F32)
        named = (drow == root.astype(F32)) & (block == owner)
        count = jnp.sum(jnp.where(named, 1.0, 0.0), axis=1, keepdims=True)
        index = iota((MB_ROWS, 1), 0)
        within = (index & (cap - 1)).astype(F32)
        live = jnp.where((within < count) | (index >= AUD_MB), 1.0, 0.0)
        return causal & (seg_col == seg_row) & ((to_row(live) > 0.5) | eye)

    def body(s, carry):
        root = lax.rem(me - s + 2 * S, S)
        masks = []
        for m in range(MB_DEV):

            @pl.when(s > 0)
            def _():
                drain(xs.at[s, m], recv_sems.at[s, m, 5])

            x = xs[s, m].astype(F32)
            square = x * x
            high = square.astype(BF16)
            low = (square - high.astype(F32)).astype(BF16)
            ones = jnp.ones((8, width), BF16)
            contract = (((1,), (1,)), ((), ()))
            sums = lax.dot_general(ones, high, contract, preferred_element_type=F32)
            sums = sums + lax.dot_general(ones, low, contract, preferred_element_type=F32)
            sssend[s, m] = jnp.concatenate([sums, sums], axis=1)
            for k in range(1, T):
                push(
                    sssend.at[s, m],
                    ssrecv.at[s, m, k - 1],
                    send_sems.at[s, m, 0],
                    recv_sems.at[s, m, 0],
                    {"tensor": tensor_peer(k)},
                )
            xg = (x * gain[...].astype(F32)).astype(BF16)
            if m == 0:

                @pl.when(s == 0)
                def _():
                    drain(wq.at[0, pl.ds(0, (T - 1) * width), :], w_sems.at[1])

            theirs = jnp.dot(xg, w_all[1 - y], preferred_element_type=F32)
            psend[s, m] = theirs.astype(BF16)
            push(
                psend.at[s, m],
                yrecv.at[s, m],
                send_sems.at[s, m, 1],
                recv_sems.at[s, m, 1],
                {"tensor": partner},
            )
            accum[m] = jnp.dot(xg, w_all[y], preferred_element_type=F32)

        for m in range(MB_DEV):
            masks.append(allowed_of(root, m))

        for m in range(MB_DEV):
            drain(yrecv.at[s, m], recv_sems.at[s, m, 1])
            accum[m] = accum[m] + yrecv[s, m].astype(F32)
            for k in range(1, Z):
                other = lax.rem(z + k, Z)
                head = lax.div(other, per_kv)
                zsend[s, m, k - 1, :, 0:HD] = accum[m, :, lanes(other)].astype(BF16)
                zsend[s, m, k - 1, :, HD : 2 * HD] = accum[m, :, lanes(Z + head)].astype(BF16)
                push(
                    zsend.at[s, m, k - 1],
                    zrecv.at[s, m, k - 1],
                    send_sems.at[s, m, 2],
                    recv_sems.at[s, m, 2],
                    {"tensor": other * 2 + y},
                )

        cosine, sine = cos_ref[...], sin_ref[...]
        is_key = y == 0
        cos_kv = jnp.where(is_key, cosine, 1.0)
        sin_kv = jnp.where(is_key, sine, 0.0)
        queries = []
        for m in range(MB_DEV):
            drain(ssrecv.at[s, m], recv_sems.at[s, m, 0])
            total = sssend[s, m] + jnp.sum(ssrecv[s, m], axis=0)
            inverse = lax.rsqrt(total[0:1, 0:MB_ROWS] / D + 1e-05)
            inverse = to_col(inverse)
            drain(zrecv.at[s, m], recv_sems.at[s, m, 2])
            head = lax.div(z, per_kv)
            arrived = jnp.sum(zrecv[s, m].astype(F32), axis=0)
            keyval = (accum[m, :, lanes(Z + head)] + arrived[:, HD:]) * inverse
            keyval = keyval * cos_kv + pltpu.roll(keyval, HD // 2, 1) * sin_kv
            kvsend[s, m] = keyval.astype(BF16)
            push(
                kvsend.at[s, m],
                kvrecv.at[s, m],
                send_sems.at[s, m, 3],
                recv_sems.at[s, m, 3],
                {"tensor": partner},
            )
            query = (accum[m, :, lanes(z)] + arrived[:, :HD]) * inverse
            query = query * cosine + pltpu.roll(query, HD // 2, 1) * sine
            queries.append(query.astype(BF16))

        for m in range(MB_DEV):
            drain(kvrecv.at[s, m], recv_sems.at[s, m, 3])
            own, got = kvsend[s, m], kvrecv[s, m]
            keys = jnp.where(is_key, own, got)
            values = jnp.where(is_key, got, own)
            scores = lax.dot_general(
                queries[m], keys, (((1,), (1,)), ((), ())), preferred_element_type=F32
            )
            scores = jnp.where(masks[m], scores * scale, -jnp.inf)
            highest = jnp.max(scores, axis=-1, keepdims=True)
            weights = jnp.exp(scores - highest)
            probs = (weights / jnp.sum(weights, axis=-1, keepdims=True)).astype(BF16)
            attended = jnp.dot(probs, values, preferred_element_type=F32)
            att[s, m, :, lanes(t)] = attended.astype(BF16)
            for k in range(1, T):
                push(
                    att.at[s, m, :, lanes(t)],
                    att.at[s, m, :, lanes(t)],
                    send_sems.at[s, m, 4],
                    recv_sems.at[s, m, 4],
                    {"tensor": tensor_peer(k)},
                )

        for m in range(MB_DEV):
            drain(att.at[s, m, :, pl.ds(0, (T - 1) * HD)], recv_sems.at[s, m, 4])
            projected = jnp.dot(att[s, m], wo[...], preferred_element_type=F32)
            xnew[s, m] = (xs[s, m].astype(F32) + projected).astype(BF16)
            push(
                xnew.at[s, m],
                xs.at[s + 1, m],
                send_sems.at[s, m, 5],
                recv_sems.at[s + 1, m, 5],
                {"section": lax.rem(me + 1, S)},
            )
        return carry

    lax.fori_loop(0, STEPS, body, 0)

    for m in range(MB_DEV):
        drain(xs.at[STEPS, m], recv_sems.at[STEPS, m, 5])
        out[m * MB_ROWS : (m + 1) * MB_ROWS, :] = xs[STEPS, m]

    drain(arecv.at[pl.ds(0, S - 1)], a_sems.at[0])
    drain(wq.at[0, pl.ds(0, (T - 1) * width), :], w_sems.at[0])

    def finish(s, carry):
        for m in range(MB_DEV):
            drain(ssrecv.at[s, m], send_sems.at[s, m, 0])
            drain(psend.at[s, m], send_sems.at[s, m, 1])
            drain(zsend.at[s, m], send_sems.at[s, m, 2])
            drain(kvsend.at[s, m], send_sems.at[s, m, 3])
            drain(att.at[s, m, :, pl.ds(0, (T - 1) * HD)], send_sems.at[s, m, 4])
            drain(xnew.at[s, m], send_sems.at[s, m, 5])
        return carry

    lax.fori_loop(0, STEPS, finish, 0)


def local(S, T, hidden, audio, audio_dest, segment, norm_gain, w_query, w_keyval, w_out):
    width = hidden.shape[1]
    rows = MB_DEV * MB_ROWS
    Z = T // 2
    cols = (Z + KVH) * HD
    cosine, sine = rope_tables()
    vmem = pl.BlockSpec(memory_space=pltpu.VMEM)
    hbm = pl.BlockSpec(memory_space=pl.ANY)
    per = (STEPS, MB_DEV)
    scratch = [
        pltpu.VMEM((2, width, cols), BF16),
        pltpu.VMEM(w_out.shape[1:], BF16),
        pltpu.VMEM((S, AUD_DEV, width), BF16),
        pltpu.VMEM((MB_DEV * TXT_MB, width), BF16),
        pltpu.VMEM((STEPS + 1, MB_DEV, MB_ROWS, width), BF16),
        pltpu.VMEM(per + (MB_ROWS, width), BF16),
        pltpu.VMEM(per + (MB_ROWS, cols), BF16),
        pltpu.VMEM(per + (MB_ROWS, cols), BF16),
        pltpu.VMEM((MB_DEV, MB_ROWS, cols), F32),
        pltpu.VMEM(per + (Z - 1, MB_ROWS, 2 * HD), BF16),
        pltpu.VMEM(per + (Z - 1, MB_ROWS, 2 * HD), BF16),
        pltpu.VMEM(per + (8, 2 * MB_ROWS), F32),
        pltpu.VMEM(per + (T - 1, 8, 2 * MB_ROWS), F32),
        pltpu.VMEM(per + (MB_ROWS, HD), BF16),
        pltpu.VMEM(per + (MB_ROWS, HD), BF16),
        pltpu.VMEM(per + (MB_ROWS, T * HD), BF16),
        pltpu.SemaphoreType.DMA((4 + 2 * KVH,)),
        pltpu.SemaphoreType.DMA((2,)),
        pltpu.SemaphoreType.DMA((2,)),
        pltpu.SemaphoreType.DMA(per + (6,)),
        pltpu.SemaphoreType.DMA((STEPS + 1, MB_DEV, 6)),
    ]
    return pl.pallas_call(
        functools.partial(kernel, S, T),
        out_shape=jax.ShapeDtypeStruct((rows, width), BF16),
        in_specs=[hbm, hbm, vmem, vmem, vmem, hbm, hbm, hbm, vmem, vmem],
        out_specs=vmem,
        scratch_shapes=scratch,
        compiler_params=pltpu.CompilerParams(
            collective_id=0, has_side_effects=True, vmem_limit_bytes=48 * 1024 * 1024
        ),
        cost_estimate=pl.CostEstimate(
            flops=STEPS * rows * width * (2 * cols + T * HD) * 2,
            bytes_accessed=8 * 1024 * 1024,
            transcendentals=0,
        ),
    )(
        hidden,
        audio,
        audio_dest,
        segment,
        norm_gain,
        w_query,
        w_keyval,
        w_out,
        jnp.asarray(cosine),
        jnp.asarray(sine),
    )


def solution(mesh):
    in_specs = (
        P("section", "tensor"),
        P("section", "tensor"),
        P(),
        P(),
        P("section", "tensor"),
        P("section", None, "tensor"),
        P("section", "tensor", None),
        P("section", None, "tensor"),
    )
    out_specs = P("section", "tensor")
    body = functools.partial(local, mesh.shape["section"], mesh.shape["tensor"])
    return jax.shard_map(body, mesh=mesh, in_specs=in_specs, out_specs=out_specs, check_vma=False)
```

```python
import functools
import math

import jax
import jax.numpy as jnp
import numpy as np
from jax import lax
from jax.experimental import pallas as pl
from jax.experimental.pallas import tpu as pltpu
from jax.sharding import PartitionSpec as P

D = 8192
HD = 128
KVH = 4
MB_DEV = 2
AUD_MB = 32
TXT_MB = 32
AUD_DEV = 32
STEPS = 4
MB_ROWS = 64
MESH = pl.DeviceIdType.MESH
F32 = jnp.float32
BF16 = jnp.bfloat16


def rope_tables():
    position = np.arange(MB_ROWS, dtype=np.float32)
    freq = np.float32(500000.0) ** (-(2.0 * np.arange(HD // 2, dtype=np.float32)) / HD)
    angle = (position[:, None] * freq[None, :].astype(np.float32)).astype(np.float32)
    cosine, sine = np.cos(angle), np.sin(angle)
    return (
        np.concatenate([cosine, cosine], 1).astype(np.float32),
        np.concatenate([-sine, sine], 1).astype(np.float32),
    )


def iota(shape, dim):
    return lax.broadcasted_iota(jnp.int32, shape, dim)


def drain(ref, sem):
    pltpu.make_async_copy(ref, ref, sem).wait()


def kernel(
    S,
    T,
    hidden,
    audio,
    dest,
    segment,
    gain,
    wq,
    wkv,
    wo_hbm,
    cos_ref,
    sin_ref,
    out,
    w_all,
    wo,
    arecv,
    hid,
    gain_own,
    gain_pair,
    xs,
    xnew,
    accum,
    qsend,
    qrecv,
    kvsend,
    kvrecv,
    sssend,
    ssrecv,
    swsend,
    swrecv,
    att,
    local_sem,
    w_sems,
    send_sems,
    recv_sems,
):
    Z = T // 2
    width = gain.shape[1]
    cap = MB_DEV * AUD_MB // S
    shift = cap.bit_length() - 1
    per_kv = Z // KVH
    q_cols = Z * HD
    kv_cols = KVH * HD
    me = lax.axis_index("section")
    t = lax.axis_index("tensor")
    y = lax.rem(t, 2)
    z = lax.div(t, 2)
    partner = t + 1 - 2 * y
    after = lax.rem(me + 1, S)
    before = lax.rem(me + S - 1, S)
    own_half = pl.ds(pl.multiple_of(y * width, width), width)

    def lanes(index):
        return pl.ds(pl.multiple_of(index * HD, HD), HD)

    def pair_rows(index):
        return pl.ds(pl.multiple_of(index * 2 * width, 2 * width), 2 * width)

    def tensor_peer(k):
        return lax.rem(t + k, T)

    def line_peer(k):
        return lax.rem(z + k, Z)

    def push(src, dst, send, recv, device):
        pltpu.make_async_remote_copy(
            src_ref=src,
            dst_ref=dst,
            send_sem=send,
            recv_sem=recv,
            device_id=device,
            device_id_type=MESH,
        ).start()

    stage = [
        pltpu.make_async_copy(audio, arecv.at[me], local_sem.at[0]),
        pltpu.make_async_copy(hidden, hid, local_sem.at[1]),
    ]
    late = [
        pltpu.make_async_copy(wo_hbm.at[0], wo, local_sem.at[2]),
        pltpu.make_async_copy(
            wq.at[0, pair_rows(z), :], w_all.at[:, lanes(z)], local_sem.at[3]
        ),
    ]
    for h in range(KVH):
        late.append(
            pltpu.make_async_copy(
                wkv.at[0, :, lanes(2 * h + y)],
                w_all.at[own_half, pl.ds(q_cols + h * HD, HD)],
                local_sem.at[4 + h],
            )
        )

    barrier = pltpu.get_barrier_semaphore()

    def greet(device):
        pl.semaphore_signal(barrier, inc=1, device_id=device, device_id_type=MESH)

    for k in range(1, T):
        greet({"tensor": tensor_peer(k)})
    for k in range(1, S):
        greet({"section": lax.rem(me + k, S)})
    greet({"section": after, "tensor": partner})
    greet({"section": before, "tensor": partner})
    for copy in stage + late:
        copy.start()
    gain_own[...] = jnp.broadcast_to(gain[...].astype(F32), (8, width))
    gain_pair[:, own_half] = gain_own[...]
    pl.semaphore_wait(barrier, T + S)

    for k in range(1, S):
        push(
            audio,
            arecv.at[me],
            w_sems.at[0, 0],
            w_sems.at[1, 0],
            {"section": lax.rem(me + k, S)},
        )
    push(
        gain_own,
        gain_pair.at[:, own_half],
        w_sems.at[0, 1],
        w_sems.at[1, 1],
        {"tensor": partner},
    )
    for h in range(KVH):
        push(
            wkv.at[0, :, lanes(2 * h + 1 - y)],
            w_all.at[own_half, pl.ds(q_cols + h * HD, HD)],
            w_sems.at[0, 3],
            w_sems.at[1, 3],
            {"tensor": partner},
        )
    for k in range(1, Z):
        other = line_peer(k)
        push(
            wq.at[0, pair_rows(other), :],
            w_all.at[:, lanes(z)],
            w_sems.at[0, 4],
            w_sems.at[1, 4],
            {"tensor": other * 2 + y},
        )

    N = dest.shape[1]
    drow = dest[...].astype(F32)
    sub, lane = iota((N, N), 0), iota((N, N), 1)
    dcol = jnp.sum(jnp.where(sub == lane, drow, 0.0), axis=1, keepdims=True)
    same = (dcol == drow) & ((sub >> 5) == (lane >> 5)) & (sub < lane)
    rank = jnp.sum(jnp.where(same, 1.0, 0.0), axis=0, keepdims=True)
    block = (iota((1, N), 1) >> 5).astype(F32)
    slot = block * float(cap) + rank
    mine = drow == me.astype(F32)

    for copy in stage:
        copy.wait()
    drain(arecv.at[pl.ds(0, S - 1)], w_sems.at[1, 0])
    every_row = arecv[...].reshape(N, width)
    for m in range(MB_DEV):
        wanted = (iota((AUD_MB, N), 0) + m * AUD_MB).astype(F32)
        chosen = jnp.where((slot == wanted) & mine, 1.0, 0.0).astype(BF16)
        rows = jnp.dot(chosen, every_row, preferred_element_type=F32)
        xs[0, m, 0:AUD_MB, own_half] = rows.astype(BF16)
        xs[0, m, AUD_MB:MB_ROWS, own_half] = hid[m * TXT_MB : (m + 1) * TXT_MB, :]
        push(
            xs.at[0, m, :, own_half],
            xs.at[0, m, :, own_half],
            w_sems.at[0, 2],
            recv_sems.at[0, m, 5],
            {"tensor": partner},
        )
    for copy in late:
        copy.wait()

    eye = iota((MB_ROWS, MB_ROWS), 0) == iota((MB_ROWS, MB_ROWS), 1)
    causal = iota((MB_ROWS, MB_ROWS), 1) <= iota((MB_ROWS, MB_ROWS), 0)
    scale = 1.0 / math.sqrt(HD)

    def to_col(row):
        return jnp.sum(jnp.where(eye, row, 0.0), axis=1, keepdims=True)

    def to_row(col):
        return jnp.sum(jnp.where(eye, col, 0.0), axis=0, keepdims=True)

    def allowed_of(root, m):
        seg_row = segment[pl.ds(root * MB_DEV + m, 1), :].astype(F32)
        seg_col = to_col(seg_row)
        position = iota((MB_ROWS, N), 0)
        owner = ((position + m * AUD_MB) >> shift).astype(F32)
        named = (drow == root.astype(F32)) & (block == owner)
        count = jnp.sum(jnp.where(named, 1.0, 0.0), axis=1, keepdims=True)
        index = iota((MB_ROWS, 1), 0)
        within = (index & (cap - 1)).astype(F32)
        live = jnp.where((within < count) | (index >= AUD_MB), 1.0, 0.0)
        return causal & (seg_col == seg_row) & ((to_row(live) > 0.5) | eye)

    def project_kv(s, m, first):
        if first:
            drain(xs.at[0, m, :, pl.ds(0, width)], recv_sems.at[0, m, 5])
        else:
            drain(xs.at[s, m], recv_sems.at[s, m, 5])
        x = xs[s, m].astype(F32)
        sums = to_row(jnp.sum(x * x, axis=1, keepdims=True))
        sums = jnp.broadcast_to(sums, (8, MB_ROWS))
        sssend[s, m] = jnp.concatenate([sums, sums], axis=1)
        for k in range(1, Z):
            push(
                sssend.at[s, m],
                ssrecv.at[s, m, k - 1],
                send_sems.at[s, m, 0],
                recv_sems.at[s, m, 0],
                {"tensor": line_peer(k) * 2 + y},
            )
        xg = (x * gain_pair[0:1, :]).astype(BF16)
        if first and m == 0:
            drain(w_all.at[pl.ds(0, width), pl.ds(0, kv_cols)], w_sems.at[1, 3])
        accum[m, :, q_cols:] = jnp.dot(xg, w_all[:, q_cols:], preferred_element_type=F32)
        for k in range(1, Z):
            other = line_peer(k)
            block_of = lanes(Z + lax.div(other, per_kv))
            kvsend[s, m, k - 1] = accum[m, :, block_of].astype(BF16)
            push(
                kvsend.at[s, m, k - 1],
                kvrecv.at[s, m, k - 1],
                send_sems.at[s, m, 2],
                recv_sems.at[s, m, 2],
                {"tensor": other * 2 + y},
            )
        return xg

    def project_q(s, m, first, xg):
        if first and m == 0:
            drain(w_all.at[:, pl.ds(0, (Z - 1) * HD)], w_sems.at[1, 4])
        accum[m, :, :q_cols] = jnp.dot(xg, w_all[:, :q_cols], preferred_element_type=F32)
        for k in range(1, Z):
            other = line_peer(k)
            qsend[s, m, k - 1] = accum[m, :, lanes(other)].astype(BF16)
            push(
                qsend.at[s, m, k - 1],
                qrecv.at[s, m, k - 1],
                send_sems.at[s, m, 1],
                recv_sems.at[s, m, 1],
                {"tensor": other * 2 + y},
            )

    is_key = y == 0

    def swap(s, m):
        drain(ssrecv.at[s, m], recv_sems.at[s, m, 0])
        total = sssend[s, m] + jnp.sum(ssrecv[s, m], axis=0)
        inverse = to_col(lax.rsqrt(total[0:1, 0:MB_ROWS] / D + 1e-05))
        drain(kvrecv.at[s, m], recv_sems.at[s, m, 2])
        arrived = jnp.sum(kvrecv[s, m].astype(F32), axis=0)
        keyval = (accum[m, :, lanes(Z + lax.div(z, per_kv))] + arrived) * inverse
        cos_kv = jnp.where(is_key, cos_ref[...], 1.0)
        sin_kv = jnp.where(is_key, sin_ref[...], 0.0)
        keyval = keyval * cos_kv + pltpu.roll(keyval, HD // 2, 1) * sin_kv
        swsend[s, m] = keyval.astype(BF16)
        push(
            swsend.at[s, m],
            swrecv.at[s, m],
            send_sems.at[s, m, 3],
            recv_sems.at[s, m, 3],
            {"tensor": partner},
        )
        return inverse

    def attend(s, m, inverse, mask):
        drain(qrecv.at[s, m], recv_sems.at[s, m, 1])
        arrived = jnp.sum(qrecv[s, m].astype(F32), axis=0)
        query = (accum[m, :, lanes(z)] + arrived) * inverse
        query = query * cos_ref[...] + pltpu.roll(query, HD // 2, 1) * sin_ref[...]
        drain(swrecv.at[s, m], recv_sems.at[s, m, 3])
        own, got = swsend[s, m], swrecv[s, m]
        keys = jnp.where(is_key, own, got)
        values = jnp.where(is_key, got, own)
        scores = lax.dot_general(
            query.astype(BF16), keys, (((1,), (1,)), ((), ())), preferred_element_type=F32
        )
        scores = jnp.where(mask, scores * scale, -jnp.inf)
        highest = jnp.max(scores, axis=-1, keepdims=True)
        weights = jnp.exp(scores - highest)
        probs = (weights / jnp.sum(weights, axis=-1, keepdims=True)).astype(BF16)
        attended = jnp.dot(probs, values, preferred_element_type=F32)
        att[s, m, :, lanes(t)] = attended.astype(BF16)
        for k in range(1, T):
            push(
                att.at[s, m, :, lanes(t)],
                att.at[s, m, :, lanes(t)],
                send_sems.at[s, m, 4],
                recv_sems.at[s, m, 4],
                {"tensor": tensor_peer(k)},
            )

    def leave(s, m, last):
        drain(att.at[s, m, :, pl.ds(0, (T - 1) * HD)], recv_sems.at[s, m, 4])
        projected = jnp.dot(att[s, m], wo[...], preferred_element_type=F32)
        xnew[s, m] = (xs[s, m, :, own_half].astype(F32) + projected).astype(BF16)
        routes = [{"section": after}]
        if not last:
            routes.append({"section": after, "tensor": partner})
        for route in routes:
            push(
                xnew.at[s, m],
                xs.at[s + 1, m, :, own_half],
                send_sems.at[s, m, 5],
                recv_sems.at[s + 1, m, 5],
                route,
            )

    def step(s, first, last):
        root = lax.rem(me - s + 2 * S, S)
        each = range(MB_DEV)
        if first:
            gained = [project_kv(s, m, first) for m in each]
            masks = [allowed_of(root, m) for m in each]
            inverses = [swap(s, m) for m in each]
            for m in each:
                project_q(s, m, first, gained[m])
        else:
            for m in each:
                project_q(s, m, first, project_kv(s, m, first))
            masks = [allowed_of(root, m) for m in each]
            inverses = [swap(s, m) for m in each]
        for m in range(MB_DEV):
            attend(s, m, inverses[m], masks[m])
        for m in range(MB_DEV):
            leave(s, m, last)

    def middle(s, carry):
        step(s, False, False)
        return carry

    drain(gain_own, w_sems.at[1, 1])
    step(0, True, False)
    lax.fori_loop(1, STEPS - 1, middle, 0)
    step(STEPS - 1, False, True)

    for m in range(MB_DEV):
        drain(xs.at[STEPS, m, :, pl.ds(0, width)], recv_sems.at[STEPS, m, 5])
        out[m * MB_ROWS : (m + 1) * MB_ROWS, :] = xs[STEPS, m, :, own_half]

    drain(arecv.at[pl.ds(0, S - 1)], w_sems.at[0, 0])
    drain(gain_own, w_sems.at[0, 1])
    drain(xs.at[0, :, :, pl.ds(0, width)], w_sems.at[0, 2])
    drain(w_all.at[pl.ds(0, width), pl.ds(0, kv_cols)], w_sems.at[0, 3])
    drain(w_all.at[:, pl.ds(0, (Z - 1) * HD)], w_sems.at[0, 4])

    def finish(s, carry):
        for m in range(MB_DEV):
            drain(ssrecv.at[s, m], send_sems.at[s, m, 0])
            drain(qsend.at[s, m], send_sems.at[s, m, 1])
            drain(kvsend.at[s, m], send_sems.at[s, m, 2])
            drain(swsend.at[s, m], send_sems.at[s, m, 3])
            drain(att.at[s, m, :, pl.ds(0, (T - 1) * HD)], send_sems.at[s, m, 4])
            drain(xnew.at[s, m], send_sems.at[s, m, 5])

            @pl.when(s < STEPS - 1)
            def _():
                drain(xnew.at[s, m], send_sems.at[s, m, 5])

        return carry

    lax.fori_loop(0, STEPS, finish, 0)


def local(S, T, hidden, audio, audio_dest, segment, norm_gain, w_query, w_keyval, w_out):
    width = hidden.shape[1]
    rows = MB_DEV * MB_ROWS
    Z = T // 2
    cols = (Z + KVH) * HD
    cosine, sine = rope_tables()
    vmem = pl.BlockSpec(memory_space=pltpu.VMEM)
    hbm = pl.BlockSpec(memory_space=pl.ANY)
    per = (STEPS, MB_DEV)
    scratch = [
        pltpu.VMEM((2 * width, cols), BF16),
        pltpu.VMEM(w_out.shape[1:], BF16),
        pltpu.VMEM((S, AUD_DEV, width), BF16),
        pltpu.VMEM((MB_DEV * TXT_MB, width), BF16),
        pltpu.VMEM((8, width), F32),
        pltpu.VMEM((8, 2 * width), F32),
        pltpu.VMEM((STEPS + 1, MB_DEV, MB_ROWS, 2 * width), BF16),
        pltpu.VMEM(per + (MB_ROWS, width), BF16),
        pltpu.VMEM((MB_DEV, MB_ROWS, cols), F32),
        pltpu.VMEM(per + (Z - 1, MB_ROWS, HD), BF16),
        pltpu.VMEM(per + (Z - 1, MB_ROWS, HD), BF16),
        pltpu.VMEM(per + (Z - 1, MB_ROWS, HD), BF16),
        pltpu.VMEM(per + (Z - 1, MB_ROWS, HD), BF16),
        pltpu.VMEM(per + (8, 2 * MB_ROWS), F32),
        pltpu.VMEM(per + (Z - 1, 8, 2 * MB_ROWS), F32),
        pltpu.VMEM(per + (MB_ROWS, HD), BF16),
        pltpu.VMEM(per + (MB_ROWS, HD), BF16),
        pltpu.VMEM(per + (MB_ROWS, T * HD), BF16),
        pltpu.SemaphoreType.DMA((4 + KVH,)),
        pltpu.SemaphoreType.DMA((2, 5)),
        pltpu.SemaphoreType.DMA(per + (6,)),
        pltpu.SemaphoreType.DMA((STEPS + 1, MB_DEV, 6)),
    ]
    return pl.pallas_call(
        functools.partial(kernel, S, T),
        out_shape=jax.ShapeDtypeStruct((rows, width), BF16),
        in_specs=[hbm, hbm, vmem, vmem, vmem, hbm, hbm, hbm, vmem, vmem],
        out_specs=vmem,
        scratch_shapes=scratch,
        compiler_params=pltpu.CompilerParams(
            collective_id=0, has_side_effects=True, vmem_limit_bytes=62 * 1024 * 1024
        ),
        cost_estimate=pl.CostEstimate(
            flops=STEPS * rows * width * (2 * cols + T * HD) * 2,
            bytes_accessed=8 * 1024 * 1024,
            transcendentals=0,
        ),
    )(
        hidden,
        audio,
        audio_dest.reshape(1, -1),
        segment,
        norm_gain,
        w_query,
        w_keyval,
        w_out,
        jnp.asarray(cosine),
        jnp.asarray(sine),
    )


def solution(mesh):
    in_specs = (
        P("section", "tensor"),
        P("section", "tensor"),
        P(),
        P(),
        P("section", "tensor"),
        P("section", None, "tensor"),
        P("section", "tensor", None),
        P("section", None, "tensor"),
    )
    out_specs = P("section", "tensor")
    body = functools.partial(local, mesh.shape["section"], mesh.shape["tensor"])
    return jax.shard_map(body, mesh=mesh, in_specs=in_specs, out_specs=out_specs, check_vma=False)
```

```python
import functools
import math

import jax
import jax.numpy as jnp
import numpy as np
from jax import lax
from jax.experimental import pallas as pl
from jax.experimental.pallas import tpu as pltpu
from jax.sharding import PartitionSpec as P

D = 8192
HD = 128
KVH = 4
MB_DEV = 2
AUD_MB = 32
TXT_MB = 32
AUD_DEV = 32
STEPS = 4
MB_ROWS = 64
MESH = pl.DeviceIdType.MESH
F32 = jnp.float32
BF16 = jnp.bfloat16


def rope_tables():
    position = np.arange(MB_ROWS, dtype=np.float32)
    freq = np.float32(500000.0) ** (-(2.0 * np.arange(HD // 2, dtype=np.float32)) / HD)
    angle = (position[:, None] * freq[None, :].astype(np.float32)).astype(np.float32)
    cosine, sine = np.cos(angle), np.sin(angle)
    return (
        np.concatenate([cosine, cosine], 1).astype(np.float32),
        np.concatenate([-sine, sine], 1).astype(np.float32),
    )


def iota(shape, dim):
    return lax.broadcasted_iota(jnp.int32, shape, dim)


def drain(ref, sem):
    pltpu.make_async_copy(ref, ref, sem).wait()


def kernel(
    S,
    T,
    hidden,
    audio,
    dest,
    segment,
    gain,
    wq,
    wkv,
    wo_hbm,
    cos_ref,
    sin_ref,
    out,
    w_all,
    wo,
    wo_before,
    arecv,
    hid,
    gain_own,
    gain_pair,
    xs,
    xold,
    xnew,
    accum,
    qsend,
    qrecv,
    kvsend,
    kvrecv,
    sssend,
    ssrecv,
    swsend,
    swrecv,
    att,
    attsend,
    local_sem,
    w_sems,
    send_sems,
    recv_sems,
):
    Z = T // 2
    width = gain.shape[1]
    cap = MB_DEV * AUD_MB // S
    shift = cap.bit_length() - 1
    per_kv = Z // KVH
    q_cols = Z * HD
    kv_cols = KVH * HD
    me = lax.axis_index("section")
    t = lax.axis_index("tensor")
    y = lax.rem(t, 2)
    z = lax.div(t, 2)
    partner = t + 1 - 2 * y
    after = lax.rem(me + 1, S)
    before = lax.rem(me + S - 1, S)
    own_half = pl.ds(pl.multiple_of(y * width, width), width)

    def lanes(index):
        return pl.ds(pl.multiple_of(index * HD, HD), HD)

    def pair_rows(index):
        return pl.ds(pl.multiple_of(index * 2 * width, 2 * width), 2 * width)

    def tensor_peer(k):
        return lax.rem(t + k, T)

    def line_peer(k):
        return lax.rem(z + k, Z)

    def push(src, dst, send, recv, device):
        pltpu.make_async_remote_copy(
            src_ref=src,
            dst_ref=dst,
            send_sem=send,
            recv_sem=recv,
            device_id=device,
            device_id_type=MESH,
        ).start()

    stage = [
        pltpu.make_async_copy(audio, arecv.at[me], local_sem.at[0]),
        pltpu.make_async_copy(hidden, hid, local_sem.at[1]),
    ]
    late = [
        pltpu.make_async_copy(wo_hbm.at[0], wo, local_sem.at[2]),
        pltpu.make_async_copy(
            wq.at[0, pair_rows(z), :], w_all.at[:, lanes(z)], local_sem.at[3]
        ),
    ]
    for h in range(KVH):
        late.append(
            pltpu.make_async_copy(
                wkv.at[0, :, lanes(2 * h + y)],
                w_all.at[own_half, pl.ds(q_cols + h * HD, HD)],
                local_sem.at[4 + h],
            )
        )

    barrier = pltpu.get_barrier_semaphore()

    def greet(device):
        pl.semaphore_signal(barrier, inc=1, device_id=device, device_id_type=MESH)

    for k in range(1, T):
        greet({"tensor": tensor_peer(k)})
    for k in range(1, S):
        greet({"section": lax.rem(me + k, S)})
    for k in range(1, T):
        greet({"section": after, "tensor": tensor_peer(k)})
        greet({"section": before, "tensor": tensor_peer(k)})
    for copy in stage + late:
        copy.start()
    gain_own[...] = jnp.broadcast_to(gain[...].astype(F32), (8, width))
    gain_pair[:, own_half] = gain_own[...]
    pl.semaphore_wait(barrier, 3 * (T - 1) + S - 1)

    for k in range(1, S):
        push(
            audio,
            arecv.at[me],
            w_sems.at[0, 0],
            w_sems.at[1, 0],
            {"section": lax.rem(me + k, S)},
        )
    push(
        gain_own,
        gain_pair.at[:, own_half],
        w_sems.at[0, 1],
        w_sems.at[1, 1],
        {"tensor": partner},
    )
    for h in range(KVH):
        push(
            wkv.at[0, :, lanes(2 * h + 1 - y)],
            w_all.at[own_half, pl.ds(q_cols + h * HD, HD)],
            w_sems.at[0, 3],
            w_sems.at[1, 3],
            {"tensor": partner},
        )
    for k in range(1, Z):
        other = line_peer(k)
        push(
            wq.at[0, pair_rows(other), :],
            w_all.at[:, lanes(z)],
            w_sems.at[0, 4],
            w_sems.at[1, 4],
            {"tensor": other * 2 + y},
        )

    for target in (t, partner):
        push(
            wo_hbm.at[0],
            wo_before.at[:, own_half],
            w_sems.at[0, 5],
            w_sems.at[1, 5],
            {"section": after, "tensor": target},
        )

    N = dest.shape[1]
    drow = dest[...].astype(F32)
    sub, lane = iota((N, N), 0), iota((N, N), 1)
    dcol = jnp.sum(jnp.where(sub == lane, drow, 0.0), axis=1, keepdims=True)
    same = (dcol == drow) & ((sub >> 5) == (lane >> 5)) & (sub < lane)
    rank = jnp.sum(jnp.where(same, 1.0, 0.0), axis=0, keepdims=True)
    block = (iota((1, N), 1) >> 5).astype(F32)
    slot = block * float(cap) + rank
    mine = drow == me.astype(F32)

    for copy in stage:
        copy.wait()
    drain(arecv.at[pl.ds(0, S - 1)], w_sems.at[1, 0])
    every_row = arecv[...].reshape(N, width)
    for m in range(MB_DEV):
        wanted = (iota((AUD_MB, N), 0) + m * AUD_MB).astype(F32)
        chosen = jnp.where((slot == wanted) & mine, 1.0, 0.0).astype(BF16)
        rows = jnp.dot(chosen, every_row, preferred_element_type=F32)
        xs[0, m, 0:AUD_MB, own_half] = rows.astype(BF16)
        xs[0, m, AUD_MB:MB_ROWS, own_half] = hid[m * TXT_MB : (m + 1) * TXT_MB, :]
        push(
            xs.at[0, m, :, own_half],
            xs.at[0, m, :, own_half],
            w_sems.at[0, 2],
            recv_sems.at[0, m, 5],
            {"tensor": partner},
        )
    for copy in late:
        copy.wait()

    eye = iota((MB_ROWS, MB_ROWS), 0) == iota((MB_ROWS, MB_ROWS), 1)
    causal = iota((MB_ROWS, MB_ROWS), 1) <= iota((MB_ROWS, MB_ROWS), 0)
    scale = 1.0 / math.sqrt(HD)

    def to_col(row):
        return jnp.sum(jnp.where(eye, row, 0.0), axis=1, keepdims=True)

    def to_row(col):
        return jnp.sum(jnp.where(eye, col, 0.0), axis=0, keepdims=True)

    def allowed_of(root, m):
        seg_row = segment[pl.ds(root * MB_DEV + m, 1), :].astype(F32)
        seg_col = to_col(seg_row)
        position = iota((MB_ROWS, N), 0)
        owner = ((position + m * AUD_MB) >> shift).astype(F32)
        named = (drow == root.astype(F32)) & (block == owner)
        count = jnp.sum(jnp.where(named, 1.0, 0.0), axis=1, keepdims=True)
        index = iota((MB_ROWS, 1), 0)
        within = (index & (cap - 1)).astype(F32)
        live = jnp.where((within < count) | (index >= AUD_MB), 1.0, 0.0)
        return causal & (seg_col == seg_row) & ((to_row(live) > 0.5) | eye)

    def arrive(s, m, columns):
        if s == 2 and m == 0:
            drain(wo_before, w_sems.at[1, 5])
        drain(xold.at[s, m], recv_sems.at[s, m, 5])
        drain(att.at[s - 1, m], recv_sems.at[s - 1, m, 4])
        projected = jnp.dot(att[s - 1, m], wo_before[:, columns], preferred_element_type=F32)
        return xold[s, m, :, columns].astype(F32) + projected

    def project_kv(s, m, first):
        if first:
            drain(xs.at[0, m, :, pl.ds(0, width)], recv_sems.at[0, m, 5])
            x = xs[s, m].astype(F32)
        elif s == 1:
            drain(xs.at[s, m], recv_sems.at[s, m, 5])
            x = xs[s, m].astype(F32)
        else:
            x = arrive(s, m, slice(None)).astype(BF16)
            xs[s, m] = x
            x = x.astype(F32)
        if not first:
            push(
                xs.at[s, m],
                xold.at[s + 1, m],
                send_sems.at[s, m, 5],
                recv_sems.at[s + 1, m, 5],
                {"section": after},
            )
        sums = to_row(jnp.sum(x * x, axis=1, keepdims=True))
        sums = jnp.broadcast_to(sums, (8, MB_ROWS))
        sssend[s, m] = jnp.concatenate([sums, sums], axis=1)
        for k in range(1, Z):
            push(
                sssend.at[s, m],
                ssrecv.at[s, m, k - 1],
                send_sems.at[s, m, 0],
                recv_sems.at[s, m, 0],
                {"tensor": line_peer(k) * 2 + y},
            )
        xg = (x * gain_pair[0:1, :]).astype(BF16)
        if first and m == 0:
            drain(w_all.at[pl.ds(0, width), pl.ds(0, kv_cols)], w_sems.at[1, 3])
        accum[m, :, q_cols:] = jnp.dot(xg, w_all[:, q_cols:], preferred_element_type=F32)
        for k in range(1, Z):
            other = line_peer(k)
            block_of = lanes(Z + lax.div(other, per_kv))
            kvsend[s, m, k - 1] = accum[m, :, block_of].astype(BF16)
            push(
                kvsend.at[s, m, k - 1],
                kvrecv.at[s, m, k - 1],
                send_sems.at[s, m, 2],
                recv_sems.at[s, m, 2],
                {"tensor": other * 2 + y},
            )
        return xg

    def project_q(s, m, first, xg):
        if first and m == 0:
            drain(w_all.at[:, pl.ds(0, (Z - 1) * HD)], w_sems.at[1, 4])
        accum[m, :, :q_cols] = jnp.dot(xg, w_all[:, :q_cols], preferred_element_type=F32)
        for k in range(1, Z):
            other = line_peer(k)
            qsend[s, m, k - 1] = accum[m, :, lanes(other)].astype(BF16)
            push(
                qsend.at[s, m, k - 1],
                qrecv.at[s, m, k - 1],
                send_sems.at[s, m, 1],
                recv_sems.at[s, m, 1],
                {"tensor": other * 2 + y},
            )

    is_key = y == 0

    def swap(s, m):
        drain(ssrecv.at[s, m], recv_sems.at[s, m, 0])
        total = sssend[s, m] + jnp.sum(ssrecv[s, m], axis=0)
        inverse = to_col(lax.rsqrt(total[0:1, 0:MB_ROWS] / D + 1e-05))
        drain(kvrecv.at[s, m], recv_sems.at[s, m, 2])
        arrived = jnp.sum(kvrecv[s, m].astype(F32), axis=0)
        keyval = (accum[m, :, lanes(Z + lax.div(z, per_kv))] + arrived) * inverse
        cos_kv = jnp.where(is_key, cos_ref[...], 1.0)
        sin_kv = jnp.where(is_key, sin_ref[...], 0.0)
        keyval = keyval * cos_kv + pltpu.roll(keyval, HD // 2, 1) * sin_kv
        swsend[s, m] = keyval.astype(BF16)
        push(
            swsend.at[s, m],
            swrecv.at[s, m],
            send_sems.at[s, m, 3],
            recv_sems.at[s, m, 3],
            {"tensor": partner},
        )
        return inverse

    def attend(s, m, inverse, mask):
        drain(qrecv.at[s, m], recv_sems.at[s, m, 1])
        arrived = jnp.sum(qrecv[s, m].astype(F32), axis=0)
        query = (accum[m, :, lanes(z)] + arrived) * inverse
        query = query * cos_ref[...] + pltpu.roll(query, HD // 2, 1) * sin_ref[...]
        drain(swrecv.at[s, m], recv_sems.at[s, m, 3])
        own, got = swsend[s, m], swrecv[s, m]
        keys = jnp.where(is_key, own, got)
        values = jnp.where(is_key, got, own)
        scores = lax.dot_general(
            query.astype(BF16), keys, (((1,), (1,)), ((), ())), preferred_element_type=F32
        )
        scores = jnp.where(mask, scores * scale, -jnp.inf)
        highest = jnp.max(scores, axis=-1, keepdims=True)
        weights = jnp.exp(scores - highest)
        probs = (weights / jnp.sum(weights, axis=-1, keepdims=True)).astype(BF16)
        attended = jnp.dot(probs, values, preferred_element_type=F32)
        if s > 0:
            attsend[s, m] = attended.astype(BF16)
            for k in range(T):
                push(
                    attsend.at[s, m],
                    att.at[s, m, :, lanes(t)],
                    send_sems.at[s, m, 4],
                    recv_sems.at[s, m, 4],
                    {"section": after, "tensor": tensor_peer(k)},
                )
            return
        att[s, m, :, lanes(t)] = attended.astype(BF16)
        for k in range(1, T):
            push(
                att.at[s, m, :, lanes(t)],
                att.at[s, m, :, lanes(t)],
                send_sems.at[s, m, 4],
                recv_sems.at[s, m, 4],
                {"tensor": tensor_peer(k)},
            )

    def leave(s, m):
        drain(att.at[s, m, :, pl.ds(0, (T - 1) * HD)], recv_sems.at[s, m, 4])
        projected = jnp.dot(att[s, m], wo[...], preferred_element_type=F32)
        xnew[m] = (xs[s, m, :, own_half].astype(F32) + projected).astype(BF16)
        for target in (t, partner):
            push(
                xnew.at[m],
                xs.at[s + 1, m, :, own_half],
                send_sems.at[s, m, 5],
                recv_sems.at[s + 1, m, 5],
                {"section": after, "tensor": target},
            )

    def step(s, first):
        root = lax.rem(me - s + 2 * S, S)
        each = range(MB_DEV)
        if first:
            gained = [project_kv(s, m, first) for m in each]
            masks = [allowed_of(root, m) for m in each]
            inverses = [swap(s, m) for m in each]
            for m in each:
                project_q(s, m, first, gained[m])
        else:
            for m in each:
                project_q(s, m, first, project_kv(s, m, first))
            masks = [allowed_of(root, m) for m in each]
            inverses = [swap(s, m) for m in each]
        for m in range(MB_DEV):
            attend(s, m, inverses[m], masks[m])
        if first:
            for m in each:
                leave(s, m)

    drain(gain_own, w_sems.at[1, 1])
    for s in range(STEPS):
        step(s, s == 0)
    for m in range(MB_DEV):
        out[m * MB_ROWS : (m + 1) * MB_ROWS, :] = arrive(STEPS, m, own_half).astype(BF16)

    drain(arecv.at[pl.ds(0, S - 1)], w_sems.at[0, 0])
    drain(gain_own, w_sems.at[0, 1])
    drain(xs.at[0, :, :, pl.ds(0, width)], w_sems.at[0, 2])
    drain(w_all.at[pl.ds(0, width), pl.ds(0, kv_cols)], w_sems.at[0, 3])
    drain(w_all.at[:, pl.ds(0, (Z - 1) * HD)], w_sems.at[0, 4])

    drain(wo_before, w_sems.at[0, 5])
    for s in range(STEPS):
        for m in range(MB_DEV):
            drain(ssrecv.at[s, m], send_sems.at[s, m, 0])
            drain(qsend.at[s, m], send_sems.at[s, m, 1])
            drain(kvsend.at[s, m], send_sems.at[s, m, 2])
            drain(swsend.at[s, m], send_sems.at[s, m, 3])
            sent = T if s > 0 else T - 1
            drain(att.at[s, m, :, pl.ds(0, sent * HD)], send_sems.at[s, m, 4])
            drain(xs.at[s, m], send_sems.at[s, m, 5])


def local(S, T, hidden, audio, audio_dest, segment, norm_gain, w_query, w_keyval, w_out):
    width = hidden.shape[1]
    rows = MB_DEV * MB_ROWS
    Z = T // 2
    cols = (Z + KVH) * HD
    cosine, sine = rope_tables()
    vmem = pl.BlockSpec(memory_space=pltpu.VMEM)
    hbm = pl.BlockSpec(memory_space=pl.ANY)
    per = (STEPS, MB_DEV)
    scratch = [
        pltpu.VMEM((2 * width, cols), BF16),
        pltpu.VMEM(w_out.shape[1:], BF16),
        pltpu.VMEM((T * HD, 2 * width), BF16),
        pltpu.VMEM((S, AUD_DEV, width), BF16),
        pltpu.VMEM((MB_DEV * TXT_MB, width), BF16),
        pltpu.VMEM((8, width), F32),
        pltpu.VMEM((8, 2 * width), F32),
        pltpu.VMEM(per + (MB_ROWS, 2 * width), BF16),
        pltpu.VMEM((STEPS + 1, MB_DEV, MB_ROWS, 2 * width), BF16),
        pltpu.VMEM((MB_DEV, MB_ROWS, width), BF16),
        pltpu.VMEM((MB_DEV, MB_ROWS, cols), F32),
        pltpu.VMEM(per + (Z - 1, MB_ROWS, HD), BF16),
        pltpu.VMEM(per + (Z - 1, MB_ROWS, HD), BF16),
        pltpu.VMEM(per + (Z - 1, MB_ROWS, HD), BF16),
        pltpu.VMEM(per + (Z - 1, MB_ROWS, HD), BF16),
        pltpu.VMEM(per + (8, 2 * MB_ROWS), F32),
        pltpu.VMEM(per + (Z - 1, 8, 2 * MB_ROWS), F32),
        pltpu.VMEM(per + (MB_ROWS, HD), BF16),
        pltpu.VMEM(per + (MB_ROWS, HD), BF16),
        pltpu.VMEM(per + (MB_ROWS, T * HD), BF16),
        pltpu.VMEM(per + (MB_ROWS, HD), BF16),
        pltpu.SemaphoreType.DMA((4 + KVH,)),
        pltpu.SemaphoreType.DMA((2, 6)),
        pltpu.SemaphoreType.DMA(per + (6,)),
        pltpu.SemaphoreType.DMA((STEPS + 1, MB_DEV, 6)),
    ]
    return pl.pallas_call(
        functools.partial(kernel, S, T),
        out_shape=jax.ShapeDtypeStruct((rows, width), BF16),
        in_specs=[hbm, hbm, vmem, vmem, vmem, hbm, hbm, hbm, vmem, vmem],
        out_specs=vmem,
        scratch_shapes=scratch,
        compiler_params=pltpu.CompilerParams(
            collective_id=0, has_side_effects=True, vmem_limit_bytes=62 * 1024 * 1024
        ),
        cost_estimate=pl.CostEstimate(
            flops=STEPS * rows * width * (2 * cols + T * HD) * 2,
            bytes_accessed=8 * 1024 * 1024,
            transcendentals=0,
        ),
    )(
        hidden,
        audio,
        audio_dest.reshape(1, -1),
        segment,
        norm_gain,
        w_query,
        w_keyval,
        w_out,
        jnp.asarray(cosine),
        jnp.asarray(sine),
    )


def solution(mesh):
    in_specs = (
        P("section", "tensor"),
        P("section", "tensor"),
        P(),
        P(),
        P("section", "tensor"),
        P("section", None, "tensor"),
        P("section", "tensor", None),
        P("section", None, "tensor"),
    )
    out_specs = P("section", "tensor")
    body = functools.partial(local, mesh.shape["section"], mesh.shape["tensor"])
    return jax.shard_map(body, mesh=mesh, in_specs=in_specs, out_specs=out_specs, check_vma=False)
```

```python
import functools
import math

import jax
import jax.numpy as jnp
import numpy as np
from jax import lax
from jax.experimental import pallas as pl
from jax.experimental.pallas import tpu as pltpu
from jax.sharding import PartitionSpec as P

D = 8192
HD = 128
KVH = 4
MB_DEV = 2
AUD_MB = 32
TXT_MB = 32
AUD_DEV = 32
STEPS = 4
DIRECT = 3
MB_ROWS = 64
SQ_ROWS = 16
MESH = pl.DeviceIdType.MESH
F32 = jnp.float32
BF16 = jnp.bfloat16


def rope_tables():
    position = np.arange(MB_ROWS, dtype=np.float32)
    freq = np.float32(500000.0) ** (-(2.0 * np.arange(HD // 2, dtype=np.float32)) / HD)
    angle = (position[:, None] * freq[None, :].astype(np.float32)).astype(np.float32)
    cosine, sine = np.cos(angle), np.sin(angle)
    return (
        np.concatenate([cosine, cosine], 1).astype(np.float32),
        np.concatenate([-sine, sine], 1).astype(np.float32),
    )


def iota(shape, dim):
    return lax.broadcasted_iota(jnp.int32, shape, dim)


def drain(ref, sem):
    pltpu.make_async_copy(ref, ref, sem).wait()


def kernel(
    S,
    T,
    hidden,
    audio,
    dest,
    segment,
    gain,
    wq,
    wkv,
    wo_hbm,
    cos_ref,
    sin_ref,
    out,
    w_all,
    wo,
    wo_before,
    arecv,
    hid,
    gain_own,
    gain_pair,
    xs,
    xold,
    xnew,
    accum,
    qsend,
    qrecv,
    kvsend,
    kvrecv,
    swsend,
    swrecv,
    att,
    attsend,
    local_sem,
    w_sems,
    send_sems,
    recv_sems,
):
    Z = T // 2
    width = gain.shape[1]
    cap = MB_DEV * AUD_MB // S
    shift = cap.bit_length() - 1
    per_kv = Z // KVH
    q_cols = Z * HD
    kv_cols = KVH * HD
    me = lax.axis_index("section")
    t = lax.axis_index("tensor")
    y = lax.rem(t, 2)
    z = lax.div(t, 2)
    partner = t + 1 - 2 * y
    after = lax.rem(me + 1, S)
    before = lax.rem(me + S - 1, S)
    own_half = pl.ds(pl.multiple_of(y * width, width), width)

    def lanes(index):
        return pl.ds(pl.multiple_of(index * HD, HD), HD)

    def pair_rows(index):
        return pl.ds(pl.multiple_of(index * 2 * width, 2 * width), 2 * width)

    def tensor_peer(k):
        return lax.rem(t + k, T)

    def line_peer(k):
        return lax.rem(z + k, Z)

    def push(src, dst, send, recv, device):
        pltpu.make_async_remote_copy(
            src_ref=src,
            dst_ref=dst,
            send_sem=send,
            recv_sem=recv,
            device_id=device,
            device_id_type=MESH,
        ).start()

    stage = [
        pltpu.make_async_copy(audio, arecv.at[me], local_sem.at[0]),
        pltpu.make_async_copy(hidden, hid, local_sem.at[1]),
    ]
    late = [
        pltpu.make_async_copy(wo_hbm.at[0], wo, local_sem.at[2]),
        pltpu.make_async_copy(
            wq.at[0, pair_rows(z), :], w_all.at[:, lanes(z)], local_sem.at[3]
        ),
    ]
    for h in range(KVH):
        late.append(
            pltpu.make_async_copy(
                wkv.at[0, :, lanes(2 * h + y)],
                w_all.at[own_half, pl.ds(q_cols + h * HD, HD)],
                local_sem.at[4 + h],
            )
        )

    barrier = pltpu.get_barrier_semaphore()

    def greet(device):
        pl.semaphore_signal(barrier, inc=1, device_id=device, device_id_type=MESH)

    for k in range(1, T):
        greet({"tensor": tensor_peer(k)})
    for k in range(1, S):
        greet({"section": lax.rem(me + k, S)})
    for k in range(1, T):
        greet({"section": after, "tensor": tensor_peer(k)})
        greet({"section": before, "tensor": tensor_peer(k)})
    for copy in stage + late:
        copy.start()
    gain_own[...] = jnp.broadcast_to(gain[...].astype(F32), (8, width))
    gain_pair[:, own_half] = gain_own[...]
    pl.semaphore_wait(barrier, 3 * (T - 1) + S - 1)

    for k in range(1, S):
        push(
            audio,
            arecv.at[me],
            w_sems.at[0, 0],
            w_sems.at[1, 0],
            {"section": lax.rem(me + k, S)},
        )
    push(
        gain_own,
        gain_pair.at[:, own_half],
        w_sems.at[0, 1],
        w_sems.at[1, 1],
        {"tensor": partner},
    )
    for h in range(KVH):
        push(
            wkv.at[0, :, lanes(2 * h + 1 - y)],
            w_all.at[own_half, pl.ds(q_cols + h * HD, HD)],
            w_sems.at[0, 3],
            w_sems.at[1, 3],
            {"tensor": partner},
        )
    for k in range(1, Z):
        other = line_peer(k)
        push(
            wq.at[0, pair_rows(other), :],
            w_all.at[:, lanes(z)],
            w_sems.at[0, 4],
            w_sems.at[1, 4],
            {"tensor": other * 2 + y},
        )

    for target in (t,) if DIRECT == STEPS - 1 else (t, partner):
        push(
            wo_hbm.at[0],
            wo_before if DIRECT == STEPS - 1 else wo_before.at[:, own_half],
            w_sems.at[0, 5],
            w_sems.at[1, 5],
            {"section": after, "tensor": target},
        )

    N = dest.shape[1]
    drow = dest[...].astype(F32)
    sub, lane = iota((N, N), 0), iota((N, N), 1)
    dcol = jnp.sum(jnp.where(sub == lane, drow, 0.0), axis=1, keepdims=True)
    same = (dcol == drow) & ((sub >> 5) == (lane >> 5)) & (sub < lane)
    rank = jnp.sum(jnp.where(same, 1.0, 0.0), axis=0, keepdims=True)
    block = (iota((1, N), 1) >> 5).astype(F32)
    slot = block * float(cap) + rank
    mine = drow == me.astype(F32)

    for copy in stage:
        copy.wait()
    drain(arecv.at[pl.ds(0, S - 1)], w_sems.at[1, 0])
    every_row = arecv[...].reshape(N, width)
    for m in range(MB_DEV):
        wanted = (iota((AUD_MB, N), 0) + m * AUD_MB).astype(F32)
        chosen = jnp.where((slot == wanted) & mine, 1.0, 0.0).astype(BF16)
        rows = jnp.dot(chosen, every_row, preferred_element_type=F32)
        xs[0, m, 0:AUD_MB, own_half] = rows.astype(BF16)
        xs[0, m, AUD_MB:MB_ROWS, own_half] = hid[m * TXT_MB : (m + 1) * TXT_MB, :]
        push(
            xs.at[0, m, :, own_half],
            xs.at[0, m, :, own_half],
            w_sems.at[0, 2],
            recv_sems.at[0, m, 5],
            {"tensor": partner},
        )
    for copy in late:
        copy.wait()

    eye = iota((MB_ROWS, MB_ROWS), 0) == iota((MB_ROWS, MB_ROWS), 1)
    causal = iota((MB_ROWS, MB_ROWS), 1) <= iota((MB_ROWS, MB_ROWS), 0)
    scale = 1.0 / math.sqrt(HD)

    def to_col(row):
        return jnp.sum(jnp.where(eye, row, 0.0), axis=1, keepdims=True)

    def to_row(col):
        return jnp.sum(jnp.where(eye, col, 0.0), axis=0, keepdims=True)

    def allowed_of(root, m):
        seg_row = segment[pl.ds(root * MB_DEV + m, 1), :].astype(F32)
        seg_col = to_col(seg_row)
        position = iota((MB_ROWS, N), 0)
        owner = ((position + m * AUD_MB) >> shift).astype(F32)
        named = (drow == root.astype(F32)) & (block == owner)
        count = jnp.sum(jnp.where(named, 1.0, 0.0), axis=1, keepdims=True)
        index = iota((MB_ROWS, 1), 0)
        within = (index & (cap - 1)).astype(F32)
        live = jnp.where((within < count) | (index >= AUD_MB), 1.0, 0.0)
        return causal & (seg_col == seg_row) & ((to_row(live) > 0.5) | eye)

    def arrive(s, m, columns):
        if s == DIRECT + 1 and m == 0:
            drain(wo_before, w_sems.at[1, 5])
        drain(xold.at[s, m, :, pl.ds(0, width if s == STEPS else 2 * width)], recv_sems.at[s, m, 5])
        drain(att.at[s - 1, m], recv_sems.at[s - 1, m, 4])
        projected = jnp.dot(
            att[s - 1, m],
            wo_before[...] if DIRECT == STEPS - 1 else wo_before[:, columns],
            preferred_element_type=F32,
        )
        return xold[s, m, :, columns].astype(F32) + projected

    def project_kv(s, m, first):
        if first:
            drain(xs.at[0, m, :, pl.ds(0, width)], recv_sems.at[0, m, 5])
            x = xs[s, m].astype(F32)
        elif s <= DIRECT:
            drain(xs.at[s, m], recv_sems.at[s, m, 5])
            x = xs[s, m].astype(F32)
        else:
            x = arrive(s, m, slice(None)).astype(BF16)
            xs[s, m] = x
            x = x.astype(F32)
        if s >= DIRECT:
            wanted = own_half if s == STEPS - 1 else slice(None)
            push(
                xs.at[s, m, :, wanted],
                xold.at[s + 1, m, :, wanted],
                send_sems.at[s, m, 5],
                recv_sems.at[s + 1, m, 5],
                {"section": after},
            )
        sums = to_row(jnp.sum(x * x, axis=1, keepdims=True))
        both = jnp.concatenate([sums, sums], axis=1)
        high = both.astype(BF16).astype(F32)
        place = iota((SQ_ROWS, HD), 0)
        squares = jnp.where(place == 0, high, jnp.where(place == 1, both - high, 0.0)).astype(BF16)
        xg = (x * gain_pair[0:1, :]).astype(BF16)
        if first and m == 0:
            drain(w_all.at[pl.ds(0, width), pl.ds(0, kv_cols)], w_sems.at[1, 3])
        accum[m, :, q_cols:] = jnp.dot(xg, w_all[:, q_cols:], preferred_element_type=F32)
        for k in range(1, Z):
            other = line_peer(k)
            block_of = lanes(Z + lax.div(other, per_kv))
            kvsend[s, m, k - 1, 0:MB_ROWS, :] = accum[m, :, block_of].astype(BF16)
            kvsend[s, m, k - 1, MB_ROWS:, :] = squares
            push(
                kvsend.at[s, m, k - 1],
                kvrecv.at[s, m, k - 1],
                send_sems.at[s, m, 2],
                recv_sems.at[s, m, 2],
                {"tensor": other * 2 + y},
            )
        return xg, sums

    def project_q(s, m, first, xg):
        if first and m == 0:
            drain(w_all.at[:, pl.ds(0, (Z - 1) * HD)], w_sems.at[1, 4])
        accum[m, :, :q_cols] = jnp.dot(xg, w_all[:, :q_cols], preferred_element_type=F32)
        for k in range(1, Z):
            other = line_peer(k)
            qsend[s, m, k - 1] = accum[m, :, lanes(other)].astype(BF16)
            push(
                qsend.at[s, m, k - 1],
                qrecv.at[s, m, k - 1],
                send_sems.at[s, m, 1],
                recv_sems.at[s, m, 1],
                {"tensor": other * 2 + y},
            )

    is_key = y == 0

    def swap(s, m, sums):
        drain(kvrecv.at[s, m], recv_sems.at[s, m, 2])
        arrived = jnp.sum(kvrecv[s, m].astype(F32), axis=0)
        squares = arrived[MB_ROWS : MB_ROWS + 1, 0:MB_ROWS]
        squares = squares + arrived[MB_ROWS + 1 : MB_ROWS + 2, 0:MB_ROWS]
        inverse = to_col(lax.rsqrt((sums + squares) / D + 1e-05))
        keyval = accum[m, :, lanes(Z + lax.div(z, per_kv))] + arrived[0:MB_ROWS]
        keyval = keyval * inverse
        cos_kv = jnp.where(is_key, cos_ref[...], 1.0)
        sin_kv = jnp.where(is_key, sin_ref[...], 0.0)
        keyval = keyval * cos_kv + pltpu.roll(keyval, HD // 2, 1) * sin_kv
        swsend[s, m] = keyval.astype(BF16)
        push(
            swsend.at[s, m],
            swrecv.at[s, m],
            send_sems.at[s, m, 3],
            recv_sems.at[s, m, 3],
            {"tensor": partner},
        )
        return inverse

    def attend(s, m, inverse, mask):
        drain(qrecv.at[s, m], recv_sems.at[s, m, 1])
        arrived = jnp.sum(qrecv[s, m].astype(F32), axis=0)
        query = (accum[m, :, lanes(z)] + arrived) * inverse
        query = query * cos_ref[...] + pltpu.roll(query, HD // 2, 1) * sin_ref[...]
        drain(swrecv.at[s, m], recv_sems.at[s, m, 3])
        own, got = swsend[s, m], swrecv[s, m]
        keys = jnp.where(is_key, own, got)
        values = jnp.where(is_key, got, own)
        scores = lax.dot_general(
            query.astype(BF16), keys, (((1,), (1,)), ((), ())), preferred_element_type=F32
        )
        scores = jnp.where(mask, scores * scale, -jnp.inf)
        highest = jnp.max(scores, axis=-1, keepdims=True)
        weights = jnp.exp(scores - highest)
        probs = (weights / jnp.sum(weights, axis=-1, keepdims=True)).astype(BF16)
        attended = jnp.dot(probs, values, preferred_element_type=F32)
        if s >= DIRECT:
            attsend[s, m] = attended.astype(BF16)
            for k in range(T):
                push(
                    attsend.at[s, m],
                    att.at[s, m, :, lanes(t)],
                    send_sems.at[s, m, 4],
                    recv_sems.at[s, m, 4],
                    {"section": after, "tensor": tensor_peer(k)},
                )
            return
        att[s, m, :, lanes(t)] = attended.astype(BF16)
        for k in range(1, T):
            push(
                att.at[s, m, :, lanes(t)],
                att.at[s, m, :, lanes(t)],
                send_sems.at[s, m, 4],
                recv_sems.at[s, m, 4],
                {"tensor": tensor_peer(k)},
            )

    def leave(s, m):
        drain(att.at[s, m, :, pl.ds(0, (T - 1) * HD)], recv_sems.at[s, m, 4])
        projected = jnp.dot(att[s, m], wo[...], preferred_element_type=F32)
        xnew[s, m] = (xs[s, m, :, own_half].astype(F32) + projected).astype(BF16)
        for target in (t, partner):
            push(
                xnew.at[s, m],
                xs.at[s + 1, m, :, own_half],
                send_sems.at[s, m, 5],
                recv_sems.at[s + 1, m, 5],
                {"section": after, "tensor": target},
            )

    def step(s, first):
        root = lax.rem(me - s + 2 * S, S)
        each = range(MB_DEV)
        gained = []
        for m in each:
            gained.append(project_kv(s, m, first))
            if not first:
                project_q(s, m, first, gained[m][0])
        masks = [allowed_of(root, m) for m in each]
        inverses = [swap(s, m, gained[m][1]) for m in each]
        if first:
            for m in each:
                project_q(s, m, first, gained[m][0])
        for m in range(MB_DEV):
            attend(s, m, inverses[m], masks[m])
        if s < DIRECT:
            for m in each:
                leave(s, m)

    drain(gain_own, w_sems.at[1, 1])
    for s in range(STEPS):
        step(s, s == 0)
    for m in range(MB_DEV):
        out[m * MB_ROWS : (m + 1) * MB_ROWS, :] = arrive(STEPS, m, own_half).astype(BF16)

    drain(arecv.at[pl.ds(0, S - 1)], w_sems.at[0, 0])
    drain(gain_own, w_sems.at[0, 1])
    drain(xs.at[0, :, :, pl.ds(0, width)], w_sems.at[0, 2])
    drain(w_all.at[pl.ds(0, width), pl.ds(0, kv_cols)], w_sems.at[0, 3])
    drain(w_all.at[:, pl.ds(0, (Z - 1) * HD)], w_sems.at[0, 4])

    drain(wo_before, w_sems.at[0, 5])
    for s in range(STEPS):
        for m in range(MB_DEV):
            drain(qsend.at[s, m], send_sems.at[s, m, 1])
            drain(kvsend.at[s, m], send_sems.at[s, m, 2])
            drain(swsend.at[s, m], send_sems.at[s, m, 3])
            sent = T if s >= DIRECT else T - 1
            drain(att.at[s, m, :, pl.ds(0, sent * HD)], send_sems.at[s, m, 4])
            sent = width if s == STEPS - 1 else 2 * width
            drain(xs.at[s, m, :, pl.ds(0, sent)], send_sems.at[s, m, 5])


def local(S, T, hidden, audio, audio_dest, segment, norm_gain, w_query, w_keyval, w_out):
    width = hidden.shape[1]
    rows = MB_DEV * MB_ROWS
    Z = T // 2
    cols = (Z + KVH) * HD
    cosine, sine = rope_tables()
    vmem = pl.BlockSpec(memory_space=pltpu.VMEM)
    hbm = pl.BlockSpec(memory_space=pl.ANY)
    per = (STEPS, MB_DEV)
    scratch = [
        pltpu.VMEM((2 * width, cols), BF16),
        pltpu.VMEM(w_out.shape[1:], BF16),
        pltpu.VMEM((T * HD, width if DIRECT == STEPS - 1 else 2 * width), BF16),
        pltpu.VMEM((S, AUD_DEV, width), BF16),
        pltpu.VMEM((MB_DEV * TXT_MB, width), BF16),
        pltpu.VMEM((8, width), F32),
        pltpu.VMEM((8, 2 * width), F32),
        pltpu.VMEM(per + (MB_ROWS, 2 * width), BF16),
        pltpu.VMEM((STEPS + 1, MB_DEV, MB_ROWS, 2 * width), BF16),
        pltpu.VMEM(per + (MB_ROWS, width), BF16),
        pltpu.VMEM((MB_DEV, MB_ROWS, cols), F32),
        pltpu.VMEM(per + (Z - 1, MB_ROWS, HD), BF16),
        pltpu.VMEM(per + (Z - 1, MB_ROWS, HD), BF16),
        pltpu.VMEM(per + (Z - 1, MB_ROWS + SQ_ROWS, HD), BF16),
        pltpu.VMEM(per + (Z - 1, MB_ROWS + SQ_ROWS, HD), BF16),
        pltpu.VMEM(per + (MB_ROWS, HD), BF16),
        pltpu.VMEM(per + (MB_ROWS, HD), BF16),
        pltpu.VMEM(per + (MB_ROWS, T * HD), BF16),
        pltpu.VMEM(per + (MB_ROWS, HD), BF16),
        pltpu.SemaphoreType.DMA((4 + KVH,)),
        pltpu.SemaphoreType.DMA((2, 6)),
        pltpu.SemaphoreType.DMA(per + (6,)),
        pltpu.SemaphoreType.DMA((STEPS + 1, MB_DEV, 6)),
    ]
    return pl.pallas_call(
        functools.partial(kernel, S, T),
        out_shape=jax.ShapeDtypeStruct((rows, width), BF16),
        in_specs=[hbm, hbm, vmem, vmem, vmem, hbm, hbm, hbm, vmem, vmem],
        out_specs=vmem,
        scratch_shapes=scratch,
        compiler_params=pltpu.CompilerParams(
            collective_id=0, has_side_effects=True, vmem_limit_bytes=62 * 1024 * 1024
        ),
        cost_estimate=pl.CostEstimate(
            flops=STEPS * rows * width * (2 * cols + T * HD) * 2,
            bytes_accessed=8 * 1024 * 1024,
            transcendentals=0,
        ),
    )(
        hidden,
        audio,
        audio_dest.reshape(1, -1),
        segment,
        norm_gain,
        w_query,
        w_keyval,
        w_out,
        jnp.asarray(cosine),
        jnp.asarray(sine),
    )


def solution(mesh):
    in_specs = (
        P("section", "tensor"),
        P("section", "tensor"),
        P(),
        P(),
        P("section", "tensor"),
        P("section", None, "tensor"),
        P("section", "tensor", None),
        P("section", None, "tensor"),
    )
    out_specs = P("section", "tensor")
    body = functools.partial(local, mesh.shape["section"], mesh.shape["tensor"])
    return jax.shard_map(body, mesh=mesh, in_specs=in_specs, out_specs=out_specs, check_vma=False)
```

```python
import functools
import math

import jax
import jax.numpy as jnp
import numpy as np
from jax import lax
from jax.experimental import pallas as pl
from jax.experimental.pallas import tpu as pltpu
from jax.sharding import PartitionSpec as P

D = 8192
HD = 128
KVH = 4
MB_DEV = 2
AUD_MB = 32
TXT_MB = 32
AUD_DEV = 32
STEPS = 4
DIRECT = 3
MB_ROWS = 64
SQ_ROWS = 16
MESH = pl.DeviceIdType.MESH
F32 = jnp.float32
BF16 = jnp.bfloat16


def rope_tables():
    position = np.arange(MB_ROWS, dtype=np.float32)
    freq = np.float32(500000.0) ** (-(2.0 * np.arange(HD // 2, dtype=np.float32)) / HD)
    angle = (position[:, None] * freq[None, :].astype(np.float32)).astype(np.float32)
    cosine, sine = np.cos(angle), np.sin(angle)
    return (
        np.concatenate([cosine, cosine], 1).astype(np.float32),
        np.concatenate([-sine, sine], 1).astype(np.float32),
    )


def iota(shape, dim):
    return lax.broadcasted_iota(jnp.int32, shape, dim)


def drain(ref, sem):
    pltpu.make_async_copy(ref, ref, sem).wait()


def kernel(
    S,
    T,
    hidden,
    audio,
    dest,
    segment,
    gain,
    wq,
    wkv,
    wo_hbm,
    cos_ref,
    sin_ref,
    out,
    w_all,
    wo,
    wo_before,
    arecv,
    hid,
    gain_own,
    gain_pair,
    xs,
    xold,
    xnew,
    accum,
    qsend,
    qrecv,
    kvsend,
    kvrecv,
    swsend,
    swrecv,
    att,
    attsend,
    local_sem,
    w_sems,
    send_sems,
    recv_sems,
):
    Z = T // 2
    width = gain.shape[1]
    cap = MB_DEV * AUD_MB // S
    shift = cap.bit_length() - 1
    per_kv = Z // KVH
    q_cols = Z * HD
    kv_cols = KVH * HD
    me = lax.axis_index("section")
    t = lax.axis_index("tensor")
    y = lax.rem(t, 2)
    z = lax.div(t, 2)
    partner = t + 1 - 2 * y
    after = lax.rem(me + 1, S)
    before = lax.rem(me + S - 1, S)
    own_half = pl.ds(pl.multiple_of(y * width, width), width)

    def lanes(index):
        return pl.ds(pl.multiple_of(index * HD, HD), HD)

    def pair_rows(index):
        return pl.ds(pl.multiple_of(index * 2 * width, 2 * width), 2 * width)

    def tensor_peer(k):
        return lax.rem(t + k, T)

    def line_peer(k):
        return lax.rem(z + k, Z)

    def push(src, dst, send, recv, device):
        pltpu.make_async_remote_copy(
            src_ref=src,
            dst_ref=dst,
            send_sem=send,
            recv_sem=recv,
            device_id=device,
            device_id_type=MESH,
        ).start()

    stage = [
        pltpu.make_async_copy(audio, arecv.at[me], local_sem.at[0]),
        pltpu.make_async_copy(hidden, hid, local_sem.at[1]),
    ]
    late = [
        pltpu.make_async_copy(wo_hbm.at[0], wo, local_sem.at[2]),
        pltpu.make_async_copy(
            wq.at[0, pair_rows(z), :], w_all.at[:, lanes(z)], local_sem.at[3]
        ),
    ]
    for h in range(KVH):
        late.append(
            pltpu.make_async_copy(
                wkv.at[0, :, lanes(2 * h + y)],
                w_all.at[own_half, pl.ds(q_cols + h * HD, HD)],
                local_sem.at[4 + h],
            )
        )

    barrier = pltpu.get_barrier_semaphore()

    def greet(device):
        pl.semaphore_signal(barrier, inc=1, device_id=device, device_id_type=MESH)

    for k in range(1, T):
        greet({"tensor": tensor_peer(k)})
    for k in range(1, S):
        greet({"section": lax.rem(me + k, S)})
    for k in range(1, T):
        greet({"section": after, "tensor": tensor_peer(k)})
        greet({"section": before, "tensor": tensor_peer(k)})
    for copy in stage + late:
        copy.start()
    gain_own[...] = jnp.broadcast_to(gain[...].astype(F32), (8, width))
    gain_pair[:, own_half] = gain_own[...]
    pl.semaphore_wait(barrier, 3 * (T - 1) + S - 1)

    for k in range(1, S):
        push(
            audio,
            arecv.at[me],
            w_sems.at[0, 0],
            w_sems.at[1, 0],
            {"section": lax.rem(me + k, S)},
        )
    push(
        gain_own,
        gain_pair.at[:, own_half],
        w_sems.at[0, 1],
        w_sems.at[1, 1],
        {"tensor": partner},
    )
    piece = 2 * width // KVH
    for h in range(KVH):
        for k in range(1, Z):
            other = line_peer(k)
            begin = other * 2 * width + h * piece
            push(
                wq.at[0, pl.ds(pl.multiple_of(begin, piece), piece), :],
                w_all.at[pl.ds(h * piece, piece), lanes(z)],
                w_sems.at[0, 4],
                w_sems.at[1, 4],
                {"tensor": other * 2 + y},
            )
        push(
            wkv.at[0, :, lanes(2 * h + 1 - y)],
            w_all.at[own_half, pl.ds(q_cols + h * HD, HD)],
            w_sems.at[0, 3],
            w_sems.at[1, 3],
            {"tensor": partner},
        )

    out_piece = T * HD // 8

    def push_out_rows(first_piece, count):
        for i in range(first_piece, first_piece + count):
            rows_of = pl.ds(i * out_piece, out_piece)
            push(
                wo_hbm.at[0, rows_of, :],
                wo_before.at[rows_of, :],
                w_sems.at[0, 5],
                w_sems.at[1, 5],
                {"section": after},
            )

    N = dest.shape[1]
    drow = dest[...].astype(F32)
    sub, lane = iota((N, N), 0), iota((N, N), 1)
    dcol = jnp.sum(jnp.where(sub == lane, drow, 0.0), axis=1, keepdims=True)
    same = (dcol == drow) & ((sub >> 5) == (lane >> 5)) & (sub < lane)
    rank = jnp.sum(jnp.where(same, 1.0, 0.0), axis=0, keepdims=True)
    block = (iota((1, N), 1) >> 5).astype(F32)
    slot = block * float(cap) + rank
    mine = drow == me.astype(F32)

    for copy in stage:
        copy.wait()
    drain(arecv.at[pl.ds(0, S - 1)], w_sems.at[1, 0])
    every_row = arecv[...].reshape(N, width)
    for m in range(MB_DEV):
        wanted = (iota((AUD_MB, N), 0) + m * AUD_MB).astype(F32)
        chosen = jnp.where((slot == wanted) & mine, 1.0, 0.0).astype(BF16)
        rows = jnp.dot(chosen, every_row, preferred_element_type=F32)
        xs[0, m, 0:AUD_MB, own_half] = rows.astype(BF16)
        xs[0, m, AUD_MB:MB_ROWS, own_half] = hid[m * TXT_MB : (m + 1) * TXT_MB, :]
        push(
            xs.at[0, m, :, own_half],
            xs.at[0, m, :, own_half],
            w_sems.at[0, 2],
            recv_sems.at[0, m, 5],
            {"tensor": partner},
        )
    for copy in late:
        copy.wait()

    eye = iota((MB_ROWS, MB_ROWS), 0) == iota((MB_ROWS, MB_ROWS), 1)
    causal = iota((MB_ROWS, MB_ROWS), 1) <= iota((MB_ROWS, MB_ROWS), 0)
    scale = 1.0 / math.sqrt(HD)

    def to_col(row):
        return jnp.sum(jnp.where(eye, row, 0.0), axis=1, keepdims=True)

    def to_row(col):
        return jnp.sum(jnp.where(eye, col, 0.0), axis=0, keepdims=True)

    def allowed_of(root, m):
        seg_row = segment[pl.ds(root * MB_DEV + m, 1), :].astype(F32)
        seg_col = to_col(seg_row)
        position = iota((MB_ROWS, N), 0)
        owner = ((position + m * AUD_MB) >> shift).astype(F32)
        named = (drow == root.astype(F32)) & (block == owner)
        count = jnp.sum(jnp.where(named, 1.0, 0.0), axis=1, keepdims=True)
        index = iota((MB_ROWS, 1), 0)
        within = (index & (cap - 1)).astype(F32)
        live = jnp.where((within < count) | (index >= AUD_MB), 1.0, 0.0)
        return causal & (seg_col == seg_row) & ((to_row(live) > 0.5) | eye)

    def arrive(s, m, columns):
        if s == DIRECT + 1 and m == 0:
            drain(wo_before, w_sems.at[1, 5])
        drain(xold.at[s, m, :, pl.ds(0, width if s == STEPS else 2 * width)], recv_sems.at[s, m, 5])
        drain(att.at[s - 1, m], recv_sems.at[s - 1, m, 4])
        projected = jnp.dot(
            att[s - 1, m],
            wo_before[...] if DIRECT == STEPS - 1 else wo_before[:, columns],
            preferred_element_type=F32,
        )
        return xold[s, m, :, columns].astype(F32) + projected

    def project_kv(s, m, first):
        if first:
            drain(xs.at[0, m, :, pl.ds(0, width)], recv_sems.at[0, m, 5])
            x = xs[s, m].astype(F32)
        elif s <= DIRECT:
            drain(xs.at[s, m], recv_sems.at[s, m, 5])
            x = xs[s, m].astype(F32)
        else:
            x = arrive(s, m, slice(None)).astype(BF16)
            xs[s, m] = x
            x = x.astype(F32)
        if s >= DIRECT:
            wanted = own_half if s == STEPS - 1 else slice(None)
            push(
                xs.at[s, m, :, wanted],
                xold.at[s + 1, m, :, wanted],
                send_sems.at[s, m, 5],
                recv_sems.at[s + 1, m, 5],
                {"section": after},
            )
        sums = to_row(jnp.sum(x * x, axis=1, keepdims=True))
        both = jnp.concatenate([sums, sums], axis=1)
        high = both.astype(BF16).astype(F32)
        place = iota((SQ_ROWS, HD), 0)
        squares = jnp.where(place == 0, high, jnp.where(place == 1, both - high, 0.0)).astype(BF16)
        xg = (x * gain_pair[0:1, :]).astype(BF16)
        if first and m == 0:
            drain(w_all.at[pl.ds(0, width), pl.ds(0, kv_cols)], w_sems.at[1, 3])
        accum[m, :, q_cols:] = jnp.dot(xg, w_all[:, q_cols:], preferred_element_type=F32)
        for k in range(1, Z):
            other = line_peer(k)
            block_of = lanes(Z + lax.div(other, per_kv))
            kvsend[s, m, k - 1, 0:MB_ROWS, :] = accum[m, :, block_of].astype(BF16)
            kvsend[s, m, k - 1, MB_ROWS:, :] = squares
            push(
                kvsend.at[s, m, k - 1],
                kvrecv.at[s, m, k - 1],
                send_sems.at[s, m, 2],
                recv_sems.at[s, m, 2],
                {"tensor": other * 2 + y},
            )
        return xg, sums

    def project_q(s, m, first, xg):
        if first and m == 0:
            drain(w_all.at[:, pl.ds(0, (Z - 1) * HD)], w_sems.at[1, 4])
        accum[m, :, :q_cols] = jnp.dot(xg, w_all[:, :q_cols], preferred_element_type=F32)
        for k in range(1, Z):
            other = line_peer(k)
            qsend[s, m, k - 1] = accum[m, :, lanes(other)].astype(BF16)
            push(
                qsend.at[s, m, k - 1],
                qrecv.at[s, m, k - 1],
                send_sems.at[s, m, 1],
                recv_sems.at[s, m, 1],
                {"tensor": other * 2 + y},
            )

    is_key = y == 0

    def swap(s, m, sums):
        drain(kvrecv.at[s, m], recv_sems.at[s, m, 2])
        arrived = jnp.sum(kvrecv[s, m].astype(F32), axis=0)
        squares = arrived[MB_ROWS : MB_ROWS + 1, 0:MB_ROWS]
        squares = squares + arrived[MB_ROWS + 1 : MB_ROWS + 2, 0:MB_ROWS]
        inverse = to_col(lax.rsqrt((sums + squares) / D + 1e-05))
        keyval = accum[m, :, lanes(Z + lax.div(z, per_kv))] + arrived[0:MB_ROWS]
        keyval = keyval * inverse
        cos_kv = jnp.where(is_key, cos_ref[...], 1.0)
        sin_kv = jnp.where(is_key, sin_ref[...], 0.0)
        keyval = keyval * cos_kv + pltpu.roll(keyval, HD // 2, 1) * sin_kv
        swsend[s, m] = keyval.astype(BF16)
        push(
            swsend.at[s, m],
            swrecv.at[s, m],
            send_sems.at[s, m, 3],
            recv_sems.at[s, m, 3],
            {"tensor": partner},
        )
        return inverse

    def attend(s, m, inverse, mask):
        drain(qrecv.at[s, m], recv_sems.at[s, m, 1])
        arrived = jnp.sum(qrecv[s, m].astype(F32), axis=0)
        query = (accum[m, :, lanes(z)] + arrived) * inverse
        query = query * cos_ref[...] + pltpu.roll(query, HD // 2, 1) * sin_ref[...]
        drain(swrecv.at[s, m], recv_sems.at[s, m, 3])
        own, got = swsend[s, m], swrecv[s, m]
        keys = jnp.where(is_key, own, got)
        values = jnp.where(is_key, got, own)
        scores = lax.dot_general(
            query.astype(BF16), keys, (((1,), (1,)), ((), ())), preferred_element_type=F32
        )
        scores = jnp.where(mask, scores * scale, -jnp.inf)
        highest = jnp.max(scores, axis=-1, keepdims=True)
        weights = jnp.exp(scores - highest)
        probs = (weights / jnp.sum(weights, axis=-1, keepdims=True)).astype(BF16)
        attended = jnp.dot(probs, values, preferred_element_type=F32)
        if s >= DIRECT:
            attsend[s, m] = attended.astype(BF16)
            for k in range(T):
                push(
                    attsend.at[s, m],
                    att.at[s, m, :, lanes(t)],
                    send_sems.at[s, m, 4],
                    recv_sems.at[s, m, 4],
                    {"section": after, "tensor": tensor_peer(k)},
                )
            return
        att[s, m, :, lanes(t)] = attended.astype(BF16)
        for k in range(1, T):
            push(
                att.at[s, m, :, lanes(t)],
                att.at[s, m, :, lanes(t)],
                send_sems.at[s, m, 4],
                recv_sems.at[s, m, 4],
                {"tensor": tensor_peer(k)},
            )

    def leave(s, m):
        drain(att.at[s, m, :, pl.ds(0, (T - 1) * HD)], recv_sems.at[s, m, 4])
        projected = jnp.dot(att[s, m], wo[...], preferred_element_type=F32)
        xnew[s, m] = (xs[s, m, :, own_half].astype(F32) + projected).astype(BF16)
        for target in (t, partner):
            push(
                xnew.at[s, m],
                xs.at[s + 1, m, :, own_half],
                send_sems.at[s, m, 5],
                recv_sems.at[s + 1, m, 5],
                {"section": after, "tensor": target},
            )

    def step(s, first):
        root = lax.rem(me - s + 2 * S, S)
        each = range(MB_DEV)
        gained = []
        for m in each:
            gained.append(project_kv(s, m, first))
            if not first:
                project_q(s, m, first, gained[m][0])
        masks = [allowed_of(root, m) for m in each]
        inverses = [swap(s, m, gained[m][1]) for m in each]
        if first:
            for m in each:
                project_q(s, m, first, gained[m][0])
        spread = s in (DIRECT - 2, DIRECT - 1)
        done = 4 * (s - DIRECT + 2)
        if spread:
            push_out_rows(done, 1)
        for m in each:
            attend(s, m, inverses[m], masks[m])
        if spread:
            push_out_rows(done + 1, 2)
        if s < DIRECT:
            for m in each:
                leave(s, m)
        if spread:
            push_out_rows(done + 3, 1)

    drain(gain_own, w_sems.at[1, 1])
    for s in range(STEPS):
        step(s, s == 0)
    for m in range(MB_DEV):
        out[m * MB_ROWS : (m + 1) * MB_ROWS, :] = arrive(STEPS, m, own_half).astype(BF16)

    drain(arecv.at[pl.ds(0, S - 1)], w_sems.at[0, 0])
    drain(gain_own, w_sems.at[0, 1])
    drain(xs.at[0, :, :, pl.ds(0, width)], w_sems.at[0, 2])
    drain(w_all.at[pl.ds(0, width), pl.ds(0, kv_cols)], w_sems.at[0, 3])
    drain(w_all.at[:, pl.ds(0, (Z - 1) * HD)], w_sems.at[0, 4])

    drain(wo_before, w_sems.at[0, 5])
    for s in range(STEPS):
        for m in range(MB_DEV):
            drain(qsend.at[s, m], send_sems.at[s, m, 1])
            drain(kvsend.at[s, m], send_sems.at[s, m, 2])
            drain(swsend.at[s, m], send_sems.at[s, m, 3])
            sent = T if s >= DIRECT else T - 1
            drain(att.at[s, m, :, pl.ds(0, sent * HD)], send_sems.at[s, m, 4])
            sent = width if s == STEPS - 1 else 2 * width
            drain(xs.at[s, m, :, pl.ds(0, sent)], send_sems.at[s, m, 5])


def local(S, T, hidden, audio, audio_dest, segment, norm_gain, w_query, w_keyval, w_out):
    width = hidden.shape[1]
    rows = MB_DEV * MB_ROWS
    Z = T // 2
    cols = (Z + KVH) * HD
    cosine, sine = rope_tables()
    vmem = pl.BlockSpec(memory_space=pltpu.VMEM)
    hbm = pl.BlockSpec(memory_space=pl.ANY)
    per = (STEPS, MB_DEV)
    scratch = [
        pltpu.VMEM((2 * width, cols), BF16),
        pltpu.VMEM(w_out.shape[1:], BF16),
        pltpu.VMEM((T * HD, width if DIRECT == STEPS - 1 else 2 * width), BF16),
        pltpu.VMEM((S, AUD_DEV, width), BF16),
        pltpu.VMEM((MB_DEV * TXT_MB, width), BF16),
        pltpu.VMEM((8, width), F32),
        pltpu.VMEM((8, 2 * width), F32),
        pltpu.VMEM(per + (MB_ROWS, 2 * width), BF16),
        pltpu.VMEM((STEPS + 1, MB_DEV, MB_ROWS, 2 * width), BF16),
        pltpu.VMEM(per + (MB_ROWS, width), BF16),
        pltpu.VMEM((MB_DEV, MB_ROWS, cols), F32),
        pltpu.VMEM(per + (Z - 1, MB_ROWS, HD), BF16),
        pltpu.VMEM(per + (Z - 1, MB_ROWS, HD), BF16),
        pltpu.VMEM(per + (Z - 1, MB_ROWS + SQ_ROWS, HD), BF16),
        pltpu.VMEM(per + (Z - 1, MB_ROWS + SQ_ROWS, HD), BF16),
        pltpu.VMEM(per + (MB_ROWS, HD), BF16),
        pltpu.VMEM(per + (MB_ROWS, HD), BF16),
        pltpu.VMEM(per + (MB_ROWS, T * HD), BF16),
        pltpu.VMEM(per + (MB_ROWS, HD), BF16),
        pltpu.SemaphoreType.DMA((4 + KVH,)),
        pltpu.SemaphoreType.DMA((2, 6)),
        pltpu.SemaphoreType.DMA(per + (6,)),
        pltpu.SemaphoreType.DMA((STEPS + 1, MB_DEV, 6)),
    ]
    return pl.pallas_call(
        functools.partial(kernel, S, T),
        out_shape=jax.ShapeDtypeStruct((rows, width), BF16),
        in_specs=[hbm, hbm, vmem, vmem, vmem, hbm, hbm, hbm, vmem, vmem],
        out_specs=vmem,
        scratch_shapes=scratch,
        compiler_params=pltpu.CompilerParams(
            collective_id=0, has_side_effects=True, vmem_limit_bytes=62 * 1024 * 1024
        ),
        cost_estimate=pl.CostEstimate(
            flops=STEPS * rows * width * (2 * cols + T * HD) * 2,
            bytes_accessed=8 * 1024 * 1024,
            transcendentals=0,
        ),
    )(
        hidden,
        audio,
        audio_dest.reshape(1, -1),
        segment,
        norm_gain,
        w_query,
        w_keyval,
        w_out,
        jnp.asarray(cosine),
        jnp.asarray(sine),
    )


def solution(mesh):
    in_specs = (
        P("section", "tensor"),
        P("section", "tensor"),
        P(),
        P(),
        P("section", "tensor"),
        P("section", None, "tensor"),
        P("section", "tensor", None),
        P("section", None, "tensor"),
    )
    out_specs = P("section", "tensor")
    body = functools.partial(local, mesh.shape["section"], mesh.shape["tensor"])
    return jax.shard_map(body, mesh=mesh, in_specs=in_specs, out_specs=out_specs, check_vma=False)
```

```python
import functools
import math

import jax
import jax.numpy as jnp
import numpy as np
from jax import lax
from jax.experimental import pallas as pl
from jax.experimental.pallas import tpu as pltpu
from jax.sharding import PartitionSpec as P

D = 8192
HD = 128
KVH = 4
MB_DEV = 2
AUD_MB = 32
TXT_MB = 32
AUD_DEV = 32
STEPS = 4
MB_ROWS = 64
SQ_ROWS = 16
MESH = pl.DeviceIdType.MESH
F32 = jnp.float32
BF16 = jnp.bfloat16


def rope_tables():
    position = np.arange(MB_ROWS, dtype=np.float32)
    freq = np.float32(500000.0) ** (-(2.0 * np.arange(HD // 2, dtype=np.float32)) / HD)
    angle = (position[:, None] * freq[None, :].astype(np.float32)).astype(np.float32)
    cosine, sine = np.cos(angle), np.sin(angle)
    return (
        np.concatenate([cosine, cosine], 1).astype(np.float32),
        np.concatenate([-sine, sine], 1).astype(np.float32),
    )


def iota(shape, dim):
    return lax.broadcasted_iota(jnp.int32, shape, dim)


def drain(ref, sem):
    pltpu.make_async_copy(ref, ref, sem).wait()


def kernel(
    S,
    T,
    hidden,
    audio,
    dest,
    segment,
    gain,
    wq,
    wkv,
    wo_hbm,
    cos_ref,
    sin_ref,
    out,
    w_all,
    wo,
    arecv,
    hid,
    gain_own,
    gain_pair,
    xs,
    xnew,
    accum,
    qsend,
    qrecv,
    kvsend,
    kvrecv,
    swsend,
    swrecv,
    att,
    xgain,
    squares_own,
    inverses,
    masks,
    local_sem,
    w_sems,
    send_sems,
    recv_sems,
):
    Z = T // 2
    width = gain.shape[1]
    cap = MB_DEV * AUD_MB // S
    shift = cap.bit_length() - 1
    per_kv = Z // KVH
    q_cols = Z * HD
    kv_cols = KVH * HD
    me = lax.axis_index("section")
    t = lax.axis_index("tensor")
    y = lax.rem(t, 2)
    z = lax.div(t, 2)
    partner = t + 1 - 2 * y
    after = lax.rem(me + 1, S)
    before = lax.rem(me + S - 1, S)
    own_half = pl.ds(pl.multiple_of(y * width, width), width)

    def lanes(index):
        return pl.ds(pl.multiple_of(index * HD, HD), HD)

    def pair_rows(index):
        return pl.ds(pl.multiple_of(index * 2 * width, 2 * width), 2 * width)

    def tensor_peer(k):
        return lax.rem(t + k, T)

    def line_peer(k):
        return lax.rem(z + k, Z)

    def push(src, dst, send, recv, device):
        pltpu.make_async_remote_copy(
            src_ref=src,
            dst_ref=dst,
            send_sem=send,
            recv_sem=recv,
            device_id=device,
            device_id_type=MESH,
        ).start()

    stage = [
        pltpu.make_async_copy(audio, arecv.at[me], local_sem.at[0]),
        pltpu.make_async_copy(hidden, hid, local_sem.at[1]),
    ]
    late = [
        pltpu.make_async_copy(wo_hbm.at[0], wo, local_sem.at[2]),
        pltpu.make_async_copy(
            wq.at[0, pair_rows(z), :], w_all.at[:, lanes(z)], local_sem.at[3]
        ),
    ]
    for h in range(KVH):
        late.append(
            pltpu.make_async_copy(
                wkv.at[0, :, lanes(2 * h + y)],
                w_all.at[own_half, pl.ds(q_cols + h * HD, HD)],
                local_sem.at[4 + h],
            )
        )

    barrier = pltpu.get_barrier_semaphore()

    def greet(device):
        pl.semaphore_signal(barrier, inc=1, device_id=device, device_id_type=MESH)

    for k in range(1, T):
        greet({"tensor": tensor_peer(k)})
    for k in range(1, S):
        greet({"section": lax.rem(me + k, S)})
    greet({"section": after, "tensor": partner})
    greet({"section": before, "tensor": partner})
    for copy in stage + late:
        copy.start()
    gain_own[...] = jnp.broadcast_to(gain[...].astype(F32), (8, width))
    gain_pair[:, own_half] = gain_own[...]
    pl.semaphore_wait(barrier, T + S)

    for k in range(1, S):
        push(
            audio,
            arecv.at[me],
            w_sems.at[0, 0],
            w_sems.at[1, 0],
            {"section": lax.rem(me + k, S)},
        )
    push(
        gain_own,
        gain_pair.at[:, own_half],
        w_sems.at[0, 1],
        w_sems.at[1, 1],
        {"tensor": partner},
    )
    for h in range(KVH):
        push(
            wkv.at[0, :, lanes(2 * h + 1 - y)],
            w_all.at[own_half, pl.ds(q_cols + h * HD, HD)],
            w_sems.at[0, 3],
            w_sems.at[1, 3],
            {"tensor": partner},
        )
    for k in range(1, Z):
        other = line_peer(k)
        push(
            wq.at[0, pair_rows(other), :],
            w_all.at[:, lanes(z)],
            w_sems.at[0, 4],
            w_sems.at[1, 4],
            {"tensor": other * 2 + y},
        )

    N = dest.shape[1]
    drow = dest[...].astype(F32)
    sub, lane = iota((N, N), 0), iota((N, N), 1)
    dcol = jnp.sum(jnp.where(sub == lane, drow, 0.0), axis=1, keepdims=True)
    same = (dcol == drow) & ((sub >> 5) == (lane >> 5)) & (sub < lane)
    rank = jnp.sum(jnp.where(same, 1.0, 0.0), axis=0, keepdims=True)
    block = (iota((1, N), 1) >> 5).astype(F32)
    slot = block * float(cap) + rank
    mine = drow == me.astype(F32)

    for copy in stage:
        copy.wait()
    drain(arecv.at[pl.ds(0, S - 1)], w_sems.at[1, 0])
    every_row = arecv[...].reshape(N, width)
    for m in range(MB_DEV):
        wanted = (iota((AUD_MB, N), 0) + m * AUD_MB).astype(F32)
        chosen = jnp.where((slot == wanted) & mine, 1.0, 0.0).astype(BF16)
        rows = jnp.dot(chosen, every_row, preferred_element_type=F32)
        xs[0, m, 0:AUD_MB, own_half] = rows.astype(BF16)
        xs[0, m, AUD_MB:MB_ROWS, own_half] = hid[m * TXT_MB : (m + 1) * TXT_MB, :]
        push(
            xs.at[0, m, :, own_half],
            xs.at[0, m, :, own_half],
            w_sems.at[0, 2],
            recv_sems.at[0, m, 5],
            {"tensor": partner},
        )
    for copy in late:
        copy.wait()

    eye = iota((MB_ROWS, MB_ROWS), 0) == iota((MB_ROWS, MB_ROWS), 1)
    causal = iota((MB_ROWS, MB_ROWS), 1) <= iota((MB_ROWS, MB_ROWS), 0)
    scale = 1.0 / math.sqrt(HD)

    def to_col(row):
        return jnp.sum(jnp.where(eye, row, 0.0), axis=1, keepdims=True)

    def to_row(col):
        return jnp.sum(jnp.where(eye, col, 0.0), axis=0, keepdims=True)

    def allowed_of(root, m):
        seg_row = segment[pl.ds(root * MB_DEV + m, 1), :].astype(F32)
        seg_col = to_col(seg_row)
        position = iota((MB_ROWS, N), 0)
        owner = ((position + m * AUD_MB) >> shift).astype(F32)
        named = (drow == root.astype(F32)) & (block == owner)
        count = jnp.sum(jnp.where(named, 1.0, 0.0), axis=1, keepdims=True)
        index = iota((MB_ROWS, 1), 0)
        within = (index & (cap - 1)).astype(F32)
        live = jnp.where((within < count) | (index >= AUD_MB), 1.0, 0.0)
        return causal & (seg_col == seg_row) & ((to_row(live) > 0.5) | eye)

    def project_kv(s, m):
        @pl.when(s == 0)
        def _():
            drain(xs.at[0, m, :, pl.ds(0, width)], recv_sems.at[0, m, 5])

        @pl.when(s > 0)
        def _():
            drain(xs.at[s, m], recv_sems.at[s, m, 5])

        x = xs[s, m].astype(F32)
        sums = to_row(jnp.sum(x * x, axis=1, keepdims=True))
        both = jnp.concatenate([sums, sums], axis=1)
        high = both.astype(BF16).astype(F32)
        place = iota((SQ_ROWS, HD), 0)
        squares = jnp.where(place == 0, high, jnp.where(place == 1, both - high, 0.0)).astype(BF16)
        squares_own[m] = jnp.broadcast_to(both, (8, HD))
        xgain[m] = (x * gain_pair[0:1, :]).astype(BF16)

        @pl.when((s == 0) & (m == 0))
        def _():
            drain(w_all.at[pl.ds(0, width), pl.ds(0, kv_cols)], w_sems.at[1, 3])
        accum[m, :, q_cols:] = jnp.dot(xgain[m], w_all[:, q_cols:], preferred_element_type=F32)
        for k in range(1, Z):
            other = line_peer(k)
            block_of = lanes(Z + lax.div(other, per_kv))
            kvsend[s, m, k - 1, 0:MB_ROWS, :] = accum[m, :, block_of].astype(BF16)
            kvsend[s, m, k - 1, MB_ROWS:, :] = squares
            push(
                kvsend.at[s, m, k - 1],
                kvrecv.at[s, m, k - 1],
                send_sems.at[s, m, 2],
                recv_sems.at[s, m, 2],
                {"tensor": other * 2 + y},
            )

    def project_q(s, m):
        @pl.when((s == 0) & (m == 0))
        def _():
            drain(w_all.at[:, pl.ds(0, (Z - 1) * HD)], w_sems.at[1, 4])
        accum[m, :, :q_cols] = jnp.dot(xgain[m], w_all[:, :q_cols], preferred_element_type=F32)
        for k in range(1, Z):
            other = line_peer(k)
            qsend[s, m, k - 1] = accum[m, :, lanes(other)].astype(BF16)
            push(
                qsend.at[s, m, k - 1],
                qrecv.at[s, m, k - 1],
                send_sems.at[s, m, 1],
                recv_sems.at[s, m, 1],
                {"tensor": other * 2 + y},
            )

    is_key = y == 0

    def swap(s, m):
        drain(kvrecv.at[s, m], recv_sems.at[s, m, 2])
        arrived = jnp.sum(kvrecv[s, m].astype(F32), axis=0)
        squares = arrived[MB_ROWS : MB_ROWS + 1, 0:MB_ROWS]
        squares = squares + arrived[MB_ROWS + 1 : MB_ROWS + 2, 0:MB_ROWS]
        inverse = to_col(lax.rsqrt((squares_own[m, 0:1, 0:MB_ROWS] + squares) / D + 1e-05))
        keyval = accum[m, :, lanes(Z + lax.div(z, per_kv))] + arrived[0:MB_ROWS]
        keyval = keyval * inverse
        cos_kv = jnp.where(is_key, cos_ref[...], 1.0)
        sin_kv = jnp.where(is_key, sin_ref[...], 0.0)
        keyval = keyval * cos_kv + pltpu.roll(keyval, HD // 2, 1) * sin_kv
        swsend[s, m] = keyval.astype(BF16)
        push(
            swsend.at[s, m],
            swrecv.at[s, m],
            send_sems.at[s, m, 3],
            recv_sems.at[s, m, 3],
            {"tensor": partner},
        )
        inverses[m] = jnp.broadcast_to(inverse, (MB_ROWS, HD))

    def attend(s, m):
        drain(qrecv.at[s, m], recv_sems.at[s, m, 1])
        arrived = jnp.sum(qrecv[s, m].astype(F32), axis=0)
        query = (accum[m, :, lanes(z)] + arrived) * inverses[m]
        query = query * cos_ref[...] + pltpu.roll(query, HD // 2, 1) * sin_ref[...]
        drain(swrecv.at[s, m], recv_sems.at[s, m, 3])
        own, got = swsend[s, m], swrecv[s, m]
        keys = jnp.where(is_key, own, got)
        values = jnp.where(is_key, got, own)
        scores = lax.dot_general(
            query.astype(BF16), keys, (((1,), (1,)), ((), ())), preferred_element_type=F32
        )
        scores = jnp.where(masks[m] > 0.5, scores * scale, -jnp.inf)
        highest = jnp.max(scores, axis=-1, keepdims=True)
        weights = jnp.exp(scores - highest)
        probs = (weights / jnp.sum(weights, axis=-1, keepdims=True)).astype(BF16)
        attended = jnp.dot(probs, values, preferred_element_type=F32)
        att[s, m, :, lanes(t)] = attended.astype(BF16)
        for k in range(1, T):
            push(
                att.at[s, m, :, lanes(t)],
                att.at[s, m, :, lanes(t)],
                send_sems.at[s, m, 4],
                recv_sems.at[s, m, 4],
                {"tensor": tensor_peer(k)},
            )

    def leave(s, m):
        drain(att.at[s, m, :, pl.ds(0, (T - 1) * HD)], recv_sems.at[s, m, 4])
        projected = jnp.dot(att[s, m], wo[...], preferred_element_type=F32)
        xnew[s, m] = (xs[s, m, :, own_half].astype(F32) + projected).astype(BF16)
        def hop(target):
            push(
                xnew.at[s, m],
                xs.at[s + 1, m, :, own_half],
                send_sems.at[s, m, 5],
                recv_sems.at[s + 1, m, 5],
                {"section": after, "tensor": target},
            )

        hop(t)

        @pl.when(s < STEPS - 1)
        def _():
            hop(partner)

    def each(phase):
        def one(m, carry):
            phase(m)
            return carry

        lax.fori_loop(0, MB_DEV, one, 0)

    def step(s, carry):
        root = lax.rem(me - s + 2 * S, S)

        def mask(m):
            masks[m] = jnp.where(allowed_of(root, m), 1.0, 0.0)

        def project(i, inner):
            high, low = lax.div(i, MB_DEV), lax.rem(i, MB_DEV)
            is_q = jnp.where(s == 0, high, low)
            m = jnp.where(s == 0, low, high)

            @pl.when(is_q == 0)
            def _():
                project_kv(s, m)

            @pl.when(is_q == 1)
            def _():
                project_q(s, m)

            return inner

        lax.fori_loop(0, 2 * MB_DEV, project, 0)
        each(mask)
        each(lambda m: swap(s, m))
        each(lambda m: attend(s, m))
        each(lambda m: leave(s, m))
        return carry

    drain(gain_own, w_sems.at[1, 1])
    lax.fori_loop(0, STEPS, step, 0)
    for m in range(MB_DEV):
        drain(xs.at[STEPS, m, :, pl.ds(0, width)], recv_sems.at[STEPS, m, 5])
        out[m * MB_ROWS : (m + 1) * MB_ROWS, :] = xs[STEPS, m, :, own_half]

    drain(arecv.at[pl.ds(0, S - 1)], w_sems.at[0, 0])
    drain(gain_own, w_sems.at[0, 1])
    drain(xs.at[0, :, :, pl.ds(0, width)], w_sems.at[0, 2])
    drain(w_all.at[pl.ds(0, width), pl.ds(0, kv_cols)], w_sems.at[0, 3])
    drain(w_all.at[:, pl.ds(0, (Z - 1) * HD)], w_sems.at[0, 4])

    def finish(s, carry):
        for m in range(MB_DEV):
            drain(qsend.at[s, m], send_sems.at[s, m, 1])
            drain(kvsend.at[s, m], send_sems.at[s, m, 2])
            drain(swsend.at[s, m], send_sems.at[s, m, 3])
            drain(att.at[s, m, :, pl.ds(0, (T - 1) * HD)], send_sems.at[s, m, 4])
            drain(xnew.at[s, m], send_sems.at[s, m, 5])

            @pl.when(s < STEPS - 1)
            def _():
                drain(xnew.at[s, m], send_sems.at[s, m, 5])

        return carry

    lax.fori_loop(0, STEPS, finish, 0)


def local(S, T, hidden, audio, audio_dest, segment, norm_gain, w_query, w_keyval, w_out):
    width = hidden.shape[1]
    rows = MB_DEV * MB_ROWS
    Z = T // 2
    cols = (Z + KVH) * HD
    cosine, sine = rope_tables()
    vmem = pl.BlockSpec(memory_space=pltpu.VMEM)
    hbm = pl.BlockSpec(memory_space=pl.ANY)
    per = (STEPS, MB_DEV)
    scratch = [
        pltpu.VMEM((2 * width, cols), BF16),
        pltpu.VMEM(w_out.shape[1:], BF16),
        pltpu.VMEM((S, AUD_DEV, width), BF16),
        pltpu.VMEM((MB_DEV * TXT_MB, width), BF16),
        pltpu.VMEM((8, width), F32),
        pltpu.VMEM((8, 2 * width), F32),
        pltpu.VMEM((STEPS + 1, MB_DEV, MB_ROWS, 2 * width), BF16),
        pltpu.VMEM(per + (MB_ROWS, width), BF16),
        pltpu.VMEM((MB_DEV, MB_ROWS, cols), F32),
        pltpu.VMEM(per + (Z - 1, MB_ROWS, HD), BF16),
        pltpu.VMEM(per + (Z - 1, MB_ROWS, HD), BF16),
        pltpu.VMEM(per + (Z - 1, MB_ROWS + SQ_ROWS, HD), BF16),
        pltpu.VMEM(per + (Z - 1, MB_ROWS + SQ_ROWS, HD), BF16),
        pltpu.VMEM(per + (MB_ROWS, HD), BF16),
        pltpu.VMEM(per + (MB_ROWS, HD), BF16),
        pltpu.VMEM(per + (MB_ROWS, T * HD), BF16),
        pltpu.VMEM((MB_DEV, MB_ROWS, 2 * width), BF16),
        pltpu.VMEM((MB_DEV, 8, HD), F32),
        pltpu.VMEM((MB_DEV, MB_ROWS, HD), F32),
        pltpu.VMEM((MB_DEV, MB_ROWS, MB_ROWS), F32),
        pltpu.SemaphoreType.DMA((4 + KVH,)),
        pltpu.SemaphoreType.DMA((2, 5)),
        pltpu.SemaphoreType.DMA(per + (6,)),
        pltpu.SemaphoreType.DMA((STEPS + 1, MB_DEV, 6)),
    ]
    return pl.pallas_call(
        functools.partial(kernel, S, T),
        out_shape=jax.ShapeDtypeStruct((rows, width), BF16),
        in_specs=[hbm, hbm, vmem, vmem, vmem, hbm, hbm, hbm, vmem, vmem],
        out_specs=vmem,
        scratch_shapes=scratch,
        compiler_params=pltpu.CompilerParams(
            collective_id=0, has_side_effects=True, vmem_limit_bytes=62 * 1024 * 1024
        ),
        cost_estimate=pl.CostEstimate(
            flops=STEPS * rows * width * (2 * cols + T * HD) * 2,
            bytes_accessed=8 * 1024 * 1024,
            transcendentals=0,
        ),
    )(
        hidden,
        audio,
        audio_dest.reshape(1, -1),
        segment,
        norm_gain,
        w_query,
        w_keyval,
        w_out,
        jnp.asarray(cosine),
        jnp.asarray(sine),
    )


def solution(mesh):
    in_specs = (
        P("section", "tensor"),
        P("section", "tensor"),
        P(),
        P(),
        P("section", "tensor"),
        P("section", None, "tensor"),
        P("section", "tensor", None),
        P("section", None, "tensor"),
    )
    out_specs = P("section", "tensor")
    body = functools.partial(local, mesh.shape["section"], mesh.shape["tensor"])
    return jax.shard_map(body, mesh=mesh, in_specs=in_specs, out_specs=out_specs, check_vma=False)
```

```python
import functools
import math

import jax
import jax.numpy as jnp
import numpy as np
from jax import lax
from jax.experimental import pallas as pl
from jax.experimental.pallas import tpu as pltpu
from jax.sharding import PartitionSpec as P

D = 8192
HD = 128
KVH = 4
MB_DEV = 2
AUD_MB = 32
TXT_MB = 32
AUD_DEV = 32
STEPS = 4
MB_ROWS = 64
SQ_ROWS = 16
MESH = pl.DeviceIdType.MESH
F32 = jnp.float32
BF16 = jnp.bfloat16


def rope_tables():
    position = np.arange(MB_ROWS, dtype=np.float32)
    freq = np.float32(500000.0) ** (-(2.0 * np.arange(HD // 2, dtype=np.float32)) / HD)
    angle = (position[:, None] * freq[None, :].astype(np.float32)).astype(np.float32)
    cosine, sine = np.cos(angle), np.sin(angle)
    return (
        np.concatenate([cosine, cosine], 1).astype(np.float32),
        np.concatenate([-sine, sine], 1).astype(np.float32),
    )


def iota(shape, dim):
    return lax.broadcasted_iota(jnp.int32, shape, dim)


def drain(ref, sem):
    pltpu.make_async_copy(ref, ref, sem).wait()


def kernel(
    S,
    T,
    hidden,
    audio,
    dest,
    segment,
    gain,
    wq,
    wkv,
    wo_hbm,
    cos_ref,
    sin_ref,
    out,
    w_all,
    wo,
    arecv,
    hid,
    gain_own,
    gain_pair,
    xs,
    xnew,
    accum,
    qsend,
    qrecv,
    kvsend,
    kvrecv,
    swsend,
    swrecv,
    att,
    xgain,
    squares_own,
    inverses,
    masks,
    partial,
    local_sem,
    w_sems,
    send_sems,
    recv_sems,
):
    Z = T // 2
    width = gain.shape[1]
    cap = MB_DEV * AUD_MB // S
    shift = cap.bit_length() - 1
    per_kv = Z // KVH
    q_cols = Z * HD
    kv_cols = KVH * HD
    me = lax.axis_index("section")
    t = lax.axis_index("tensor")
    y = lax.rem(t, 2)
    z = lax.div(t, 2)
    partner = t + 1 - 2 * y
    after = lax.rem(me + 1, S)
    before = lax.rem(me + S - 1, S)
    own_half = pl.ds(pl.multiple_of(y * width, width), width)

    def lanes(index):
        return pl.ds(pl.multiple_of(index * HD, HD), HD)

    def pair_rows(index):
        return pl.ds(pl.multiple_of(index * 2 * width, 2 * width), 2 * width)

    def tensor_peer(k):
        return lax.rem(t + k, T)

    def line_peer(k):
        return lax.rem(z + k, Z)

    def push(src, dst, send, recv, device):
        pltpu.make_async_remote_copy(
            src_ref=src,
            dst_ref=dst,
            send_sem=send,
            recv_sem=recv,
            device_id=device,
            device_id_type=MESH,
        ).start()

    stage = [
        pltpu.make_async_copy(audio, arecv.at[me], local_sem.at[0]),
        pltpu.make_async_copy(hidden, hid, local_sem.at[1]),
    ]
    late = [
        pltpu.make_async_copy(
            wq.at[0, pair_rows(z), :], w_all.at[:, lanes(z)], local_sem.at[3]
        ),
    ]
    for h in range(KVH):
        late.append(
            pltpu.make_async_copy(
                wkv.at[0, :, lanes(2 * h + y)],
                w_all.at[own_half, pl.ds(q_cols + h * HD, HD)],
                local_sem.at[4 + h],
            )
        )

    for head in range(T):
        late.append(
            pltpu.make_async_copy(
                wo_hbm.at[0, pl.ds(head * HD, HD), :],
                wo.at[pl.ds((head % 2 * Z + head // 2) * HD, HD), :],
                local_sem.at[4 + KVH + head],
            )
        )

    barrier = pltpu.get_barrier_semaphore()

    def greet(device):
        pl.semaphore_signal(barrier, inc=1, device_id=device, device_id_type=MESH)

    for k in range(1, T):
        greet({"tensor": tensor_peer(k)})
    for k in range(1, S):
        greet({"section": lax.rem(me + k, S)})
    greet({"section": after, "tensor": partner})
    greet({"section": before, "tensor": partner})
    for copy in stage + late:
        copy.start()
    gain_own[...] = jnp.broadcast_to(gain[...].astype(F32), (8, width))
    gain_pair[:, own_half] = gain_own[...]
    pl.semaphore_wait(barrier, T + S)

    for k in range(1, S):
        push(
            audio,
            arecv.at[me],
            w_sems.at[0, 0],
            w_sems.at[1, 0],
            {"section": lax.rem(me + k, S)},
        )
    push(
        gain_own,
        gain_pair.at[:, own_half],
        w_sems.at[0, 1],
        w_sems.at[1, 1],
        {"tensor": partner},
    )
    for h in range(KVH):
        push(
            wkv.at[0, :, lanes(2 * h + 1 - y)],
            w_all.at[own_half, pl.ds(q_cols + h * HD, HD)],
            w_sems.at[0, 3],
            w_sems.at[1, 3],
            {"tensor": partner},
        )
    for k in range(1, Z):
        other = line_peer(k)
        push(
            wq.at[0, pair_rows(other), :],
            w_all.at[:, lanes(z)],
            w_sems.at[0, 4],
            w_sems.at[1, 4],
            {"tensor": other * 2 + y},
        )

    N = dest.shape[1]
    drow = dest[...].astype(F32)
    sub, lane = iota((N, N), 0), iota((N, N), 1)
    dcol = jnp.sum(jnp.where(sub == lane, drow, 0.0), axis=1, keepdims=True)
    same = (dcol == drow) & ((sub >> 5) == (lane >> 5)) & (sub < lane)
    rank = jnp.sum(jnp.where(same, 1.0, 0.0), axis=0, keepdims=True)
    block = (iota((1, N), 1) >> 5).astype(F32)
    slot = block * float(cap) + rank
    mine = drow == me.astype(F32)

    for copy in stage:
        copy.wait()
    drain(arecv.at[pl.ds(0, S - 1)], w_sems.at[1, 0])
    every_row = arecv[...].reshape(N, width)
    for m in range(MB_DEV):
        wanted = (iota((AUD_MB, N), 0) + m * AUD_MB).astype(F32)
        chosen = jnp.where((slot == wanted) & mine, 1.0, 0.0).astype(BF16)
        rows = jnp.dot(chosen, every_row, preferred_element_type=F32)
        xs[0, m, 0:AUD_MB, own_half] = rows.astype(BF16)
        xs[0, m, AUD_MB:MB_ROWS, own_half] = hid[m * TXT_MB : (m + 1) * TXT_MB, :]
        push(
            xs.at[0, m, :, own_half],
            xs.at[0, m, :, own_half],
            w_sems.at[0, 2],
            recv_sems.at[0, m, 5],
            {"tensor": partner},
        )
    for copy in late:
        copy.wait()

    eye = iota((MB_ROWS, MB_ROWS), 0) == iota((MB_ROWS, MB_ROWS), 1)
    causal = iota((MB_ROWS, MB_ROWS), 1) <= iota((MB_ROWS, MB_ROWS), 0)
    scale = 1.0 / math.sqrt(HD)

    def to_col(row):
        return jnp.sum(jnp.where(eye, row, 0.0), axis=1, keepdims=True)

    def to_row(col):
        return jnp.sum(jnp.where(eye, col, 0.0), axis=0, keepdims=True)

    def allowed_of(root, m):
        seg_row = segment[pl.ds(root * MB_DEV + m, 1), :].astype(F32)
        seg_col = to_col(seg_row)
        position = iota((MB_ROWS, N), 0)
        owner = ((position + m * AUD_MB) >> shift).astype(F32)
        named = (drow == root.astype(F32)) & (block == owner)
        count = jnp.sum(jnp.where(named, 1.0, 0.0), axis=1, keepdims=True)
        index = iota((MB_ROWS, 1), 0)
        within = (index & (cap - 1)).astype(F32)
        live = jnp.where((within < count) | (index >= AUD_MB), 1.0, 0.0)
        return causal & (seg_col == seg_row) & ((to_row(live) > 0.5) | eye)

    def project_kv(s, m):
        @pl.when(s == 0)
        def _():
            drain(xs.at[0, m, :, pl.ds(0, width)], recv_sems.at[0, m, 5])

        @pl.when(s > 0)
        def _():
            drain(xs.at[s, m], recv_sems.at[s, m, 5])

        x = xs[s, m].astype(F32)
        sums = to_row(jnp.sum(x * x, axis=1, keepdims=True))
        both = jnp.concatenate([sums, sums], axis=1)
        high = both.astype(BF16).astype(F32)
        place = iota((SQ_ROWS, HD), 0)
        squares = jnp.where(place == 0, high, jnp.where(place == 1, both - high, 0.0)).astype(BF16)
        squares_own[m] = jnp.broadcast_to(both, (8, HD))
        xgain[m] = (x * gain_pair[0:1, :]).astype(BF16)

        @pl.when((s == 0) & (m == 0))
        def _():
            drain(w_all.at[pl.ds(0, width), pl.ds(0, kv_cols)], w_sems.at[1, 3])
        accum[m, :, q_cols:] = jnp.dot(xgain[m], w_all[:, q_cols:], preferred_element_type=F32)
        for k in range(1, Z):
            other = line_peer(k)
            block_of = lanes(Z + lax.div(other, per_kv))
            kvsend[s, m, k - 1, 0:MB_ROWS, :] = accum[m, :, block_of].astype(BF16)
            kvsend[s, m, k - 1, MB_ROWS:, :] = squares
            push(
                kvsend.at[s, m, k - 1],
                kvrecv.at[s, m, k - 1],
                send_sems.at[s, m, 2],
                recv_sems.at[s, m, 2],
                {"tensor": other * 2 + y},
            )

    def project_q(s, m):
        @pl.when((s == 0) & (m == 0))
        def _():
            drain(w_all.at[:, pl.ds(0, (Z - 1) * HD)], w_sems.at[1, 4])
        accum[m, :, :q_cols] = jnp.dot(xgain[m], w_all[:, :q_cols], preferred_element_type=F32)
        for k in range(1, Z):
            other = line_peer(k)
            qsend[s, m, k - 1] = accum[m, :, lanes(other)].astype(BF16)
            push(
                qsend.at[s, m, k - 1],
                qrecv.at[s, m, k - 1],
                send_sems.at[s, m, 1],
                recv_sems.at[s, m, 1],
                {"tensor": other * 2 + y},
            )

    is_key = y == 0

    def swap(s, m):
        drain(kvrecv.at[s, m], recv_sems.at[s, m, 2])
        arrived = jnp.sum(kvrecv[s, m].astype(F32), axis=0)
        squares = arrived[MB_ROWS : MB_ROWS + 1, 0:MB_ROWS]
        squares = squares + arrived[MB_ROWS + 1 : MB_ROWS + 2, 0:MB_ROWS]
        inverse = to_col(lax.rsqrt((squares_own[m, 0:1, 0:MB_ROWS] + squares) / D + 1e-05))
        keyval = accum[m, :, lanes(Z + lax.div(z, per_kv))] + arrived[0:MB_ROWS]
        keyval = keyval * inverse
        cos_kv = jnp.where(is_key, cos_ref[...], 1.0)
        sin_kv = jnp.where(is_key, sin_ref[...], 0.0)
        keyval = keyval * cos_kv + pltpu.roll(keyval, HD // 2, 1) * sin_kv
        swsend[s, m] = keyval.astype(BF16)
        push(
            swsend.at[s, m],
            swrecv.at[s, m],
            send_sems.at[s, m, 3],
            recv_sems.at[s, m, 3],
            {"tensor": partner},
        )
        inverses[m] = jnp.broadcast_to(inverse, (MB_ROWS, HD))

    def attend(s, m):
        drain(qrecv.at[s, m], recv_sems.at[s, m, 1])
        arrived = jnp.sum(qrecv[s, m].astype(F32), axis=0)
        query = (accum[m, :, lanes(z)] + arrived) * inverses[m]
        query = query * cos_ref[...] + pltpu.roll(query, HD // 2, 1) * sin_ref[...]
        drain(swrecv.at[s, m], recv_sems.at[s, m, 3])
        own, got = swsend[s, m], swrecv[s, m]
        keys = jnp.where(is_key, own, got)
        values = jnp.where(is_key, got, own)
        scores = lax.dot_general(
            query.astype(BF16), keys, (((1,), (1,)), ((), ())), preferred_element_type=F32
        )
        scores = jnp.where(masks[m] > 0.5, scores * scale, -jnp.inf)
        highest = jnp.max(scores, axis=-1, keepdims=True)
        weights = jnp.exp(scores - highest)
        probs = (weights / jnp.sum(weights, axis=-1, keepdims=True)).astype(BF16)
        attended = jnp.dot(probs, values, preferred_element_type=F32)
        att[s, m, :, lanes(y * Z + z)] = attended.astype(BF16)
        for k in range(1, Z):
            push(
                att.at[s, m, :, lanes(y * Z + z)],
                att.at[s, m, :, lanes(y * Z + z)],
                send_sems.at[s, m, 4],
                recv_sems.at[s, m, 4],
                {"tensor": line_peer(k) * 2 + y},
            )

    def parity(index):
        return pl.ds(pl.multiple_of(index * q_cols, q_cols), q_cols)

    def forward(s, m):
        drain(att.at[s, m, :, pl.ds(0, (Z - 1) * HD)], recv_sems.at[s, m, 4])
        push(
            att.at[s, m, :, parity(y)],
            att.at[s, m, :, parity(y)],
            send_sems.at[s, m, 0],
            recv_sems.at[s, m, 0],
            {"tensor": partner},
        )
        projected = jnp.dot(
            att[s, m, :, parity(y)], wo[parity(y), :], preferred_element_type=F32
        )
        partial[m] = xs[s, m, :, own_half].astype(F32) + projected

    def leave(s, m):
        drain(att.at[s, m, :, pl.ds(0, q_cols)], recv_sems.at[s, m, 0])
        projected = jnp.dot(
            att[s, m, :, parity(1 - y)], wo[parity(1 - y), :], preferred_element_type=F32
        )
        xnew[s, m] = (partial[m] + projected).astype(BF16)
        def hop(target):
            push(
                xnew.at[s, m],
                xs.at[s + 1, m, :, own_half],
                send_sems.at[s, m, 5],
                recv_sems.at[s + 1, m, 5],
                {"section": after, "tensor": target},
            )

        hop(t)

        @pl.when(s < STEPS - 1)
        def _():
            hop(partner)

    def each(phase):
        def one(m, carry):
            phase(m)
            return carry

        lax.fori_loop(0, MB_DEV, one, 0)

    def step(s, carry):
        root = lax.rem(me - s + 2 * S, S)

        def mask(m):
            masks[m] = jnp.where(allowed_of(root, m), 1.0, 0.0)

        def project(i, inner):
            high, low = lax.div(i, MB_DEV), lax.rem(i, MB_DEV)
            is_q = jnp.where(s == 0, high, low)
            m = jnp.where(s == 0, low, high)

            @pl.when(is_q == 0)
            def _():
                project_kv(s, m)

            @pl.when(is_q == 1)
            def _():
                project_q(s, m)

            return inner

        lax.fori_loop(0, 2 * MB_DEV, project, 0)
        each(mask)
        each(lambda m: swap(s, m))
        each(lambda m: attend(s, m))
        each(lambda m: forward(s, m))
        each(lambda m: leave(s, m))
        return carry

    drain(gain_own, w_sems.at[1, 1])
    lax.fori_loop(0, STEPS, step, 0)
    for m in range(MB_DEV):
        drain(xs.at[STEPS, m, :, pl.ds(0, width)], recv_sems.at[STEPS, m, 5])
        out[m * MB_ROWS : (m + 1) * MB_ROWS, :] = xs[STEPS, m, :, own_half]

    drain(arecv.at[pl.ds(0, S - 1)], w_sems.at[0, 0])
    drain(gain_own, w_sems.at[0, 1])
    drain(xs.at[0, :, :, pl.ds(0, width)], w_sems.at[0, 2])
    drain(w_all.at[pl.ds(0, width), pl.ds(0, kv_cols)], w_sems.at[0, 3])
    drain(w_all.at[:, pl.ds(0, (Z - 1) * HD)], w_sems.at[0, 4])

    def finish(s, carry):
        for m in range(MB_DEV):
            drain(qsend.at[s, m], send_sems.at[s, m, 1])
            drain(kvsend.at[s, m], send_sems.at[s, m, 2])
            drain(swsend.at[s, m], send_sems.at[s, m, 3])
            drain(att.at[s, m, :, pl.ds(0, q_cols)], send_sems.at[s, m, 0])
            drain(att.at[s, m, :, pl.ds(0, (Z - 1) * HD)], send_sems.at[s, m, 4])
            drain(xnew.at[s, m], send_sems.at[s, m, 5])

            @pl.when(s < STEPS - 1)
            def _():
                drain(xnew.at[s, m], send_sems.at[s, m, 5])

        return carry

    lax.fori_loop(0, STEPS, finish, 0)


def local(S, T, hidden, audio, audio_dest, segment, norm_gain, w_query, w_keyval, w_out):
    width = hidden.shape[1]
    rows = MB_DEV * MB_ROWS
    Z = T // 2
    cols = (Z + KVH) * HD
    cosine, sine = rope_tables()
    vmem = pl.BlockSpec(memory_space=pltpu.VMEM)
    hbm = pl.BlockSpec(memory_space=pl.ANY)
    per = (STEPS, MB_DEV)
    scratch = [
        pltpu.VMEM((2 * width, cols), BF16),
        pltpu.VMEM(w_out.shape[1:], BF16),
        pltpu.VMEM((S, AUD_DEV, width), BF16),
        pltpu.VMEM((MB_DEV * TXT_MB, width), BF16),
        pltpu.VMEM((8, width), F32),
        pltpu.VMEM((8, 2 * width), F32),
        pltpu.VMEM((STEPS + 1, MB_DEV, MB_ROWS, 2 * width), BF16),
        pltpu.VMEM(per + (MB_ROWS, width), BF16),
        pltpu.VMEM((MB_DEV, MB_ROWS, cols), F32),
        pltpu.VMEM(per + (Z - 1, MB_ROWS, HD), BF16),
        pltpu.VMEM(per + (Z - 1, MB_ROWS, HD), BF16),
        pltpu.VMEM(per + (Z - 1, MB_ROWS + SQ_ROWS, HD), BF16),
        pltpu.VMEM(per + (Z - 1, MB_ROWS + SQ_ROWS, HD), BF16),
        pltpu.VMEM(per + (MB_ROWS, HD), BF16),
        pltpu.VMEM(per + (MB_ROWS, HD), BF16),
        pltpu.VMEM(per + (MB_ROWS, T * HD), BF16),
        pltpu.VMEM((MB_DEV, MB_ROWS, 2 * width), BF16),
        pltpu.VMEM((MB_DEV, 8, HD), F32),
        pltpu.VMEM((MB_DEV, MB_ROWS, HD), F32),
        pltpu.VMEM((MB_DEV, MB_ROWS, MB_ROWS), F32),
        pltpu.VMEM((MB_DEV, MB_ROWS, width), F32),
        pltpu.SemaphoreType.DMA((4 + KVH + T,)),
        pltpu.SemaphoreType.DMA((2, 5)),
        pltpu.SemaphoreType.DMA(per + (6,)),
        pltpu.SemaphoreType.DMA((STEPS + 1, MB_DEV, 6)),
    ]
    return pl.pallas_call(
        functools.partial(kernel, S, T),
        out_shape=jax.ShapeDtypeStruct((rows, width), BF16),
        in_specs=[hbm, hbm, vmem, vmem, vmem, hbm, hbm, hbm, vmem, vmem],
        out_specs=vmem,
        scratch_shapes=scratch,
        compiler_params=pltpu.CompilerParams(
            collective_id=0, has_side_effects=True, vmem_limit_bytes=62 * 1024 * 1024
        ),
        cost_estimate=pl.CostEstimate(
            flops=STEPS * rows * width * (2 * cols + T * HD) * 2,
            bytes_accessed=8 * 1024 * 1024,
            transcendentals=0,
        ),
    )(
        hidden,
        audio,
        audio_dest.reshape(1, -1),
        segment,
        norm_gain,
        w_query,
        w_keyval,
        w_out,
        jnp.asarray(cosine),
        jnp.asarray(sine),
    )


def solution(mesh):
    in_specs = (
        P("section", "tensor"),
        P("section", "tensor"),
        P(),
        P(),
        P("section", "tensor"),
        P("section", None, "tensor"),
        P("section", "tensor", None),
        P("section", None, "tensor"),
    )
    out_specs = P("section", "tensor")
    body = functools.partial(local, mesh.shape["section"], mesh.shape["tensor"])
    return jax.shard_map(body, mesh=mesh, in_specs=in_specs, out_specs=out_specs, check_vma=False)
```

```python
import functools
import math

import jax
import jax.numpy as jnp
import numpy as np
from jax import lax
from jax.experimental import pallas as pl
from jax.experimental.pallas import tpu as pltpu
from jax.sharding import PartitionSpec as P

D = 8192
HD = 128
KVH = 4
MB_DEV = 2
AUD_MB = 32
TXT_MB = 32
AUD_DEV = 32
STEPS = 4
MB_ROWS = 64
SQ_ROWS = 16
ROWS = MB_DEV * MB_ROWS
HALVES = 2
MESH = pl.DeviceIdType.MESH
F32 = jnp.float32
BF16 = jnp.bfloat16


def rope_tables():
    position = np.arange(MB_ROWS, dtype=np.float32)
    freq = np.float32(500000.0) ** (-(2.0 * np.arange(HD // 2, dtype=np.float32)) / HD)
    angle = (position[:, None] * freq[None, :].astype(np.float32)).astype(np.float32)
    cosine, sine = np.cos(angle), np.sin(angle)
    return (
        np.tile(cosine, (MB_DEV, 2)).astype(np.float32),
        np.tile(np.concatenate([-sine, sine], 1), (MB_DEV, 1)).astype(np.float32),
    )


def iota(shape, dim):
    return lax.broadcasted_iota(jnp.int32, shape, dim)


def drain(ref, sem):
    pltpu.make_async_copy(ref, ref, sem).wait()


def kernel(
    S,
    T,
    hidden,
    audio,
    dest,
    segment,
    gain,
    wq,
    wkv,
    wo_hbm,
    cos_ref,
    sin_ref,
    out,
    w_all,
    wo,
    arecv,
    hid,
    gain_own,
    gain_pair,
    xs,
    xnew,
    accum,
    qsend,
    qrecv,
    kvsend,
    kvrecv,
    swsend,
    swrecv,
    att,
    xgain,
    squares_own,
    inverses,
    masks,
    local_sem,
    w_sems,
    send_sems,
    recv_sems,
):
    Z = T // 2
    width = gain.shape[1]
    cap = MB_DEV * AUD_MB // S
    shift = cap.bit_length() - 1
    per_kv = Z // KVH
    q_cols = Z * HD
    kv_cols = KVH * HD
    me = lax.axis_index("section")
    t = lax.axis_index("tensor")
    y = lax.rem(t, 2)
    z = lax.div(t, 2)
    partner = t + 1 - 2 * y
    after = lax.rem(me + 1, S)
    before = lax.rem(me + S - 1, S)
    own_half = pl.ds(pl.multiple_of(y * width, width), width)

    def lanes(index):
        return pl.ds(pl.multiple_of(index * HD, HD), HD)

    def pair_rows(index):
        return pl.ds(pl.multiple_of(index * 2 * width, 2 * width), 2 * width)

    def tensor_peer(k):
        return lax.rem(t + k, T)

    def line_peer(k):
        return lax.rem(z + k, Z)

    def push(src, dst, send, recv, device):
        pltpu.make_async_remote_copy(
            src_ref=src,
            dst_ref=dst,
            send_sem=send,
            recv_sem=recv,
            device_id=device,
            device_id_type=MESH,
        ).start()

    stage = [
        pltpu.make_async_copy(audio, arecv.at[me], local_sem.at[0]),
        pltpu.make_async_copy(hidden, hid, local_sem.at[1]),
    ]
    late = [
        pltpu.make_async_copy(wo_hbm.at[0], wo, local_sem.at[2]),
        pltpu.make_async_copy(
            wq.at[0, pair_rows(z), :], w_all.at[:, lanes(z)], local_sem.at[3]
        ),
    ]
    for h in range(KVH):
        late.append(
            pltpu.make_async_copy(
                wkv.at[0, :, lanes(2 * h + y)],
                w_all.at[own_half, pl.ds(q_cols + h * HD, HD)],
                local_sem.at[4 + h],
            )
        )

    barrier = pltpu.get_barrier_semaphore()

    def greet(device):
        pl.semaphore_signal(barrier, inc=1, device_id=device, device_id_type=MESH)

    for k in range(1, T):
        greet({"tensor": tensor_peer(k)})
    for k in range(1, S):
        greet({"section": lax.rem(me + k, S)})
    greet({"section": after, "tensor": partner})
    greet({"section": before, "tensor": partner})
    for copy in stage + late:
        copy.start()
    gain_own[...] = jnp.broadcast_to(gain[...].astype(F32), (8, width))
    gain_pair[:, own_half] = gain_own[...]
    pl.semaphore_wait(barrier, T + S)

    for k in range(1, S):
        push(
            audio,
            arecv.at[me],
            w_sems.at[0, 0],
            w_sems.at[1, 0],
            {"section": lax.rem(me + k, S)},
        )
    push(
        gain_own,
        gain_pair.at[:, own_half],
        w_sems.at[0, 1],
        w_sems.at[1, 1],
        {"tensor": partner},
    )
    for h in range(KVH):
        push(
            wkv.at[0, :, lanes(2 * h + 1 - y)],
            w_all.at[own_half, pl.ds(q_cols + h * HD, HD)],
            w_sems.at[0, 3],
            w_sems.at[1, 3],
            {"tensor": partner},
        )
    for k in range(1, Z):
        other = line_peer(k)
        push(
            wq.at[0, pair_rows(other), :],
            w_all.at[:, lanes(z)],
            w_sems.at[0, 4],
            w_sems.at[1, 4],
            {"tensor": other * 2 + y},
        )

    N = dest.shape[1]
    drow = dest[...].astype(F32)
    sub, lane = iota((N, N), 0), iota((N, N), 1)
    dcol = jnp.sum(jnp.where(sub == lane, drow, 0.0), axis=1, keepdims=True)
    same = (dcol == drow) & ((sub >> 5) == (lane >> 5)) & (sub < lane)
    rank = jnp.sum(jnp.where(same, 1.0, 0.0), axis=0, keepdims=True)
    block = (iota((1, N), 1) >> 5).astype(F32)
    slot = block * float(cap) + rank
    mine = drow == me.astype(F32)

    for copy in stage:
        copy.wait()
    drain(arecv.at[pl.ds(0, S - 1)], w_sems.at[1, 0])
    every_row = arecv[...].reshape(N, width)
    for m in range(MB_DEV):
        wanted = (iota((AUD_MB, N), 0) + m * AUD_MB).astype(F32)
        chosen = jnp.where((slot == wanted) & mine, 1.0, 0.0).astype(BF16)
        rows = jnp.dot(chosen, every_row, preferred_element_type=F32)
        top = m * MB_ROWS
        xs[0, top : top + AUD_MB, own_half] = rows.astype(BF16)
        text = hid[m * TXT_MB : (m + 1) * TXT_MB, :]
        xs[0, top + AUD_MB : top + MB_ROWS, own_half] = text
    push(
        xs.at[0, :, own_half],
        xs.at[0, :, own_half],
        w_sems.at[0, 2],
        recv_sems.at[0, 5],
        {"tensor": partner},
    )
    for copy in late:
        copy.wait()

    eye = iota((MB_ROWS, MB_ROWS), 0) == iota((MB_ROWS, MB_ROWS), 1)
    causal = iota((MB_ROWS, MB_ROWS), 1) <= iota((MB_ROWS, MB_ROWS), 0)
    scale = 1.0 / math.sqrt(HD)

    eye_all = iota((ROWS, ROWS), 0) == iota((ROWS, ROWS), 1)

    def to_col(row, where):
        return jnp.sum(jnp.where(where, row, 0.0), axis=1, keepdims=True)

    def to_row(col, where):
        return jnp.sum(jnp.where(where, col, 0.0), axis=0, keepdims=True)

    def allowed_of(root, m):
        seg_row = segment[pl.ds(root * MB_DEV + m, 1), :].astype(F32)
        seg_col = to_col(seg_row, eye)
        position = iota((MB_ROWS, N), 0)
        owner = ((position + m * AUD_MB) >> shift).astype(F32)
        named = (drow == root.astype(F32)) & (block == owner)
        count = jnp.sum(jnp.where(named, 1.0, 0.0), axis=1, keepdims=True)
        index = iota((MB_ROWS, 1), 0)
        within = (index & (cap - 1)).astype(F32)
        live = jnp.where((within < count) | (index >= AUD_MB), 1.0, 0.0)
        return causal & (seg_col == seg_row) & ((to_row(live, eye) > 0.5) | eye)

    def project_kv(s):
        @pl.when(s == 0)
        def _():
            drain(xs.at[0, :, pl.ds(0, width)], recv_sems.at[0, 5])

        @pl.when(s > 0)
        def _():
            drain(xs.at[s], recv_sems.at[s, 5])

        x = xs[s].astype(F32)
        sums = to_row(jnp.sum(x * x, axis=1, keepdims=True), eye_all)
        high = sums.astype(BF16).astype(F32)
        place = iota((SQ_ROWS, HD), 0)
        squares = jnp.where(place == 0, high, jnp.where(place == 1, sums - high, 0.0)).astype(BF16)
        squares_own[...] = jnp.broadcast_to(sums, (8, HD))
        xgain[...] = (x * gain_pair[0:1, :]).astype(BF16)

        @pl.when(s == 0)
        def _():
            drain(w_all.at[pl.ds(0, width), pl.ds(0, kv_cols)], w_sems.at[1, 3])
        accum[:, q_cols:] = jnp.dot(xgain[...], w_all[:, q_cols:], preferred_element_type=F32)
        for k in range(1, Z):
            other = line_peer(k)
            block_of = lanes(Z + lax.div(other, per_kv))
            kvsend[s, k - 1, 0:ROWS, :] = accum[:, block_of].astype(BF16)
            kvsend[s, k - 1, ROWS:, :] = squares
            push(
                kvsend.at[s, k - 1],
                kvrecv.at[s, k - 1],
                send_sems.at[s, 2],
                recv_sems.at[s, 2],
                {"tensor": other * 2 + y},
            )

    def project_q(s):
        @pl.when(s == 0)
        def _():
            drain(w_all.at[:, pl.ds(0, (Z - 1) * HD)], w_sems.at[1, 4])
        accum[:, :q_cols] = jnp.dot(xgain[...], w_all[:, :q_cols], preferred_element_type=F32)
        for k in range(1, Z):
            other = line_peer(k)
            qsend[s, k - 1] = accum[:, lanes(other)].astype(BF16)
            push(
                qsend.at[s, k - 1],
                qrecv.at[s, k - 1],
                send_sems.at[s, 1],
                recv_sems.at[s, 1],
                {"tensor": other * 2 + y},
            )

    is_key = y == 0

    def swap(s):
        drain(kvrecv.at[s], recv_sems.at[s, 2])
        arrived = jnp.sum(kvrecv[s].astype(F32), axis=0)
        squares = arrived[ROWS : ROWS + 1]
        squares = squares + arrived[ROWS + 1 : ROWS + 2]
        inverse = to_col(lax.rsqrt((squares_own[0:1, :] + squares) / D + 1e-05), eye_all)
        keyval = accum[:, lanes(Z + lax.div(z, per_kv))] + arrived[0:ROWS]
        keyval = keyval * inverse
        cos_kv = jnp.where(is_key, cos_ref[...], 1.0)
        sin_kv = jnp.where(is_key, sin_ref[...], 0.0)
        keyval = keyval * cos_kv + pltpu.roll(keyval, HD // 2, 1) * sin_kv
        swsend[s] = keyval.astype(BF16)
        push(
            swsend.at[s],
            swrecv.at[s],
            send_sems.at[s, 3],
            recv_sems.at[s, 3],
            {"tensor": partner},
        )
        inverses[...] = jnp.broadcast_to(inverse, (ROWS, HD))

    def attend(s):
        drain(qrecv.at[s], recv_sems.at[s, 1])
        arrived = jnp.sum(qrecv[s].astype(F32), axis=0)
        query = (accum[:, lanes(z)] + arrived) * inverses[...]
        query = query * cos_ref[...] + pltpu.roll(query, HD // 2, 1) * sin_ref[...]
        drain(swrecv.at[s], recv_sems.at[s, 3])
        own, got = swsend[s], swrecv[s]
        keys = jnp.where(is_key, own, got)
        values = jnp.where(is_key, got, own)
        query = query.astype(BF16)
        for m in range(MB_DEV):
            part = slice(m * MB_ROWS, (m + 1) * MB_ROWS)
            scores = lax.dot_general(
                query[part], keys[part], (((1,), (1,)), ((), ())), preferred_element_type=F32
            )
            scores = jnp.where(masks[m] > 0.5, scores * scale, -jnp.inf)
            highest = jnp.max(scores, axis=-1, keepdims=True)
            weights = jnp.exp(scores - highest)
            probs = (weights / jnp.sum(weights, axis=-1, keepdims=True)).astype(BF16)
            attended = jnp.dot(probs, values[part], preferred_element_type=F32)
            att[s, part, lanes(t)] = attended.astype(BF16)
        for k in range(1, T):
            push(
                att.at[s, :, lanes(t)],
                att.at[s, :, lanes(t)],
                send_sems.at[s, 4],
                recv_sems.at[s, 4],
                {"tensor": tensor_peer(k)},
            )

    def leave(s):
        drain(att.at[s, :, pl.ds(0, (T - 1) * HD)], recv_sems.at[s, 4])
        size = width // HALVES
        for half in range(HALVES):
            columns = slice(half * size, (half + 1) * size)
            place = pl.ds(pl.multiple_of(y * width + half * size, size), size)
            projected = jnp.dot(att[s], wo[:, columns], preferred_element_type=F32)
            xnew[s, :, columns] = (xs[s, :, place].astype(F32) + projected).astype(BF16)

            def hop(target):
                push(
                    xnew.at[s, :, columns],
                    xs.at[s + 1, :, place],
                    send_sems.at[s, 5],
                    recv_sems.at[s + 1, 5],
                    {"section": after, "tensor": target},
                )

            hop(t)

            @pl.when(s < STEPS - 1)
            def _():
                hop(partner)

    def step(s, carry):
        root = lax.rem(me - s + 2 * S, S)

        for m in range(MB_DEV):
            masks[m] = jnp.where(allowed_of(root, m), 1.0, 0.0)
        project_kv(s)

        @pl.when(s == 0)
        def _():
            swap(s)

        project_q(s)

        @pl.when(s > 0)
        def _():
            swap(s)

        attend(s)
        leave(s)
        return carry

    drain(gain_own, w_sems.at[1, 1])
    lax.fori_loop(0, STEPS, step, 0)
    drain(xs.at[STEPS, :, pl.ds(0, width)], recv_sems.at[STEPS, 5])
    out[...] = xs[STEPS, :, own_half]

    drain(arecv.at[pl.ds(0, S - 1)], w_sems.at[0, 0])
    drain(gain_own, w_sems.at[0, 1])
    drain(xs.at[0, :, pl.ds(0, width)], w_sems.at[0, 2])
    drain(w_all.at[pl.ds(0, width), pl.ds(0, kv_cols)], w_sems.at[0, 3])
    drain(w_all.at[:, pl.ds(0, (Z - 1) * HD)], w_sems.at[0, 4])

    def finish(s, carry):
        drain(qsend.at[s], send_sems.at[s, 1])
        drain(kvsend.at[s], send_sems.at[s, 2])
        drain(swsend.at[s], send_sems.at[s, 3])
        drain(att.at[s, :, pl.ds(0, (T - 1) * HD)], send_sems.at[s, 4])
        drain(xnew.at[s], send_sems.at[s, 5])

        @pl.when(s < STEPS - 1)
        def _():
            drain(xnew.at[s], send_sems.at[s, 5])

        return carry

    lax.fori_loop(0, STEPS, finish, 0)


def local(S, T, hidden, audio, audio_dest, segment, norm_gain, w_query, w_keyval, w_out):
    width = hidden.shape[1]
    rows = MB_DEV * MB_ROWS
    Z = T // 2
    cols = (Z + KVH) * HD
    cosine, sine = rope_tables()
    vmem = pl.BlockSpec(memory_space=pltpu.VMEM)
    hbm = pl.BlockSpec(memory_space=pl.ANY)
    scratch = [
        pltpu.VMEM((2 * width, cols), BF16),
        pltpu.VMEM(w_out.shape[1:], BF16),
        pltpu.VMEM((S, AUD_DEV, width), BF16),
        pltpu.VMEM((MB_DEV * TXT_MB, width), BF16),
        pltpu.VMEM((8, width), F32),
        pltpu.VMEM((8, 2 * width), F32),
        pltpu.VMEM((STEPS + 1, ROWS, 2 * width), BF16),
        pltpu.VMEM((STEPS, ROWS, width), BF16),
        pltpu.VMEM((ROWS, cols), F32),
        pltpu.VMEM((STEPS, Z - 1, ROWS, HD), BF16),
        pltpu.VMEM((STEPS, Z - 1, ROWS, HD), BF16),
        pltpu.VMEM((STEPS, Z - 1, ROWS + SQ_ROWS, HD), BF16),
        pltpu.VMEM((STEPS, Z - 1, ROWS + SQ_ROWS, HD), BF16),
        pltpu.VMEM((STEPS, ROWS, HD), BF16),
        pltpu.VMEM((STEPS, ROWS, HD), BF16),
        pltpu.VMEM((STEPS, ROWS, T * HD), BF16),
        pltpu.VMEM((ROWS, 2 * width), BF16),
        pltpu.VMEM((8, HD), F32),
        pltpu.VMEM((ROWS, HD), F32),
        pltpu.VMEM((MB_DEV, MB_ROWS, MB_ROWS), F32),
        pltpu.SemaphoreType.DMA((4 + KVH,)),
        pltpu.SemaphoreType.DMA((2, 5)),
        pltpu.SemaphoreType.DMA((STEPS, 6)),
        pltpu.SemaphoreType.DMA((STEPS + 1, 6)),
    ]
    return pl.pallas_call(
        functools.partial(kernel, S, T),
        out_shape=jax.ShapeDtypeStruct((rows, width), BF16),
        in_specs=[hbm, hbm, vmem, vmem, vmem, hbm, hbm, hbm, vmem, vmem],
        out_specs=vmem,
        scratch_shapes=scratch,
        compiler_params=pltpu.CompilerParams(
            collective_id=0, has_side_effects=True, vmem_limit_bytes=62 * 1024 * 1024
        ),
        cost_estimate=pl.CostEstimate(
            flops=STEPS * rows * width * (2 * cols + T * HD) * 2,
            bytes_accessed=8 * 1024 * 1024,
            transcendentals=0,
        ),
    )(
        hidden,
        audio,
        audio_dest.reshape(1, -1),
        segment,
        norm_gain,
        w_query,
        w_keyval,
        w_out,
        jnp.asarray(cosine),
        jnp.asarray(sine),
    )


def solution(mesh):
    in_specs = (
        P("section", "tensor"),
        P("section", "tensor"),
        P(),
        P(),
        P("section", "tensor"),
        P("section", None, "tensor"),
        P("section", "tensor", None),
        P("section", None, "tensor"),
    )
    out_specs = P("section", "tensor")
    body = functools.partial(local, mesh.shape["section"], mesh.shape["tensor"])
    return jax.shard_map(body, mesh=mesh, in_specs=in_specs, out_specs=out_specs, check_vma=False)
```

```python
import functools
import math

import jax
import jax.numpy as jnp
import numpy as np
from jax import lax
from jax.experimental import pallas as pl
from jax.experimental.pallas import tpu as pltpu
from jax.sharding import PartitionSpec as P

D = 8192
HD = 128
KVH = 4
MB_DEV = 2
AUD_MB = 32
TXT_MB = 32
AUD_DEV = 32
STEPS = 4
MB_ROWS = 64
HALVES = 2
MESH = pl.DeviceIdType.MESH
F32 = jnp.float32
BF16 = jnp.bfloat16


def rope_tables():
    position = np.arange(MB_ROWS, dtype=np.float32)
    freq = np.float32(500000.0) ** (-(2.0 * np.arange(HD // 2, dtype=np.float32)) / HD)
    angle = (position[:, None] * freq[None, :].astype(np.float32)).astype(np.float32)
    cosine, sine = np.cos(angle), np.sin(angle)
    return (
        np.concatenate([cosine, cosine], 1).astype(np.float32),
        np.concatenate([-sine, sine], 1).astype(np.float32),
    )


def iota(shape, dim):
    return lax.broadcasted_iota(jnp.int32, shape, dim)


def drain(ref, sem):
    pltpu.make_async_copy(ref, ref, sem).wait()


def kernel(
    S,
    T,
    hidden,
    audio,
    dest,
    segment,
    gain,
    wq,
    wkv,
    wo_hbm,
    cos_ref,
    sin_ref,
    out,
    w_all,
    wo,
    arecv,
    hid,
    gain_own,
    gain_pair,
    xs,
    xnew,
    accum,
    qsend,
    qrecv,
    kvsend,
    kvrecv,
    sssend,
    ssrecv,
    swsend,
    swrecv,
    att,
    local_sem,
    w_sems,
    send_sems,
    recv_sems,
):
    Z = T // 2
    width = gain.shape[1]
    cap = MB_DEV * AUD_MB // S
    shift = cap.bit_length() - 1
    per_kv = Z // KVH
    q_cols = Z * HD
    kv_cols = KVH * HD
    me = lax.axis_index("section")
    t = lax.axis_index("tensor")
    y = lax.rem(t, 2)
    z = lax.div(t, 2)
    partner = t + 1 - 2 * y
    after = lax.rem(me + 1, S)
    before = lax.rem(me + S - 1, S)
    own_half = pl.ds(pl.multiple_of(y * width, width), width)

    def lanes(index):
        return pl.ds(pl.multiple_of(index * HD, HD), HD)

    def pair_rows(index):
        return pl.ds(pl.multiple_of(index * 2 * width, 2 * width), 2 * width)

    def tensor_peer(k):
        return lax.rem(t + k, T)

    def line_peer(k):
        return lax.rem(z + k, Z)

    def push(src, dst, send, recv, device):
        pltpu.make_async_remote_copy(
            src_ref=src,
            dst_ref=dst,
            send_sem=send,
            recv_sem=recv,
            device_id=device,
            device_id_type=MESH,
        ).start()

    stage = [
        pltpu.make_async_copy(audio, arecv.at[me], local_sem.at[0]),
        pltpu.make_async_copy(hidden, hid, local_sem.at[1]),
    ]
    late = [
        pltpu.make_async_copy(wo_hbm.at[0], wo, local_sem.at[2]),
        pltpu.make_async_copy(
            wq.at[0, pair_rows(z), :], w_all.at[:, lanes(z)], local_sem.at[3]
        ),
    ]
    for h in range(KVH):
        late.append(
            pltpu.make_async_copy(
                wkv.at[0, :, lanes(2 * h + y)],
                w_all.at[own_half, pl.ds(q_cols + h * HD, HD)],
                local_sem.at[4 + h],
            )
        )

    barrier = pltpu.get_barrier_semaphore()

    def greet(device):
        pl.semaphore_signal(barrier, inc=1, device_id=device, device_id_type=MESH)

    for k in range(1, T):
        greet({"tensor": tensor_peer(k)})
    for k in range(1, S):
        greet({"section": lax.rem(me + k, S)})
    greet({"section": after, "tensor": partner})
    greet({"section": before, "tensor": partner})
    for copy in stage + late:
        copy.start()
    gain_own[...] = jnp.broadcast_to(gain[...].astype(F32), (8, width))
    gain_pair[:, own_half] = gain_own[...]
    pl.semaphore_wait(barrier, T + S)

    for k in range(1, S):
        push(
            audio,
            arecv.at[me],
            w_sems.at[0, 0],
            w_sems.at[1, 0],
            {"section": lax.rem(me + k, S)},
        )
    push(
        gain_own,
        gain_pair.at[:, own_half],
        w_sems.at[0, 1],
        w_sems.at[1, 1],
        {"tensor": partner},
    )
    for h in range(KVH):
        push(
            wkv.at[0, :, lanes(2 * h + 1 - y)],
            w_all.at[own_half, pl.ds(q_cols + h * HD, HD)],
            w_sems.at[0, 3],
            w_sems.at[1, 3],
            {"tensor": partner},
        )
    for k in range(1, Z):
        other = line_peer(k)
        push(
            wq.at[0, pair_rows(other), :],
            w_all.at[:, lanes(z)],
            w_sems.at[0, 4],
            w_sems.at[1, 4],
            {"tensor": other * 2 + y},
        )

    N = dest.shape[1]
    drow = dest[...].astype(F32)
    sub, lane = iota((N, N), 0), iota((N, N), 1)
    dcol = jnp.sum(jnp.where(sub == lane, drow, 0.0), axis=1, keepdims=True)
    same = (dcol == drow) & ((sub >> 5) == (lane >> 5)) & (sub < lane)
    rank = jnp.sum(jnp.where(same, 1.0, 0.0), axis=0, keepdims=True)
    block = (iota((1, N), 1) >> 5).astype(F32)
    slot = block * float(cap) + rank
    mine = drow == me.astype(F32)

    for copy in stage:
        copy.wait()
    drain(arecv.at[pl.ds(0, S - 1)], w_sems.at[1, 0])
    every_row = arecv[...].reshape(N, width)
    for m in range(MB_DEV):
        wanted = (iota((AUD_MB, N), 0) + m * AUD_MB).astype(F32)
        chosen = jnp.where((slot == wanted) & mine, 1.0, 0.0).astype(BF16)
        rows = jnp.dot(chosen, every_row, preferred_element_type=F32)
        xs[0, m, 0:AUD_MB, own_half] = rows.astype(BF16)
        xs[0, m, AUD_MB:MB_ROWS, own_half] = hid[m * TXT_MB : (m + 1) * TXT_MB, :]
        push(
            xs.at[0, m, :, own_half],
            xs.at[0, m, :, own_half],
            w_sems.at[0, 2],
            recv_sems.at[0, m, 5],
            {"tensor": partner},
        )
    for copy in late:
        copy.wait()

    eye = iota((MB_ROWS, MB_ROWS), 0) == iota((MB_ROWS, MB_ROWS), 1)
    causal = iota((MB_ROWS, MB_ROWS), 1) <= iota((MB_ROWS, MB_ROWS), 0)
    scale = 1.0 / math.sqrt(HD)

    def to_col(row):
        return jnp.sum(jnp.where(eye, row, 0.0), axis=1, keepdims=True)

    def to_row(col):
        return jnp.sum(jnp.where(eye, col, 0.0), axis=0, keepdims=True)

    def allowed_of(root, m):
        seg_row = segment[pl.ds(root * MB_DEV + m, 1), :].astype(F32)
        seg_col = to_col(seg_row)
        position = iota((MB_ROWS, N), 0)
        owner = ((position + m * AUD_MB) >> shift).astype(F32)
        named = (drow == root.astype(F32)) & (block == owner)
        count = jnp.sum(jnp.where(named, 1.0, 0.0), axis=1, keepdims=True)
        index = iota((MB_ROWS, 1), 0)
        within = (index & (cap - 1)).astype(F32)
        live = jnp.where((within < count) | (index >= AUD_MB), 1.0, 0.0)
        return causal & (seg_col == seg_row) & ((to_row(live) > 0.5) | eye)

    def project_kv(s, m, first):
        if first:
            drain(xs.at[0, m, :, pl.ds(0, width)], recv_sems.at[0, m, 5])
        else:
            drain(xs.at[s, m], recv_sems.at[s, m, 5])
        x = xs[s, m].astype(F32)
        sums = to_row(jnp.sum(x * x, axis=1, keepdims=True))
        sums = jnp.broadcast_to(sums, (8, MB_ROWS))
        sssend[s, m] = jnp.concatenate([sums, sums], axis=1)
        for k in range(1, Z):
            push(
                sssend.at[s, m],
                ssrecv.at[s, m, k - 1],
                send_sems.at[s, m, 0],
                recv_sems.at[s, m, 0],
                {"tensor": line_peer(k) * 2 + y},
            )
        xg = (x * gain_pair[0:1, :]).astype(BF16)
        if first and m == 0:
            drain(w_all.at[pl.ds(0, width), pl.ds(0, kv_cols)], w_sems.at[1, 3])
        accum[m, :, q_cols:] = jnp.dot(xg, w_all[:, q_cols:], preferred_element_type=F32)
        for k in range(1, Z):
            other = line_peer(k)
            block_of = lanes(Z + lax.div(other, per_kv))
            kvsend[s, m, k - 1] = accum[m, :, block_of].astype(BF16)
            push(
                kvsend.at[s, m, k - 1],
                kvrecv.at[s, m, k - 1],
                send_sems.at[s, m, 2],
                recv_sems.at[s, m, 2],
                {"tensor": other * 2 + y},
            )
        return xg

    def project_q(s, m, first, xg):
        if first and m == 0:
            drain(w_all.at[:, pl.ds(0, (Z - 1) * HD)], w_sems.at[1, 4])
        accum[m, :, :q_cols] = jnp.dot(xg, w_all[:, :q_cols], preferred_element_type=F32)
        for k in range(1, Z):
            other = line_peer(k)
            qsend[s, m, k - 1] = accum[m, :, lanes(other)].astype(BF16)
            push(
                qsend.at[s, m, k - 1],
                qrecv.at[s, m, k - 1],
                send_sems.at[s, m, 1],
                recv_sems.at[s, m, 1],
                {"tensor": other * 2 + y},
            )

    is_key = y == 0

    def swap(s, m):
        drain(ssrecv.at[s, m], recv_sems.at[s, m, 0])
        total = sssend[s, m] + jnp.sum(ssrecv[s, m], axis=0)
        inverse = to_col(lax.rsqrt(total[0:1, 0:MB_ROWS] / D + 1e-05))
        drain(kvrecv.at[s, m], recv_sems.at[s, m, 2])
        arrived = jnp.sum(kvrecv[s, m].astype(F32), axis=0)
        keyval = (accum[m, :, lanes(Z + lax.div(z, per_kv))] + arrived) * inverse
        cos_kv = jnp.where(is_key, cos_ref[...], 1.0)
        sin_kv = jnp.where(is_key, sin_ref[...], 0.0)
        keyval = keyval * cos_kv + pltpu.roll(keyval, HD // 2, 1) * sin_kv
        swsend[s, m] = keyval.astype(BF16)
        push(
            swsend.at[s, m],
            swrecv.at[s, m],
            send_sems.at[s, m, 3],
            recv_sems.at[s, m, 3],
            {"tensor": partner},
        )
        return inverse

    def attend(s, m, inverse, mask):
        drain(qrecv.at[s, m], recv_sems.at[s, m, 1])
        arrived = jnp.sum(qrecv[s, m].astype(F32), axis=0)
        query = (accum[m, :, lanes(z)] + arrived) * inverse
        query = query * cos_ref[...] + pltpu.roll(query, HD // 2, 1) * sin_ref[...]
        drain(swrecv.at[s, m], recv_sems.at[s, m, 3])
        own, got = swsend[s, m], swrecv[s, m]
        keys = jnp.where(is_key, own, got)
        values = jnp.where(is_key, got, own)
        scores = lax.dot_general(
            query.astype(BF16), keys, (((1,), (1,)), ((), ())), preferred_element_type=F32
        )
        scores = jnp.where(mask, scores * scale, -jnp.inf)
        highest = jnp.max(scores, axis=-1, keepdims=True)
        weights = jnp.exp(scores - highest)
        probs = (weights / jnp.sum(weights, axis=-1, keepdims=True)).astype(BF16)
        attended = jnp.dot(probs, values, preferred_element_type=F32)
        att[s, m, :, lanes(t)] = attended.astype(BF16)
        for k in range(1, T):
            push(
                att.at[s, m, :, lanes(t)],
                att.at[s, m, :, lanes(t)],
                send_sems.at[s, m, 4],
                recv_sems.at[s, m, 4],
                {"tensor": tensor_peer(k)},
            )

    def leave(s, m, last):
        drain(att.at[s, m, :, pl.ds(0, (T - 1) * HD)], recv_sems.at[s, m, 4])
        size = width // HALVES
        routes = [{"section": after}]
        if not last:
            routes.insert(0, {"section": after, "tensor": partner})
        for half in range(HALVES):
            columns = slice(half * size, (half + 1) * size)
            place = pl.ds(pl.multiple_of(y * width + half * size, size), size)
            projected = jnp.dot(att[s, m], wo[:, columns], preferred_element_type=F32)
            xnew[s, m, :, columns] = (xs[s, m, :, place].astype(F32) + projected).astype(BF16)
            for route in routes:
                push(
                    xnew.at[s, m, :, columns],
                    xs.at[s + 1, m, :, place],
                    send_sems.at[s, m, 5],
                    recv_sems.at[s + 1, m, 5],
                    route,
                )

    def step(s, first, last):
        root = lax.rem(me - s + 2 * S, S)
        each = range(MB_DEV)
        masks = [allowed_of(root, m) for m in each]
        if first:
            gained = [project_kv(s, m, first) for m in each]
            inverses = [swap(s, m) for m in each]
            for m in each:
                project_q(s, m, first, gained[m])
        else:
            for m in each:
                project_q(s, m, first, project_kv(s, m, first))
            inverses = [swap(s, m) for m in each]
        for m in range(MB_DEV):
            attend(s, m, inverses[m], masks[m])
        for m in range(MB_DEV):
            leave(s, m, last)

    def middle(s, carry):
        step(s, False, False)
        return carry

    drain(gain_own, w_sems.at[1, 1])
    step(0, True, False)
    lax.fori_loop(1, STEPS - 1, middle, 0)
    step(STEPS - 1, False, True)

    for m in range(MB_DEV):
        drain(xs.at[STEPS, m, :, pl.ds(0, width)], recv_sems.at[STEPS, m, 5])
        out[m * MB_ROWS : (m + 1) * MB_ROWS, :] = xs[STEPS, m, :, own_half]

    drain(arecv.at[pl.ds(0, S - 1)], w_sems.at[0, 0])
    drain(gain_own, w_sems.at[0, 1])
    drain(xs.at[0, :, :, pl.ds(0, width)], w_sems.at[0, 2])
    drain(w_all.at[pl.ds(0, width), pl.ds(0, kv_cols)], w_sems.at[0, 3])
    drain(w_all.at[:, pl.ds(0, (Z - 1) * HD)], w_sems.at[0, 4])

    def finish(s, carry):
        for m in range(MB_DEV):
            drain(ssrecv.at[s, m], send_sems.at[s, m, 0])
            drain(qsend.at[s, m], send_sems.at[s, m, 1])
            drain(kvsend.at[s, m], send_sems.at[s, m, 2])
            drain(swsend.at[s, m], send_sems.at[s, m, 3])
            drain(att.at[s, m, :, pl.ds(0, (T - 1) * HD)], send_sems.at[s, m, 4])
            drain(xnew.at[s, m], send_sems.at[s, m, 5])

            @pl.when(s < STEPS - 1)
            def _():
                drain(xnew.at[s, m], send_sems.at[s, m, 5])

        return carry

    lax.fori_loop(0, STEPS, finish, 0)


def local(S, T, hidden, audio, audio_dest, segment, norm_gain, w_query, w_keyval, w_out):
    width = hidden.shape[1]
    rows = MB_DEV * MB_ROWS
    Z = T // 2
    cols = (Z + KVH) * HD
    cosine, sine = rope_tables()
    vmem = pl.BlockSpec(memory_space=pltpu.VMEM)
    hbm = pl.BlockSpec(memory_space=pl.ANY)
    per = (STEPS, MB_DEV)
    scratch = [
        pltpu.VMEM((2 * width, cols), BF16),
        pltpu.VMEM(w_out.shape[1:], BF16),
        pltpu.VMEM((S, AUD_DEV, width), BF16),
        pltpu.VMEM((MB_DEV * TXT_MB, width), BF16),
        pltpu.VMEM((8, width), F32),
        pltpu.VMEM((8, 2 * width), F32),
        pltpu.VMEM((STEPS + 1, MB_DEV, MB_ROWS, 2 * width), BF16),
        pltpu.VMEM(per + (MB_ROWS, width), BF16),
        pltpu.VMEM((MB_DEV, MB_ROWS, cols), F32),
        pltpu.VMEM(per + (Z - 1, MB_ROWS, HD), BF16),
        pltpu.VMEM(per + (Z - 1, MB_ROWS, HD), BF16),
        pltpu.VMEM(per + (Z - 1, MB_ROWS, HD), BF16),
        pltpu.VMEM(per + (Z - 1, MB_ROWS, HD), BF16),
        pltpu.VMEM(per + (8, 2 * MB_ROWS), F32),
        pltpu.VMEM(per + (Z - 1, 8, 2 * MB_ROWS), F32),
        pltpu.VMEM(per + (MB_ROWS, HD), BF16),
        pltpu.VMEM(per + (MB_ROWS, HD), BF16),
        pltpu.VMEM(per + (MB_ROWS, T * HD), BF16),
        pltpu.SemaphoreType.DMA((4 + KVH,)),
        pltpu.SemaphoreType.DMA((2, 5)),
        pltpu.SemaphoreType.DMA(per + (6,)),
        pltpu.SemaphoreType.DMA((STEPS + 1, MB_DEV, 6)),
    ]
    return pl.pallas_call(
        functools.partial(kernel, S, T),
        out_shape=jax.ShapeDtypeStruct((rows, width), BF16),
        in_specs=[hbm, hbm, vmem, vmem, vmem, hbm, hbm, hbm, vmem, vmem],
        out_specs=vmem,
        scratch_shapes=scratch,
        compiler_params=pltpu.CompilerParams(
            collective_id=0, has_side_effects=True, vmem_limit_bytes=62 * 1024 * 1024
        ),
        cost_estimate=pl.CostEstimate(
            flops=STEPS * rows * width * (2 * cols + T * HD) * 2,
            bytes_accessed=8 * 1024 * 1024,
            transcendentals=0,
        ),
    )(
        hidden,
        audio,
        audio_dest.reshape(1, -1),
        segment,
        norm_gain,
        w_query,
        w_keyval,
        w_out,
        jnp.asarray(cosine),
        jnp.asarray(sine),
    )


def solution(mesh):
    in_specs = (
        P("section", "tensor"),
        P("section", "tensor"),
        P(),
        P(),
        P("section", "tensor"),
        P("section", None, "tensor"),
        P("section", "tensor", None),
        P("section", None, "tensor"),
    )
    out_specs = P("section", "tensor")
    body = functools.partial(local, mesh.shape["section"], mesh.shape["tensor"])
    return jax.shard_map(body, mesh=mesh, in_specs=in_specs, out_specs=out_specs, check_vma=False)
```

```python
import functools
import math

import jax
import jax.numpy as jnp
import numpy as np
from jax import lax
from jax.experimental import pallas as pl
from jax.experimental.pallas import tpu as pltpu
from jax.sharding import PartitionSpec as P

D = 8192
HD = 128
KVH = 4
MB_DEV = 2
AUD_MB = 32
TXT_MB = 32
AUD_DEV = 32
STEPS = 4
MB_ROWS = 64
HALVES = 2
MESH = pl.DeviceIdType.MESH
F32 = jnp.float32
BF16 = jnp.bfloat16


def rope_tables():
    position = np.arange(MB_ROWS, dtype=np.float32)
    freq = np.float32(500000.0) ** (-(2.0 * np.arange(HD // 2, dtype=np.float32)) / HD)
    angle = (position[:, None] * freq[None, :].astype(np.float32)).astype(np.float32)
    cosine, sine = np.cos(angle), np.sin(angle)
    return (
        np.concatenate([cosine, cosine], 1).astype(np.float32),
        np.concatenate([-sine, sine], 1).astype(np.float32),
    )


def iota(shape, dim):
    return lax.broadcasted_iota(jnp.int32, shape, dim)


def drain(ref, sem):
    pltpu.make_async_copy(ref, ref, sem).wait()


def kernel(
    S,
    T,
    hidden,
    audio,
    dest,
    segment,
    gain,
    wq,
    wkv,
    wo_hbm,
    cos_ref,
    sin_ref,
    out,
    w_all,
    wo,
    arecv,
    hid,
    gain_own,
    gain_pair,
    xs,
    xnew,
    accum,
    qsend,
    qrecv,
    kvsend,
    kvrecv,
    sssend,
    ssrecv,
    swsend,
    swrecv,
    att,
    local_sem,
    w_sems,
    send_sems,
    recv_sems,
):
    Z = T // 2
    width = gain.shape[1]
    cap = MB_DEV * AUD_MB // S
    shift = cap.bit_length() - 1
    per_kv = Z // KVH
    q_cols = Z * HD
    kv_cols = KVH * HD
    me = lax.axis_index("section")
    t = lax.axis_index("tensor")
    y = lax.rem(t, 2)
    z = lax.div(t, 2)
    partner = t + 1 - 2 * y
    after = lax.rem(me + 1, S)
    before = lax.rem(me + S - 1, S)
    own_half = pl.ds(pl.multiple_of(y * width, width), width)

    def lanes(index):
        return pl.ds(pl.multiple_of(index * HD, HD), HD)

    def pair_rows(index):
        return pl.ds(pl.multiple_of(index * 2 * width, 2 * width), 2 * width)

    def tensor_peer(k):
        return lax.rem(t + k, T)

    def line_peer(k):
        return lax.rem(z + k, Z)

    def push(src, dst, send, recv, device):
        pltpu.make_async_remote_copy(
            src_ref=src,
            dst_ref=dst,
            send_sem=send,
            recv_sem=recv,
            device_id=device,
            device_id_type=MESH,
        ).start()

    stage = [
        pltpu.make_async_copy(audio, arecv.at[me], local_sem.at[0]),
        pltpu.make_async_copy(hidden, hid, local_sem.at[1]),
    ]
    late = [
        pltpu.make_async_copy(wo_hbm.at[0], wo, local_sem.at[2]),
        pltpu.make_async_copy(
            wq.at[0, pair_rows(z), :], w_all.at[:, lanes(z)], local_sem.at[3]
        ),
    ]
    for h in range(KVH):
        late.append(
            pltpu.make_async_copy(
                wkv.at[0, :, lanes(2 * h + y)],
                w_all.at[own_half, pl.ds(q_cols + h * HD, HD)],
                local_sem.at[4 + h],
            )
        )

    barrier = pltpu.get_barrier_semaphore()

    def greet(device):
        pl.semaphore_signal(barrier, inc=1, device_id=device, device_id_type=MESH)

    for k in range(1, T):
        greet({"tensor": tensor_peer(k)})
    for k in range(1, S):
        greet({"section": lax.rem(me + k, S)})
    greet({"section": after, "tensor": partner})
    greet({"section": before, "tensor": partner})
    for copy in stage + late:
        copy.start()
    gain_own[...] = jnp.broadcast_to(gain[...].astype(F32), (8, width))
    gain_pair[:, own_half] = gain_own[...]
    pl.semaphore_wait(barrier, T + S)

    for k in range(1, S):
        push(
            audio,
            arecv.at[me],
            w_sems.at[0, 0],
            w_sems.at[1, 0],
            {"section": lax.rem(me + k, S)},
        )
    push(
        gain_own,
        gain_pair.at[:, own_half],
        w_sems.at[0, 1],
        w_sems.at[1, 1],
        {"tensor": partner},
    )
    for h in range(KVH):
        push(
            wkv.at[0, :, lanes(2 * h + 1 - y)],
            w_all.at[own_half, pl.ds(q_cols + h * HD, HD)],
            w_sems.at[0, 3],
            w_sems.at[1, 3],
            {"tensor": partner},
        )
    for k in range(1, Z):
        other = line_peer(k)
        push(
            wq.at[0, pair_rows(other), :],
            w_all.at[:, lanes(z)],
            w_sems.at[0, 4],
            w_sems.at[1, 4],
            {"tensor": other * 2 + y},
        )

    N = dest.shape[1]
    drow = dest[...].astype(F32)
    sub, lane = iota((N, N), 0), iota((N, N), 1)
    dcol = jnp.sum(jnp.where(sub == lane, drow, 0.0), axis=1, keepdims=True)
    same = (dcol == drow) & ((sub >> 5) == (lane >> 5)) & (sub < lane)
    rank = jnp.sum(jnp.where(same, 1.0, 0.0), axis=0, keepdims=True)
    block = (iota((1, N), 1) >> 5).astype(F32)
    slot = block * float(cap) + rank
    mine = drow == me.astype(F32)

    for copy in stage:
        copy.wait()
    drain(arecv.at[pl.ds(0, S - 1)], w_sems.at[1, 0])
    every_row = arecv[...].reshape(N, width)
    for m in range(MB_DEV):
        wanted = (iota((AUD_MB, N), 0) + m * AUD_MB).astype(F32)
        chosen = jnp.where((slot == wanted) & mine, 1.0, 0.0).astype(BF16)
        rows = jnp.dot(chosen, every_row, preferred_element_type=F32)
        xs[0, m, 0:AUD_MB, own_half] = rows.astype(BF16)
        xs[0, m, AUD_MB:MB_ROWS, own_half] = hid[m * TXT_MB : (m + 1) * TXT_MB, :]
        push(
            xs.at[0, m, :, own_half],
            xs.at[0, m, :, own_half],
            w_sems.at[0, 2],
            recv_sems.at[0, m, 5],
            {"tensor": partner},
        )
    for copy in late:
        copy.wait()

    eye = iota((MB_ROWS, MB_ROWS), 0) == iota((MB_ROWS, MB_ROWS), 1)
    causal = iota((MB_ROWS, MB_ROWS), 1) <= iota((MB_ROWS, MB_ROWS), 0)
    scale = 1.0 / math.sqrt(HD)

    def to_col(row):
        return jnp.sum(jnp.where(eye, row, 0.0), axis=1, keepdims=True)

    def to_row(col):
        return jnp.sum(jnp.where(eye, col, 0.0), axis=0, keepdims=True)

    def allowed_of(root, m):
        seg_row = segment[pl.ds(root * MB_DEV + m, 1), :].astype(F32)
        seg_col = to_col(seg_row)
        position = iota((MB_ROWS, N), 0)
        owner = ((position + m * AUD_MB) >> shift).astype(F32)
        named = (drow == root.astype(F32)) & (block == owner)
        count = jnp.sum(jnp.where(named, 1.0, 0.0), axis=1, keepdims=True)
        index = iota((MB_ROWS, 1), 0)
        within = (index & (cap - 1)).astype(F32)
        live = jnp.where((within < count) | (index >= AUD_MB), 1.0, 0.0)
        return causal & (seg_col == seg_row) & ((to_row(live) > 0.5) | eye)

    def project_kv(s, m, first):
        if first:
            drain(xs.at[0, m, :, pl.ds(0, width)], recv_sems.at[0, m, 5])
        else:
            drain(xs.at[s, m], recv_sems.at[s, m, 5])
        x = xs[s, m].astype(F32)
        sums = to_row(jnp.sum(x * x, axis=1, keepdims=True))
        sums = jnp.broadcast_to(sums, (8, MB_ROWS))
        sssend[s, m] = jnp.concatenate([sums, sums], axis=1)
        for k in range(1, Z):
            push(
                sssend.at[s, m],
                ssrecv.at[s, m, k - 1],
                send_sems.at[s, m, 0],
                recv_sems.at[s, m, 0],
                {"tensor": line_peer(k) * 2 + y},
            )
        xg = (x * gain_pair[0:1, :]).astype(BF16)
        if first and m == 0:
            drain(w_all.at[pl.ds(0, width), pl.ds(0, kv_cols)], w_sems.at[1, 3])
        accum[m, :, q_cols:] = jnp.dot(xg, w_all[:, q_cols:], preferred_element_type=F32)
        for k in range(1, Z):
            other = line_peer(k)
            block_of = lanes(Z + lax.div(other, per_kv))
            kvsend[s, m, k - 1] = accum[m, :, block_of].astype(BF16)
            push(
                kvsend.at[s, m, k - 1],
                kvrecv.at[s, m, k - 1],
                send_sems.at[s, m, 2],
                recv_sems.at[s, m, 2],
                {"tensor": other * 2 + y},
            )
        return xg

    def project_q(s, m, first, xg):
        if first and m == 0:
            drain(w_all.at[:, pl.ds(0, (Z - 1) * HD)], w_sems.at[1, 4])
        accum[m, :, :q_cols] = jnp.dot(xg, w_all[:, :q_cols], preferred_element_type=F32)
        for k in range(1, Z):
            other = line_peer(k)
            qsend[s, m, k - 1] = accum[m, :, lanes(other)].astype(BF16)
            push(
                qsend.at[s, m, k - 1],
                qrecv.at[s, m, k - 1],
                send_sems.at[s, m, 1],
                recv_sems.at[s, m, 1],
                {"tensor": other * 2 + y},
            )

    is_key = y == 0

    def swap(s, m):
        drain(ssrecv.at[s, m], recv_sems.at[s, m, 0])
        total = sssend[s, m] + jnp.sum(ssrecv[s, m], axis=0)
        inverse = to_col(lax.rsqrt(total[0:1, 0:MB_ROWS] / D + 1e-05))
        drain(kvrecv.at[s, m], recv_sems.at[s, m, 2])
        arrived = jnp.sum(kvrecv[s, m].astype(F32), axis=0)
        keyval = (accum[m, :, lanes(Z + lax.div(z, per_kv))] + arrived) * inverse
        cos_kv = jnp.where(is_key, cos_ref[...], 1.0)
        sin_kv = jnp.where(is_key, sin_ref[...], 0.0)
        keyval = keyval * cos_kv + pltpu.roll(keyval, HD // 2, 1) * sin_kv
        swsend[s, m] = keyval.astype(BF16)
        push(
            swsend.at[s, m],
            swrecv.at[s, m],
            send_sems.at[s, m, 3],
            recv_sems.at[s, m, 3],
            {"tensor": partner},
        )
        return inverse

    def attend(s, m, inverse, mask):
        drain(qrecv.at[s, m], recv_sems.at[s, m, 1])
        arrived = jnp.sum(qrecv[s, m].astype(F32), axis=0)
        query = (accum[m, :, lanes(z)] + arrived) * inverse
        query = query * cos_ref[...] + pltpu.roll(query, HD // 2, 1) * sin_ref[...]
        drain(swrecv.at[s, m], recv_sems.at[s, m, 3])
        own, got = swsend[s, m], swrecv[s, m]
        keys = jnp.where(is_key, own, got)
        values = jnp.where(is_key, got, own)
        scores = lax.dot_general(
            query.astype(BF16), keys, (((1,), (1,)), ((), ())), preferred_element_type=F32
        )
        scores = jnp.where(mask, scores * scale, -jnp.inf)
        highest = jnp.max(scores, axis=-1, keepdims=True)
        weights = jnp.exp(scores - highest)
        probs = (weights / jnp.sum(weights, axis=-1, keepdims=True)).astype(BF16)
        attended = jnp.dot(probs, values, preferred_element_type=F32)
        att[s, m, :, lanes(t)] = attended.astype(BF16)
        for k in range(1, T):
            push(
                att.at[s, m, :, lanes(t)],
                att.at[s, m, :, lanes(t)],
                send_sems.at[s, m, 4],
                recv_sems.at[s, m, 4],
                {"tensor": tensor_peer(k)},
            )

    def leave(s, m, last):
        drain(att.at[s, m, :, pl.ds(0, (T - 1) * HD)], recv_sems.at[s, m, 4])
        size = width // HALVES
        routes = [{"section": after}]
        if not last:
            routes.insert(0, {"section": after, "tensor": partner})
        for half in range(HALVES):
            columns = slice(half * size, (half + 1) * size)
            place = pl.ds(pl.multiple_of(y * width + half * size, size), size)
            projected = jnp.dot(att[s, m], wo[:, columns], preferred_element_type=F32)
            xnew[s, m, :, columns] = (xs[s, m, :, place].astype(F32) + projected).astype(BF16)
            for route in routes:
                push(
                    xnew.at[s, m, :, columns],
                    xs.at[s + 1, m, :, place],
                    send_sems.at[s, m, 5],
                    recv_sems.at[s + 1, m, 5],
                    route,
                )

    def step(s, first, last):
        root = lax.rem(me - s + 2 * S, S)
        each = range(MB_DEV)
        masks = [allowed_of(root, m) for m in each]
        if first:
            gained = [project_kv(s, m, first) for m in each]
            inverses = [swap(s, m) for m in each]
            for m in each:
                project_q(s, m, first, gained[m])
            for m in each:
                attend(s, m, inverses[m], masks[m])
        else:
            for m in each:
                project_q(s, m, first, project_kv(s, m, first))
                if m > 0:
                    attend(s, m - 1, inverse, masks[m - 1])
                inverse = swap(s, m)
            attend(s, MB_DEV - 1, inverse, masks[-1])
        for m in range(MB_DEV):
            leave(s, m, last)

    def middle(s, carry):
        step(s, False, False)
        return carry

    drain(gain_own, w_sems.at[1, 1])
    step(0, True, False)
    lax.fori_loop(1, STEPS - 1, middle, 0)
    step(STEPS - 1, False, True)

    for m in range(MB_DEV):
        drain(xs.at[STEPS, m, :, pl.ds(0, width)], recv_sems.at[STEPS, m, 5])
        out[m * MB_ROWS : (m + 1) * MB_ROWS, :] = xs[STEPS, m, :, own_half]

    drain(arecv.at[pl.ds(0, S - 1)], w_sems.at[0, 0])
    drain(gain_own, w_sems.at[0, 1])
    drain(xs.at[0, :, :, pl.ds(0, width)], w_sems.at[0, 2])
    drain(w_all.at[pl.ds(0, width), pl.ds(0, kv_cols)], w_sems.at[0, 3])
    drain(w_all.at[:, pl.ds(0, (Z - 1) * HD)], w_sems.at[0, 4])

    def finish(s, carry):
        for m in range(MB_DEV):
            drain(ssrecv.at[s, m], send_sems.at[s, m, 0])
            drain(qsend.at[s, m], send_sems.at[s, m, 1])
            drain(kvsend.at[s, m], send_sems.at[s, m, 2])
            drain(swsend.at[s, m], send_sems.at[s, m, 3])
            drain(att.at[s, m, :, pl.ds(0, (T - 1) * HD)], send_sems.at[s, m, 4])
            drain(xnew.at[s, m], send_sems.at[s, m, 5])

            @pl.when(s < STEPS - 1)
            def _():
                drain(xnew.at[s, m], send_sems.at[s, m, 5])

        return carry

    lax.fori_loop(0, STEPS, finish, 0)


def local(S, T, hidden, audio, audio_dest, segment, norm_gain, w_query, w_keyval, w_out):
    width = hidden.shape[1]
    rows = MB_DEV * MB_ROWS
    Z = T // 2
    cols = (Z + KVH) * HD
    cosine, sine = rope_tables()
    vmem = pl.BlockSpec(memory_space=pltpu.VMEM)
    hbm = pl.BlockSpec(memory_space=pl.ANY)
    per = (STEPS, MB_DEV)
    scratch = [
        pltpu.VMEM((2 * width, cols), BF16),
        pltpu.VMEM(w_out.shape[1:], BF16),
        pltpu.VMEM((S, AUD_DEV, width), BF16),
        pltpu.VMEM((MB_DEV * TXT_MB, width), BF16),
        pltpu.VMEM((8, width), F32),
        pltpu.VMEM((8, 2 * width), F32),
        pltpu.VMEM((STEPS + 1, MB_DEV, MB_ROWS, 2 * width), BF16),
        pltpu.VMEM(per + (MB_ROWS, width), BF16),
        pltpu.VMEM((MB_DEV, MB_ROWS, cols), F32),
        pltpu.VMEM(per + (Z - 1, MB_ROWS, HD), BF16),
        pltpu.VMEM(per + (Z - 1, MB_ROWS, HD), BF16),
        pltpu.VMEM(per + (Z - 1, MB_ROWS, HD), BF16),
        pltpu.VMEM(per + (Z - 1, MB_ROWS, HD), BF16),
        pltpu.VMEM(per + (8, 2 * MB_ROWS), F32),
        pltpu.VMEM(per + (Z - 1, 8, 2 * MB_ROWS), F32),
        pltpu.VMEM(per + (MB_ROWS, HD), BF16),
        pltpu.VMEM(per + (MB_ROWS, HD), BF16),
        pltpu.VMEM(per + (MB_ROWS, T * HD), BF16),
        pltpu.SemaphoreType.DMA((4 + KVH,)),
        pltpu.SemaphoreType.DMA((2, 5)),
        pltpu.SemaphoreType.DMA(per + (6,)),
        pltpu.SemaphoreType.DMA((STEPS + 1, MB_DEV, 6)),
    ]
    return pl.pallas_call(
        functools.partial(kernel, S, T),
        out_shape=jax.ShapeDtypeStruct((rows, width), BF16),
        in_specs=[hbm, hbm, vmem, vmem, vmem, hbm, hbm, hbm, vmem, vmem],
        out_specs=vmem,
        scratch_shapes=scratch,
        compiler_params=pltpu.CompilerParams(
            collective_id=0, has_side_effects=True, vmem_limit_bytes=62 * 1024 * 1024
        ),
        cost_estimate=pl.CostEstimate(
            flops=STEPS * rows * width * (2 * cols + T * HD) * 2,
            bytes_accessed=8 * 1024 * 1024,
            transcendentals=0,
        ),
    )(
        hidden,
        audio,
        audio_dest.reshape(1, -1),
        segment,
        norm_gain,
        w_query,
        w_keyval,
        w_out,
        jnp.asarray(cosine),
        jnp.asarray(sine),
    )


def solution(mesh):
    in_specs = (
        P("section", "tensor"),
        P("section", "tensor"),
        P(),
        P(),
        P("section", "tensor"),
        P("section", None, "tensor"),
        P("section", "tensor", None),
        P("section", None, "tensor"),
    )
    out_specs = P("section", "tensor")
    body = functools.partial(local, mesh.shape["section"], mesh.shape["tensor"])
    return jax.shard_map(body, mesh=mesh, in_specs=in_specs, out_specs=out_specs, check_vma=False)
```
